256 devices in a mesh: dp: 128 (over z, x_hi, y, core), fsdp: 2 (over x_lo).
Axes of the slice: x: 4 (x_hi: 2, x_lo: 2; x = x_hi * 2 + x_lo), y: 4, z: 8, core: 2. Of those that a mesh axis runs over, the one named last changes fastest.
Arguments:
- super_image: bfloat16 [81920, 1152], P(('dp', 'fsdp')), may hold values from -0.35 to 0.35
- super_text: bfloat16 [81920, 1152], P(('dp', 'fsdp')), may hold values from -0.35 to 0.35
- selected: int32 [16384], P(('dp', 'fsdp')), may hold values from 0 to 319, as said below
- buckets: int32 [16384], P(('dp', 'fsdp')), may hold values from 0 to 15
- bucket_weights: float32 [16], replicated, may hold values from 3 to 4
- image_proj: bfloat16 [1152, 576], P('fsdp'), may hold values from -0.11785113 to 0.11785113
- text_proj: bfloat16 [1152, 576], P('fsdp'), may hold values from -0.11785113 to 0.11785113
- logit_scale: float32 [1], replicated, may hold values from 5 to 10
- logit_bias: float32 [1], replicated, may hold values from -5 to -2
- loss_scale: float32 [1], replicated, may hold values from 1024 to 8192
Outputs:
- grad_image_proj: float32 [1152, 576], P('fsdp')
- grad_text_proj: float32 [1152, 576], P('fsdp')
- grad_super_image: float32 [81920, 1152], P(('dp', 'fsdp'))
- grad_super_text: float32 [81920, 1152], P(('dp', 'fsdp'))
The draws below stay inside these ranges and needn't reach their ends.
Inputs may be any that keep to these rules, and one draw needn't show every extreme that they name: `selected`: the 64 entries of each aligned block of 64 (one device's pairs) are distinct.
All inputs are finite; a program needn't handle non-finite values.
Results may differ from the reference program's by a relative error of at most 0.0085.
Values may be sent and summed in bfloat16 or wider, within the bound.
A program may use at most 128 MiB of HBM per device.

```python
import math
import jax
import jax.numpy as jnp
from jax import lax

D = 1152
E = 576
P_DEV = 64
S_DEV = 320
NB = 16
PAIRS = 16384
SUPER = 81920


def draw_selected(key, part):
    key = jax.random.fold_in(key, 7)
    blocks = PAIRS // P_DEV
    keys = jax.random.split(key, blocks)
    orders = jax.vmap(lambda single: jax.random.permutation(single, S_DEV))(keys)
    return orders[:, :P_DEV].reshape(-1).astype(jnp.int32)


def cluster_centres(key):
    clusters = max(PAIRS // 8, 1)
    centre_key = jax.random.fold_in(key, 101)
    member_key = jax.random.fold_in(key, 102)
    centres = jnp.clip(jax.random.normal(centre_key, (clusters, D), jnp.float32), -3.0, 3.0)
    members = jax.random.randint(member_key, (SUPER,), 0, clusters)
    return jnp.take(centres, members, axis=0)


def shared_head(key):
    return jax.random.normal(jax.random.fold_in(key, 201), (D, E), jnp.float32)


def draw_super_image(key, part):
    shared = cluster_centres(key)
    key = jax.random.fold_in(key, 11)
    noise = jnp.clip(jax.random.normal(key, (SUPER, D), jnp.float32), -3.0, 3.0)
    return jnp.clip(0.045 * shared + 0.0225 * noise, -0.35, 0.35).astype(jnp.bfloat16)


def draw_super_text(key, part):
    shared = cluster_centres(key)
    key = jax.random.fold_in(key, 12)
    noise = jnp.clip(jax.random.normal(key, (SUPER, D), jnp.float32), -3.0, 3.0)
    return jnp.clip(0.045 * shared + 0.0225 * noise, -0.35, 0.35).astype(jnp.bfloat16)


def draw_image_proj(key, part):
    common = shared_head(key)
    key = jax.random.fold_in(key, 21)
    own = jax.random.normal(key, (D, E), jnp.float32)
    return (jnp.clip(0.95 * common + 0.3122 * own, -4.0, 4.0) / math.sqrt(D)).astype(jnp.bfloat16)


def draw_text_proj(key, part):
    common = shared_head(key)
    key = jax.random.fold_in(key, 22)
    own = jax.random.normal(key, (D, E), jnp.float32)
    return (jnp.clip(0.95 * common + 0.3122 * own, -4.0, 4.0) / math.sqrt(D)).astype(jnp.bfloat16)


def place_ends(values, stream_key, least, top_value):
    index_at = [jax.random.randint(jax.random.fold_in(stream_key, axis), (), 0, length) for axis, length in enumerate(values.shape)]
    longest = values.shape.index(max(values.shape))
    neighbour = index_at[:longest] + [(index_at[longest] + 1) % values.shape[longest]] + index_at[longest + 1:]
    return values.at[tuple(index_at)].set(least).at[tuple(neighbour)].set(top_value)


def setup_inputs(seed: int = 0) -> dict:
    streams_of = jax.random.split(jax.random.key(seed), 11)
    return {
        "super_image": draw_super_image(jax.random.fold_in(streams_of[10], 71), 0),
        "super_text": draw_super_text(jax.random.fold_in(streams_of[10], 71), 0),
        "selected": draw_selected(jax.random.fold_in(streams_of[10], 71), 0),
        "buckets": place_ends(jax.random.randint(streams_of[3], (PAIRS,), 0, NB), jax.random.fold_in(streams_of[3], 1), 0, NB - 1).astype(jnp.int32),
        "bucket_weights": jnp.clip(jax.random.uniform(streams_of[4], (NB,), jnp.float32, 3.0, 4.0), 3.0, 4.0),
        "image_proj": draw_image_proj(jax.random.fold_in(streams_of[10], 71), 0),
        "text_proj": draw_text_proj(jax.random.fold_in(streams_of[10], 71), 0),
        "logit_scale": jnp.clip(jax.random.uniform(streams_of[7], (1,), jnp.float32, 5.0, 10.0), 5.0, 10.0),
        "logit_bias": jnp.clip(jax.random.uniform(streams_of[8], (1,), jnp.float32, -5.0, -2.0), -5.0, -2.0),
        "loss_scale": jnp.clip(jax.random.uniform(streams_of[9], (1,), jnp.float32, 1024.0, 8192.0), 1024.0, 8192.0),
    }


def project(rows, weight):
    raw = jnp.dot(rows, weight, preferred_element_type=jnp.float32)
    length = jnp.sqrt(lax.optimization_barrier(jnp.sum(raw * raw, axis=1, keepdims=True)) + 1e-06)
    return (raw / length, length)

def unproject(grad, unit, length):
    return ((grad - unit * lax.optimization_barrier(jnp.sum(unit * grad, axis=1, keepdims=True))) / length).astype(jnp.bfloat16)

def reference(super_image, super_text, selected, buckets, bucket_weights, image_proj, text_proj, logit_scale, logit_bias, loss_scale):
    blocks = PAIRS // P_DEV
    sel = selected.reshape(blocks, P_DEV)
    image_rows = jnp.take_along_axis(super_image.reshape(blocks, S_DEV, D), sel[:, :, None], axis=1).reshape(PAIRS, D)
    text_rows = jnp.take_along_axis(super_text.reshape(blocks, S_DEV, D), sel[:, :, None], axis=1).reshape(PAIRS, D)
    image_unit, image_len = project(image_rows, image_proj)
    text_unit, text_len = project(text_rows, text_proj)
    image_emb = image_unit.astype(jnp.bfloat16)
    text_emb = text_unit.astype(jnp.bfloat16)
    coef = loss_scale[0] * bucket_weights[buckets] / PAIRS
    scale = logit_scale[0]
    bias = logit_bias[0]
    col_ids = jnp.arange(PAIRS, dtype=jnp.int32)

    def step(carry, block):
        emb, cf, ids = block
        logits = scale * jnp.dot(emb, text_emb.T, preferred_element_type=jnp.float32) + bias
        sign = jnp.where(ids[:, None] == col_ids[None, :], 1.0, -1.0).astype(jnp.float32)
        grad = (-cf[:, None] * sign * jax.nn.sigmoid(-sign * logits)).astype(jnp.bfloat16)
        gi = scale * jnp.dot(grad, text_emb, preferred_element_type=jnp.float32)
        gt = scale * jnp.dot(grad.T, emb, preferred_element_type=jnp.float32)
        return (carry + gt, gi)
    init = jnp.zeros((PAIRS, E), jnp.float32)
    grad_text_emb, gi_blocks = lax.scan(step, init, (image_emb.reshape(blocks, P_DEV, E), coef.reshape(blocks, P_DEV), col_ids.reshape(blocks, P_DEV)))
    grad_image_emb = gi_blocks.reshape(PAIRS, E)
    image_back = unproject(grad_image_emb, image_unit, image_len)
    text_back = unproject(grad_text_emb, text_unit, text_len)
    grad_image_proj = jnp.dot(image_rows.T, image_back, preferred_element_type=jnp.float32)
    grad_text_proj = jnp.dot(text_rows.T, text_back, preferred_element_type=jnp.float32)
    image_feat = jnp.dot(image_back, image_proj.T, preferred_element_type=jnp.float32).reshape(blocks, P_DEV, D)
    text_feat = jnp.dot(text_back, text_proj.T, preferred_element_type=jnp.float32).reshape(blocks, P_DEV, D)
    owners = jnp.arange(blocks, dtype=jnp.int32)[:, None]
    grad_super_image = jnp.zeros((blocks, S_DEV, D), jnp.float32).at[owners, sel].set(image_feat).reshape(SUPER, D)
    grad_super_text = jnp.zeros((blocks, S_DEV, D), jnp.float32).at[owners, sel].set(text_feat).reshape(SUPER, D)
    return (grad_image_proj, grad_text_proj, grad_super_image, grad_super_text)
```

```python
import functools

import jax
import jax.numpy as jnp
from jax import lax
from jax.experimental import pallas as pl
from jax.experimental.pallas import tpu as pltpu
from jax.sharding import PartitionSpec as P

MESH = pl.DeviceIdType.MESH
BF = jnp.bfloat16
F32 = jnp.float32
NX, NY, NZ = 4, 4, 8
PLANE = NX * NY
PAIRS = 16384
N = 64
N2 = 2 * N
S = 320
D = 1152
H = D // 2
E = 576
EP = 640
PIECE = D // PLANE
PR = 80
NB = 16


def place():
    dp, x_lo = lax.axis_index("dp"), lax.axis_index("fsdp")
    core = lax.rem(dp, 2)
    y = lax.rem(lax.div(dp, 2), NY)
    x = lax.rem(lax.div(dp, 2 * NY), 2) * 2 + x_lo
    z = lax.div(dp, 4 * NY)
    return x, y, z, core


def device(x, y, z, core):
    return (((z * 2 + lax.div(x, 2)) * NY + y) * 2 + core, lax.rem(x, 2))


def dot(a, b, contract):
    return lax.dot_general(a, b, (contract, ((), ())), preferred_element_type=F32)


def kernel(
    sup_i, sup_t, sel, bkt, wts, head_i, head_t, lscale, lbias, oscale,
    gs, gw,
    a, stage, cbuf, wfull, wother, unit, length,
    em, img, txt, g, p_f, p_out, p_in, t_out, rs_i, rs_t,
    bk, bo, gsv, dwf, dws, r1, psum, r2, fin, res,
    w_s, w_r, rows_s, rows_r, c_s, c_r, wo_s, wo_r,
    ia_s, ia_r, if_s, ta_s, ta_r, pi_s, pi_r, ri_s, ri_r, rt_s, rt_r,
    bk_s, bk_r, gs_s, r1_s, r1_r, r2_s, r2_r, f_s, f_r, own_s, ag_s, ag_r, ad_s, ad_r,
):
    x, y, z, core = place()
    half = lax.rem(x, 2)
    sib = device(x, y, z, 1 - core)
    first = core == 0

    def line(k, c=core):
        return device(x, y, lax.rem(z + k, NZ), c)

    def plane(k, c=core):
        return device(lax.rem(x + k // NY, NX), lax.rem(y + k % NY, NY), z, c)

    def back_slot(k):
        return (-(k // NY)) % NX * NY + (-(k % NY)) % NY

    def remote(src, dst, send, recv, to):
        return pltpu.make_async_remote_copy(
            src_ref=src, dst_ref=dst, send_sem=send, recv_sem=recv,
            device_id=to, device_id_type=MESH,
        )

    def arrived(dst, recv, send):
        remote(dst, dst, send, recv, sib).wait_recv()

    def rows(ref, start, count):
        return ref.at[pl.ds(start, count), :]

    barrier = pltpu.get_barrier_semaphore()

    def greet(to):
        pl.semaphore_signal(barrier, inc=1, device_id=to, device_id_type=MESH)

    greet(sib)
    for k in range(1, NZ):
        greet(line(k))
    for k in range(1, PLANE):
        greet(plane(k, 0))
        greet(plane(k, 1))

    h_off = pl.multiple_of(half * H, H)
    wfull[pl.ds(h_off, H), :] = jnp.where(first, head_i[...], head_t[...])
    onehot = (lax.broadcasted_iota(jnp.int32, (S, N), 0) == sel[...]).astype(BF)
    rows_i = dot(onehot, sup_i[...], ((0,), (0,))).astype(BF)
    rows_t = dot(onehot, sup_t[...], ((0,), (0,))).astype(BF)
    mine = pl.multiple_of(core * N, N)
    a[pl.ds(mine, N), :] = jnp.where(first, rows_i, rows_t)
    stage[...] = jnp.where(first, rows_t, rows_i)
    weight = jnp.zeros((1, N), F32)
    for n in range(NB):
        weight = jnp.where(bkt[...] == n, wts[n], weight)
    weight = oscale[0] * weight / PAIRS
    cbuf[pl.ds(pl.multiple_of(core * 8, 8), 8), :] = jnp.concatenate(
        [jnp.broadcast_to(weight, (8, N)), jnp.zeros((8, N), F32)], axis=1
    )

    pl.semaphore_wait(barrier, 1 + (NZ - 1) + 2 * (PLANE - 1))

    heads = []
    for k, step in ((0, 1), (1, NX - 1)):
        src = rows(wfull, pl.multiple_of(h_off + k * (H // 2), H // 2), H // 2)
        heads.append(
            remote(src, src, w_s.at[k], w_r.at[k], device(lax.rem(x + step, NX), y, z, core))
        )
    rows_copy = remote(stage, rows(a, mine, N), rows_s, rows_r, sib)
    c_own = rows(cbuf, pl.multiple_of(core * 8, 8), 8)
    c_copy = remote(c_own, c_own, c_s, c_r, sib)
    for copy in heads:
        copy.start()
    rows_copy.start()
    c_copy.start()
    theirs = pl.multiple_of((1 - core) * N, N)
    o_off = pl.multiple_of((1 - half) * H, H)
    arrived(rows(a, theirs, N), rows_r, rows_s)
    arrived(rows(cbuf, pl.multiple_of((1 - core) * 8, 8), 8), c_r, c_s)
    for k in range(2):
        arrived(
            rows(wfull, pl.multiple_of(o_off + k * (H // 2), H // 2), H // 2), w_r.at[k], w_s.at[k]
        )

    raw = dot(a[...], wfull[...], ((1,), (0,)))
    size = jnp.sqrt(jnp.sum(raw * raw, axis=1, keepdims=True) + 1e-06)
    u = raw / size
    unit[...] = u
    length[...] = jnp.broadcast_to(size, (N2, 128))
    eye = lax.broadcasted_iota(jnp.int32, (N, N), 0) == lax.broadcasted_iota(jnp.int32, (N, N), 1)
    column = jnp.concatenate(
        [
            jnp.sum(jnp.where(eye, cbuf[8 * c : 8 * c + 1, 0:N], 0.0), axis=1, keepdims=True)
            for c in range(2)
        ],
        axis=0,
    )
    column = jnp.where(first, column, jnp.zeros_like(column))
    high = column.astype(BF)
    low = (column - high.astype(F32)).astype(BF)
    em[...] = jnp.concatenate([u.astype(BF), high, low, jnp.zeros((N2, EP - E - 2), BF)], axis=1)

    line_order = (1, 7, 2, 6, 3, 5, 4)
    plane_order = sorted(
        range(1, PLANE),
        key=lambda k: (min(k // 4, 4 - k // 4) + min(k % 4, 4 - k % 4), k),
    )

    def ia(k):
        return remote(
            em, rows(img, (NZ - k) % NZ * N2, N2), ia_s.at[k], ia_r.at[(NZ - k) % NZ], line(k)
        )

    def fwd(s):
        block = rows(img, s * N2, N2)
        src = em if s == 0 else block
        return remote(src, block, if_s.at[s], ia_r.at[s], sib)

    def ta(k, c):
        return remote(
            rows(em, c * N, N), rows(txt, back_slot(k) * N, N),
            ta_s.at[2 * k + c], ta_r.at[back_slot(k)], plane(k, c),
        )

    @pl.when(first)
    def _():
        for k in line_order:
            ia(k).start()
        fwd(0).start()
        img[0:N2, :] = em[...]

    @pl.when(core == 1)
    def _():
        for k in plane_order:
            ta(k, 0).start()
            ta(k, 1).start()
        ta(0, 0).start()
        txt[0:N, :] = em[N:N2, :]

    wo_copy = remote(wfull, wother, wo_s, wo_r, sib)
    wo_copy.start()

    @pl.when(first)
    def _():
        arrived(rows(txt, 0, N), ta_r.at[0], ta_s.at[0])

    for k in plane_order:
        arrived(rows(txt, k * N, N), ta_r.at[k], ta_s.at[0])

    scale = lscale[0]
    neg_scale, neg_bias = -lscale[0], -lbias[0]

    def image_block(s):
        block = img[pl.ds(pl.multiple_of(s * N2, N2), N2), :]
        weight = block[:, E : E + 1].astype(F32) + block[:, E + 1 : E + 2].astype(F32)
        e = jnp.exp(neg_scale * dot(block, txt[...], ((1,), (1,))) + neg_bias)
        positive = weight / (1.0 + e)
        return e, positive

    def take(s):
        @pl.when(first)
        def _():
            if s:
                arrived(rows(img, s * N2, N2), ia_r.at[s], ia_s.at[0])
                fwd(s).start()

        @pl.when(core == 1)
        def _():
            arrived(rows(img, s * N2, N2), ia_r.at[s], ia_s.at[0])

    for s in (0,) + line_order:
        take(s)
        e, positive = image_block(s)
        if s == 0:
            r = lax.broadcasted_iota(jnp.int32, (N2, PLANE * N), 0)
            c = lax.broadcasted_iota(jnp.int32, (N2, PLANE * N), 1)
            same = (r == c + core * N) & (c < N)
            positive = jnp.where(same, -positive * e, positive)
        g[s * N2 : (s + 1) * N2, :] = positive.astype(BF)

    def partial_i(s):
        off = pl.multiple_of(s * N2, N2)
        return dot(g[pl.ds(off, N2), :], txt[:, 0:E], ((1,), (0,)))

    def pi(s):
        return remote(rows(p_out, s * N2, N2), rows(p_in, s * N2, N2), pi_s.at[s], pi_r.at[s], sib)

    def ri(k):
        return remote(
            rows(p_out, k * N2, N2), rows(rs_i, (NZ - k) % NZ * N2, N2),
            ri_s.at[k], ri_r.at[(NZ - k) % NZ], line(k),
        )

    def wait_fwd(s):
        fwd(s).wait_send()

    @pl.when(first)
    def _():
        for k in line_order:
            ia(k).wait_send()
        for s in range(NZ):
            wait_fwd(s)

    @pl.when(core == 1)
    def _():
        for k in plane_order:
            ta(k, 0).wait_send()
            ta(k, 1).wait_send()
        ta(0, 0).wait_send()

    send_order = line_order + (0,)
    for s in send_order:
        p_f[s * N2 : (s + 1) * N2, :] = partial_i(s)

        @pl.when(core == 1)
        def _(s=s):
            p_out[s * N2 : (s + 1) * N2, :] = p_f[s * N2 : (s + 1) * N2, :].astype(BF)
            pi(s).start()

    @pl.when(first)
    def _():
        for s in send_order:
            arrived(rows(p_in, s * N2, N2), pi_r.at[s], pi_s.at[s])
            total = p_f[s * N2 : (s + 1) * N2, :] + p_in[s * N2 : (s + 1) * N2, :].astype(F32)
            if s:
                p_out[s * N2 : (s + 1) * N2, :] = total.astype(BF)
                ri(s).start()
            else:
                p_f[0:N2, :] = total

    def rt(k):
        return remote(
            rows(t_out, k * N, N), rows(rs_t, (core * PLANE + back_slot(k)) * N, N),
            rt_s.at[k], rt_r.at[core * PLANE + back_slot(k)], plane(k, 1),
        )

    for b in range(PLANE // 2):
        block = dot(g[:, b * N2 : (b + 1) * N2], img[:, 0:E], ((0,), (0,)))
        t_out[b * N2 : (b + 1) * N2, :] = block.astype(BF)
        for k in (2 * b, 2 * b + 1):
            if k:
                rt(k).start()
            else:

                @pl.when(first)
                def _():
                    rt(0).start()

                @pl.when(core == 1)
                def _(block=block):
                    p_f[N : 2 * N, :] = block[0:N, :]

    @pl.when(core == 1)
    def _():
        arrived(rows(rs_t, 0, N), rt_r.at[0], rt_s.at[0])
        p_f[0:N, :] = rs_t[0:N, :].astype(F32)
        for k in plane_order:
            for c in range(2):
                at = c * PLANE + k
                arrived(rows(rs_t, at * N, N), rt_r.at[at], rt_s.at[0])
                p_f[c * N : (c + 1) * N, :] += rs_t[at * N : (at + 1) * N, :].astype(F32)

    @pl.when(first)
    def _():
        for s in line_order:
            arrived(rows(rs_i, s * N2, N2), ri_r.at[s], ri_s.at[0])
            p_f[0:N2, :] += rs_i[s * N2 : (s + 1) * N2, :].astype(F32)

    grad = p_f[0:N2, :] * scale
    u = unit[...]
    back = ((grad - u * jnp.sum(u * grad, axis=1, keepdims=True)) / length[:, 0:1]).astype(BF)
    bk[...] = back
    bk_copy = remote(rows(bk, theirs, N), bo, bk_s, bk_r, sib)
    bk_copy.start()

    dwf[...] = dot(a[...], back, ((0,), (0,)))

    def piece(px, py):
        return (lax.rem(px, 2) * 2 + lax.div(px, 2)) * NY + py

    def r1_copy(k):
        return remote(
            rows(dws, k * PR, PR), rows(r1, back_slot(k) * PR, PR),
            r1_s.at[k], r1_r.at[back_slot(k)], plane(k),
        )

    def part(k):
        q = piece(lax.rem(x + k // NY, NX), lax.rem(y + k % NY, NY))
        return dwf[pl.ds(pl.multiple_of(q * PIECE, 8), PIECE), :]

    for k in plane_order:
        dws[k * PR : (k + 1) * PR, :] = jnp.concatenate(
            [part(k), jnp.zeros((PR - PIECE, E), F32)], axis=0
        ).astype(BF)
        r1_copy(k).start()

    arrived(bo, bk_r, bk_s)
    arrived(wother, wo_r, wo_s)
    own = bk[pl.ds(mine, N), :]
    moved = dot(onehot, own, ((1,), (0,))).astype(BF)
    gsv[core] = dot(moved, wfull[...], ((1,), (1,)))
    moved = dot(onehot, bo[...], ((1,), (0,))).astype(BF)
    gsv[1 - core] = dot(moved, wother[...], ((1,), (1,)))
    gs_copy = pltpu.make_async_copy(gsv, gs, gs_s)
    gs_copy.start()

    total = part(0)
    for k in plane_order:
        arrived(rows(r1, k * PR, PR), r1_r.at[k], r1_s.at[k])
        total += r1[k * PR : (k + 1) * PR, :].astype(F32)[0:PIECE, :]
    whole = jnp.concatenate([total, jnp.zeros((PR - PIECE, E), F32)], axis=0)
    psum[...] = whole.astype(BF)

    rank = lax.rem(z + 4 * core, NZ)

    def rank_of(k):
        return lax.rem(rank + k, NZ)

    def tile(ref, at, base=0):
        return rows(ref, pl.multiple_of(base + at * 16, 16), 16)

    def r2_copy(k):
        back_k = (NZ - k) % NZ
        return remote(
            tile(psum, rank_of(k)), rows(r2, back_k * 16, 16), r2_s.at[k], r2_r.at[back_k], line(k)
        )

    for k in line_order:

        @pl.when(rank_of(k) < 5)
        def _(k=k):
            r2_copy(k).start()

    def f_copy(k):
        return remote(res, tile(fin, rank), f_s.at[k], f_r.at[(NZ - k) % NZ], line(k))

    @pl.when(rank < 5)
    def _():
        total = psum[pl.ds(pl.multiple_of(rank * 16, 16), 16), :].astype(F32)
        for k in line_order:
            arrived(rows(r2, k * 16, 16), r2_r.at[k], r2_s.at[k])
            total += r2[k * 16 : (k + 1) * 16, :].astype(F32)
        res[...] = total.astype(BF)
        for k in line_order:
            f_copy(k).start()
        fin[pl.ds(pl.multiple_of(rank * 16, 16), 16), :] = total.astype(BF)

    for k in line_order:

        @pl.when(rank_of(k) < 5)
        def _(k=k):
            arrived(tile(fin, rank_of(k)), f_r.at[k], f_s.at[k])

    def held(px, py):
        return pl.multiple_of((lax.div(px, 2) * NY + py) * PR, PR)

    mates = [k for k in plane_order if (k // NY) % 2 == 0]

    def mate(k):
        return lax.rem(x + k // NY, NX), lax.rem(y + k % NY, NY)

    def ag_copy(k):
        return remote(
            fin, gw.at[core, pl.ds(held(x, y), PR), :],
            ag_s.at[k], ag_r.at[back_slot(k)], plane(k),
        )

    def ad_copy(k):
        block = gw.at[core, pl.ds(held(*mate(k)), PR), :]
        return remote(fin if k == 0 else block, block, ad_s.at[k], ad_r.at[k], sib)

    for k in mates:
        ag_copy(k).start()
    ad_copy(0).start()
    own_copy = pltpu.make_async_copy(fin, gw.at[core, pl.ds(held(x, y), PR), :], own_s)
    own_copy.start()
    for k in mates:
        arrived(gw.at[core, pl.ds(held(*mate(k)), PR), :], ag_r.at[k], ag_s.at[k])
        ad_copy(k).start()
    for k in [0] + mates:
        arrived(gw.at[1 - core, pl.ds(held(*mate(k)), PR), :], ad_r.at[k], ad_s.at[k])

    for copy in heads + [rows_copy, c_copy, wo_copy, bk_copy]:
        copy.wait_send()

    @pl.when(first)
    def _():
        for k in line_order:
            ri(k).wait_send()
        rt(0).wait_send()

    @pl.when(core == 1)
    def _():
        for s in range(NZ):
            pi(s).wait_send()

    for k in plane_order:
        rt(k).wait_send()
        r1_copy(k).wait_send()
    for k in line_order:

        @pl.when(rank_of(k) < 5)
        def _(k=k):
            r2_copy(k).wait_send()

    @pl.when(rank < 5)
    def _():
        for k in line_order:
            f_copy(k).wait_send()

    for k in mates:
        ag_copy(k).wait_send()
    for k in [0] + mates:
        ad_copy(k).wait_send()
    own_copy.wait()
    gs_copy.wait()


def body(sup_i, sup_t, selected, buckets, weights, head_i, head_t, lscale, lbias, oscale):
    vmem = pl.BlockSpec(memory_space=pltpu.VMEM)
    smem = pl.BlockSpec(memory_space=pltpu.SMEM)
    hbm = pl.BlockSpec(memory_space=pl.ANY)

    def space(shape, dtype=BF):
        return pltpu.VMEM(shape, dtype)

    dma = pltpu.SemaphoreType.DMA
    buffers = [
        space((N2, D)), space((N, D)), space((16, 128), F32), space((D, E)), space((D, E)),
        space((N2, E), F32), space((N2, 128), F32),
        space((N2, EP)), space((NZ * N2, EP)), space((PLANE * N, EP)),
        space((NZ * N2, PLANE * N)),
        space((NZ * N2, E), F32), space((NZ * N2, E)), space((NZ * N2, E)), space((PLANE * N, E)),
        space((NZ * N2, E)), space((2 * PLANE * N, E)),
        space((N2, E)), space((N, E)), space((2, S, D), F32), space((D, E), F32),
        space((PLANE * PR, E)), space((PLANE * PR, E)), space((PR, E)), space((NZ * 16, E)),
        space((PR, E)), space((16, E)),
    ]
    counts = [
        2, 2, 0, 0, 0, 0, 0, 0,
        NZ, NZ, NZ, 2 * PLANE, PLANE, NZ, NZ, NZ, NZ, PLANE, 2 * PLANE,
        0, 0, 0, PLANE, PLANE, NZ, NZ, NZ, NZ, 0, PLANE, PLANE, PLANE, PLANE,
    ]
    sems = [dma((n,)) if n else dma for n in counts]
    gs, gw = pl.pallas_call(
        kernel,
        out_shape=(
            jax.ShapeDtypeStruct((2, S, D), F32),
            jax.ShapeDtypeStruct((2, 8 * PR, E), BF),
        ),
        in_specs=[vmem] * 4 + [smem] + [vmem] * 2 + [smem] * 3,
        out_specs=(hbm, hbm),
        scratch_shapes=buffers + sems,
        compiler_params=pltpu.CompilerParams(
            collective_id=0, has_side_effects=True, vmem_limit_bytes=56 * 1024 * 1024
        ),
    )(
        sup_i, sup_t, selected.reshape(1, N), buckets.reshape(1, N), weights,
        head_i, head_t, lscale, lbias, oscale,
    )
    gw = gw.reshape(2, 8, PR, E)[:, :, 0:PIECE, :].reshape(2, H, E).astype(F32)
    return gw[0], gw[1], gs[0], gs[1]


def solution(mesh):
    both = P(("dp", "fsdp"))
    wide = P(("dp", "fsdp"), None)
    head = P("fsdp", None)
    in_specs = (wide, wide, both, both, P(), head, head, P(), P(), P())
    out_specs = (head, head, wide, wide)
    return jax.shard_map(body, mesh=mesh, in_specs=in_specs, out_specs=out_specs, check_vma=False)
```

```python
import functools

import jax
import jax.numpy as jnp
from jax import lax
from jax.experimental import pallas as pl
from jax.experimental.pallas import tpu as pltpu
from jax.sharding import PartitionSpec as P

MESH = pl.DeviceIdType.MESH
BF = jnp.bfloat16
F32 = jnp.float32
NX, NY, NZ = 4, 4, 8
PLANE = NX * NY
PAIRS = 16384
N = 64
N2 = 2 * N
S = 320
D = 1152
H = D // 2
E = 576
EP = 640
PIECE = D // PLANE
B = 256
PR = 80
NB = 16
LOG2E = 1.4426950408889634


def hops(k):
    return min(k // NY, NX - k // NY) + min(k % NY, NY - k % NY)


def back_slot(k):
    return (-(k // NY)) % NX * NY + (-(k % NY)) % NY


LINE = (0, 1, 7, 2, 6, 3, 5, 4)
SHEET = tuple(sorted(range(PLANE), key=lambda k: (hops(k), k)))


def place():
    dp, x_lo = lax.axis_index("dp"), lax.axis_index("fsdp")
    core = lax.rem(dp, 2)
    y = lax.rem(lax.div(dp, 2), NY)
    x = lax.rem(lax.div(dp, 2 * NY), 2) * 2 + x_lo
    z = lax.div(dp, 4 * NY)
    return x, y, z, core


def device(x, y, z, core):
    return (((z * 2 + lax.div(x, 2)) * NY + y) * 2 + core, lax.rem(x, 2))


def dot(a, b, contract):
    return lax.dot_general(a, b, (contract, ((), ())), preferred_element_type=F32)


def kernel(
    sup_i, sup_t, sel, bkt, wts, head_i, head_t, lscale, lbias, oscale,
    gs_i, gs_t, gw,
    va, vt, a, stage, cbuf, wfull, wother, unit, length,
    em, img, txt, g, p_f, p_out, p_in, t_out, rs_i, rs_t,
    bk, bo, gsv, dwf, dws, r1, psum, r2, fin, res,
    in_s, w_s, w_r, rows_s, rows_r, c_s, c_r, wo_s, wo_r,
    ia_s, ia_r, if_s, ta_s, ta_r, pi_s, pi_r, ri_s, ri_r, rt_s, rt_r,
    bk_s, bk_r, gs_s, r1_s, r1_r, r2_s, r2_r, f_s, f_r, own_s, ag_s, ag_r, ad_s, ad_r,
):
    x, y, z, core = place()
    half = lax.rem(x, 2)
    sib = device(x, y, z, 1 - core)
    first = core == 0

    def line(k, c=core):
        return device(x, y, lax.rem(z + k, NZ), c)

    def plane(k, c=core):
        return device(lax.rem(x + k // NY, NX), lax.rem(y + k % NY, NY), z, c)

    def remote(src, dst, send, recv, to):
        return pltpu.make_async_remote_copy(
            src_ref=src, dst_ref=dst, send_sem=send, recv_sem=recv,
            device_id=to, device_id_type=MESH,
        )

    def arrived(dst, recv, send):
        remote(dst, dst, send, recv, sib).wait_recv()

    def rows(ref, start, count):
        return ref.at[pl.ds(start, count), :]

    barrier = pltpu.get_barrier_semaphore()

    def greet(to):
        pl.semaphore_signal(barrier, inc=1, device_id=to, device_id_type=MESH)

    h_off = pl.multiple_of(half * H, H)
    sup_copies = [
        pltpu.make_async_copy(sup_i, va, in_s.at[0]),
        pltpu.make_async_copy(sup_t, vt, in_s.at[1]),
    ]
    head_copy = pltpu.make_async_copy(head_i, rows(wfull, h_off, H), in_s.at[2])
    for copy in sup_copies:
        copy.start()

    @pl.when(first)
    def _():
        head_copy.start()

    @pl.when(core == 1)
    def _():
        pltpu.make_async_copy(head_t, rows(wfull, h_off, H), in_s.at[2]).start()

    greet(sib)
    for k in range(1, NZ):
        greet(line(k))
    for k in range(1, PLANE):
        greet(plane(k, 0))
        greet(plane(k, 1))

    for copy in sup_copies:
        copy.wait()
    onehot = (lax.broadcasted_iota(jnp.int32, (S, N), 0) == sel[...]).astype(BF)
    rows_i = dot(onehot, va[...], ((0,), (0,))).astype(BF)
    rows_t = dot(onehot, vt[...], ((0,), (0,))).astype(BF)
    mine = pl.multiple_of(core * N, N)
    a[pl.ds(mine, N), :] = jnp.where(first, rows_i, rows_t)
    stage[...] = jnp.where(first, rows_t, rows_i)
    weight = jnp.zeros((1, N), F32)
    for n in range(NB):
        weight = jnp.where(bkt[...] == n, wts[n], weight)
    weight = oscale[0] * weight / PAIRS
    cbuf[pl.ds(pl.multiple_of(core * 8, 8), 8), :] = jnp.concatenate(
        [jnp.broadcast_to(weight, (8, N)), jnp.zeros((8, N), F32)], axis=1
    )

    head_copy.wait()
    pl.semaphore_wait(barrier, 1 + (NZ - 1) + 2 * (PLANE - 1))

    heads = []
    for k, step in ((0, 1), (1, NX - 1)):
        src = rows(wfull, pl.multiple_of(h_off + k * (H // 2), H // 2), H // 2)
        heads.append(
            remote(src, src, w_s.at[k], w_r.at[k], device(lax.rem(x + step, NX), y, z, core))
        )
    rows_copy = remote(stage, rows(a, mine, N), rows_s, rows_r, sib)
    c_own = rows(cbuf, pl.multiple_of(core * 8, 8), 8)
    c_copy = remote(c_own, c_own, c_s, c_r, sib)
    for copy in heads:
        copy.start()
    rows_copy.start()
    c_copy.start()
    theirs = pl.multiple_of((1 - core) * N, N)
    o_off = pl.multiple_of((1 - half) * H, H)
    arrived(rows(a, theirs, N), rows_r, rows_s)
    arrived(rows(cbuf, pl.multiple_of((1 - core) * 8, 8), 8), c_r, c_s)
    for k in range(2):
        arrived(
            rows(wfull, pl.multiple_of(o_off + k * (H // 2), H // 2), H // 2), w_r.at[k], w_s.at[k]
        )

    raw = dot(a[...], wfull[...], ((1,), (0,)))
    size = jnp.sqrt(jnp.sum(raw * raw, axis=1, keepdims=True) + 1e-06)
    u = raw / size
    unit[...] = u
    length[...] = jnp.broadcast_to(size, (N2, 128))
    eye = lax.broadcasted_iota(jnp.int32, (N, N), 0) == lax.broadcasted_iota(jnp.int32, (N, N), 1)
    column = jnp.concatenate(
        [
            jnp.sum(jnp.where(eye, cbuf[8 * c : 8 * c + 1, 0:N], 0.0), axis=1, keepdims=True)
            for c in range(2)
        ],
        axis=0,
    )
    column = jnp.where(first, column, jnp.zeros_like(column))
    high = column.astype(BF)
    low = (column - high.astype(F32)).astype(BF)
    em[...] = jnp.concatenate([u.astype(BF), high, low, jnp.zeros((N2, EP - E - 2), BF)], axis=1)

    line_order, plane_order = LINE[1:], SHEET[1:]

    def img_at(k):
        return LINE.index(k % NZ) * N2

    def txt_at(k):
        return SHEET.index(k) * N

    def ia(k):
        return remote(
            em, rows(img, img_at(-k), N2), ia_s.at[k], ia_r.at[(NZ - k) % NZ], line(k)
        )

    def fwd(k):
        block = rows(img, img_at(k), N2)
        return remote(em if k == 0 else block, block, if_s.at[k], ia_r.at[k], sib)

    def ta(k, c):
        return remote(
            rows(em, c * N, N), rows(txt, txt_at(back_slot(k)), N),
            ta_s.at[2 * k + c], ta_r.at[back_slot(k)], plane(k, c),
        )

    @pl.when(first)
    def _():
        for k in line_order:
            ia(k).start()
        fwd(0).start()
        img[0:N2, :] = em[...]

    @pl.when(core == 1)
    def _():
        ta(0, 0).start()
        for k in plane_order:
            ta(k, 0).start()
            ta(k, 1).start()
        txt[0:N, :] = em[N:N2, :]

    wo_copy = remote(wfull, wother, wo_s, wo_r, sib)
    wo_copy.start()

    scale = lscale[0]
    neg_scale, neg_bias = -LOG2E * lscale[0], -LOG2E * lbias[0]

    def take_image(k):
        @pl.when(first)
        def _():
            if k:
                arrived(rows(img, img_at(k), N2), ia_r.at[k], ia_s.at[0])
                fwd(k).start()

        @pl.when(core == 1)
        def _():
            arrived(rows(img, img_at(k), N2), ia_r.at[k], ia_s.at[0])

    def take_text(k):
        if k:
            arrived(rows(txt, txt_at(k), N), ta_r.at[k], ta_s.at[0])
        else:

            @pl.when(first)
            def _():
                arrived(rows(txt, 0, N), ta_r.at[0], ta_s.at[0])

    def tile(i, j, diagonal=False):
        block = img[pl.ds(pl.multiple_of(i * B, B), B), :]
        weight = block[:, E : E + 1].astype(F32) + block[:, E + 1 : E + 2].astype(F32)
        other = txt[pl.ds(pl.multiple_of(j * B, B), B), :]
        e = jnp.exp2(neg_scale * dot(block, other, ((1,), (1,))) + neg_bias)
        value = weight / (1.0 + e)
        if diagonal:
            r = lax.broadcasted_iota(jnp.int32, (B, B), 0)
            c = lax.broadcasted_iota(jnp.int32, (B, B), 1)
            value = jnp.where((r == c + core * N) & (c < N), -value * e, value)
        g[pl.ds(pl.multiple_of(i * B, B), B), pl.ds(pl.multiple_of(j * B, B), B)] = value.astype(BF)

    for t in range(NZ * N2 // B):
        for k in SHEET[4 * t : 4 * t + 4]:
            take_text(k)
        for k in LINE[2 * t : 2 * t + 2]:
            take_image(k)
        tile(t, t, t == 0)
        if t:

            @pl.loop(0, t)
            def _(i, t=t):
                tile(i, t)
                tile(t, i)

    def pi(k):
        return remote(
            rows(p_out, img_at(k), N2), rows(p_in, img_at(k), N2), pi_s.at[k], pi_r.at[k], sib
        )

    def ri(k):
        return remote(
            rows(p_out, img_at(k), N2), rows(rs_i, (NZ - k) % NZ * N2, N2),
            ri_s.at[k], ri_r.at[(NZ - k) % NZ], line(k),
        )

    def rt(k):
        return remote(
            rows(t_out, txt_at(k), N), rows(rs_t, (core * PLANE + back_slot(k)) * N, N),
            rt_s.at[k], rt_r.at[core * PLANE + back_slot(k)], plane(k, 1),
        )

    def combine(k):
        at = img_at(k)
        arrived(rows(p_in, at, N2), pi_r.at[k], pi_s.at[k])
        total = p_f[at : at + N2, :] + p_in[at : at + N2, :].astype(F32)
        if k:
            p_out[at : at + N2, :] = total.astype(BF)
            ri(k).start()
        else:
            p_f[0:N2, :] = total

    back_order = LINE[::-1]
    for n in range(NZ + 1):
        if n < NZ:
            k = back_order[n]
            at = img_at(k)
            p_f[at : at + N2, :] = dot(g[at : at + N2, :], txt[:, 0:E], ((1,), (0,)))

            @pl.when(core == 1)
            def _(k=k, at=at):
                p_out[at : at + N2, :] = p_f[at : at + N2, :].astype(BF)
                pi(k).start()

            b = NZ - 1 - n
            block = dot(g[:, b * N2 : (b + 1) * N2], img[:, 0:E], ((0,), (0,)))
            t_out[b * N2 : (b + 1) * N2, :] = block.astype(BF)
            for k in SHEET[2 * b : 2 * b + 2]:
                if k:
                    rt(k).start()
        if n:

            @pl.when(first)
            def _(n=n):
                combine(back_order[n - 1])

    @pl.when(first)
    def _():
        rt(0).start()
        for k in line_order:
            arrived(rows(rs_i, k * N2, N2), ri_r.at[k], ri_s.at[0])
            p_f[0:N2, :] += rs_i[k * N2 : (k + 1) * N2, :].astype(F32)

    @pl.when(core == 1)
    def _(block=block):
        arrived(rows(rs_t, 0, N), rt_r.at[0], rt_s.at[0])
        p_f[0:N, :] = rs_t[0:N, :].astype(F32)
        p_f[N:N2, :] = block[0:N, :]
        for k in plane_order:
            for c in range(2):
                at = c * PLANE + k
                arrived(rows(rs_t, at * N, N), rt_r.at[at], rt_s.at[0])
                p_f[c * N : (c + 1) * N, :] += rs_t[at * N : (at + 1) * N, :].astype(F32)

    grad = p_f[0:N2, :] * scale
    u = unit[...]
    back = ((grad - u * jnp.sum(u * grad, axis=1, keepdims=True)) / length[:, 0:1]).astype(BF)
    bk[...] = back
    bk_copy = remote(rows(bk, theirs, N), bo, bk_s, bk_r, sib)
    bk_copy.start()

    dwf[...] = dot(a[...], back, ((0,), (0,)))

    def piece(px, py):
        return (lax.rem(px, 2) * 2 + lax.div(px, 2)) * NY + py

    def r1_copy(k):
        return remote(
            rows(dws, k * PR, PR), rows(r1, back_slot(k) * PR, PR),
            r1_s.at[k], r1_r.at[back_slot(k)], plane(k),
        )

    def part(k):
        q = piece(lax.rem(x + k // NY, NX), lax.rem(y + k % NY, NY))
        return dwf[pl.ds(pl.multiple_of(q * PIECE, 8), PIECE), :]

    for k in plane_order:
        dws[k * PR : (k + 1) * PR, :] = jnp.concatenate(
            [part(k), jnp.zeros((PR - PIECE, E), F32)], axis=0
        ).astype(BF)
        r1_copy(k).start()

    arrived(bo, bk_r, bk_s)
    arrived(wother, wo_r, wo_s)
    own = bk[pl.ds(mine, N), :]
    moved = dot(onehot, own, ((1,), (0,))).astype(BF)
    gsv[core] = dot(moved, wfull[...], ((1,), (1,)))
    moved = dot(onehot, bo[...], ((1,), (0,))).astype(BF)
    gsv[1 - core] = dot(moved, wother[...], ((1,), (1,)))
    gs_copies = [
        pltpu.make_async_copy(gsv.at[0], gs_i, gs_s.at[0]),
        pltpu.make_async_copy(gsv.at[1], gs_t, gs_s.at[1]),
    ]
    for copy in gs_copies:
        copy.start()

    total = part(0)
    for k in plane_order:
        arrived(rows(r1, k * PR, PR), r1_r.at[k], r1_s.at[k])
        total += r1[k * PR : (k + 1) * PR, :].astype(F32)[0:PIECE, :]
    whole = jnp.concatenate([total, jnp.zeros((PR - PIECE, E), F32)], axis=0)
    psum[...] = whole.astype(BF)

    rank = lax.rem(z + 4 * core, NZ)

    def rank_of(k):
        return lax.rem(rank + k, NZ)

    def tile(ref, at, base=0):
        return rows(ref, pl.multiple_of(base + at * 16, 16), 16)

    def r2_copy(k):
        back_k = (NZ - k) % NZ
        return remote(
            tile(psum, rank_of(k)), rows(r2, back_k * 16, 16), r2_s.at[k], r2_r.at[back_k], line(k)
        )

    for k in line_order:

        @pl.when(rank_of(k) < 5)
        def _(k=k):
            r2_copy(k).start()

    def f_copy(k):
        return remote(res, tile(fin, rank), f_s.at[k], f_r.at[(NZ - k) % NZ], line(k))

    @pl.when(rank < 5)
    def _():
        total = psum[pl.ds(pl.multiple_of(rank * 16, 16), 16), :].astype(F32)
        for k in line_order:
            arrived(rows(r2, k * 16, 16), r2_r.at[k], r2_s.at[k])
            total += r2[k * 16 : (k + 1) * 16, :].astype(F32)
        res[...] = total.astype(BF)
        for k in line_order:
            f_copy(k).start()
        fin[pl.ds(pl.multiple_of(rank * 16, 16), 16), :] = total.astype(BF)

    for k in line_order:

        @pl.when(rank_of(k) < 5)
        def _(k=k):
            arrived(tile(fin, rank_of(k)), f_r.at[k], f_s.at[k])

    def held(px, py):
        return pl.multiple_of((lax.div(px, 2) * NY + py) * PR, PR)

    mates = [k for k in plane_order if (k // NY) % 2 == 0]

    def mate(k):
        return lax.rem(x + k // NY, NX), lax.rem(y + k % NY, NY)

    def ag_copy(k):
        return remote(
            fin, gw.at[core, pl.ds(held(x, y), PR), :],
            ag_s.at[k], ag_r.at[back_slot(k)], plane(k),
        )

    def ad_copy(k):
        block = gw.at[core, pl.ds(held(*mate(k)), PR), :]
        return remote(fin if k == 0 else block, block, ad_s.at[k], ad_r.at[k], sib)

    for k in mates:
        ag_copy(k).start()
    ad_copy(0).start()
    own_copy = pltpu.make_async_copy(fin, gw.at[core, pl.ds(held(x, y), PR), :], own_s)
    own_copy.start()
    for k in mates:
        arrived(gw.at[core, pl.ds(held(*mate(k)), PR), :], ag_r.at[k], ag_s.at[k])
        ad_copy(k).start()
    for k in [0] + mates:
        arrived(gw.at[1 - core, pl.ds(held(*mate(k)), PR), :], ad_r.at[k], ad_s.at[k])

    for copy in heads + [rows_copy, c_copy, wo_copy, bk_copy]:
        copy.wait_send()

    @pl.when(first)
    def _():
        for k in line_order:
            ia(k).wait_send()
            ri(k).wait_send()
        for k in LINE:
            fwd(k).wait_send()
        rt(0).wait_send()

    @pl.when(core == 1)
    def _():
        for k in LINE:
            pi(k).wait_send()
        ta(0, 0).wait_send()
        for k in plane_order:
            ta(k, 0).wait_send()
            ta(k, 1).wait_send()

    for k in plane_order:
        rt(k).wait_send()
        r1_copy(k).wait_send()
    for k in line_order:

        @pl.when(rank_of(k) < 5)
        def _(k=k):
            r2_copy(k).wait_send()

    @pl.when(rank < 5)
    def _():
        for k in line_order:
            f_copy(k).wait_send()

    for k in mates:
        ag_copy(k).wait_send()
    for k in [0] + mates:
        ad_copy(k).wait_send()
    own_copy.wait()
    for copy in gs_copies:
        copy.wait()


def body(sup_i, sup_t, selected, buckets, weights, head_i, head_t, lscale, lbias, oscale):
    vmem = pl.BlockSpec(memory_space=pltpu.VMEM)
    smem = pl.BlockSpec(memory_space=pltpu.SMEM)
    hbm = pl.BlockSpec(memory_space=pl.ANY)

    def space(shape, dtype=BF):
        return pltpu.VMEM(shape, dtype)

    dma = pltpu.SemaphoreType.DMA
    buffers = [
        space((S, D)), space((S, D)), space((N2, D)), space((N, D)), space((16, 128), F32), space((D, E)), space((D, E)),
        space((N2, E), F32), space((N2, 128), F32),
        space((N2, EP)), space((NZ * N2, EP)), space((PLANE * N, EP)),
        space((NZ * N2, PLANE * N)),
        space((NZ * N2, E), F32), space((NZ * N2, E)), space((NZ * N2, E)), space((PLANE * N, E)),
        space((NZ * N2, E)), space((2 * PLANE * N, E)),
        space((N2, E)), space((N, E)), space((2, S, D), F32), space((D, E), F32),
        space((PLANE * PR, E)), space((PLANE * PR, E)), space((PR, E)), space((NZ * 16, E)),
        space((PR, E)), space((16, E)),
    ]
    counts = [
        3, 2, 2, 0, 0, 0, 0, 0, 0,
        NZ, NZ, NZ, 2 * PLANE, PLANE, NZ, NZ, NZ, NZ, PLANE, 2 * PLANE,
        0, 0, 2, PLANE, PLANE, NZ, NZ, NZ, NZ, 0, PLANE, PLANE, PLANE, PLANE,
    ]
    sems = [dma((n,)) if n else dma for n in counts]
    gs_i, gs_t, gw = pl.pallas_call(
        kernel,
        out_shape=(
            jax.ShapeDtypeStruct((S, D), F32),
            jax.ShapeDtypeStruct((S, D), F32),
            jax.ShapeDtypeStruct((2, 8 * PR, E), BF),
        ),
        in_specs=[hbm] * 2 + [vmem] * 2 + [smem] + [hbm] * 2 + [smem] * 3,
        out_specs=(hbm, hbm, hbm),
        scratch_shapes=buffers + sems,
        compiler_params=pltpu.CompilerParams(
            collective_id=0, has_side_effects=True, vmem_limit_bytes=56 * 1024 * 1024
        ),
    )(
        sup_i, sup_t, selected.reshape(1, N), buckets.reshape(1, N), weights,
        head_i, head_t, lscale, lbias, oscale,
    )
    gw = gw.reshape(2, 8, PR, E)[:, :, 0:PIECE, :].reshape(2, H, E).astype(F32)
    return gw[0], gw[1], gs_i, gs_t


def solution(mesh):
    both = P(("dp", "fsdp"))
    wide = P(("dp", "fsdp"), None)
    head = P("fsdp", None)
    in_specs = (wide, wide, both, both, P(), head, head, P(), P(), P())
    out_specs = (head, head, wide, wide)
    return jax.shard_map(body, mesh=mesh, in_specs=in_specs, out_specs=out_specs, check_vma=False)
```

```python
import functools

import jax
import jax.numpy as jnp
from jax import lax
from jax.experimental import pallas as pl
from jax.experimental.pallas import tpu as pltpu
from jax.sharding import PartitionSpec as P

MESH = pl.DeviceIdType.MESH
BF = jnp.bfloat16
F32 = jnp.float32
NX, NY, NZ = 4, 4, 8
PLANE = NX * NY
PAIRS = 16384
N = 64
N2 = 2 * N
S = 320
D = 1152
H = D // 2
E = 576
EP = 640
PIECE = 48
Z_ROWS = PIECE * NZ // 2
B = 256
NB = 16
LOG2E = 1.4426950408889634


def hops(k):
    return min(k // NY, NX - k // NY) + min(k % NY, NY - k % NY)


def back_slot(k):
    return (-(k // NY)) % NX * NY + (-(k % NY)) % NY


LINE = (0, 1, 7, 2, 6, 3, 5, 4)
SHEET = tuple(sorted(range(PLANE), key=lambda k: (hops(k), k)))


def place():
    dp, x_lo = lax.axis_index("dp"), lax.axis_index("fsdp")
    core = lax.rem(dp, 2)
    y = lax.rem(lax.div(dp, 2), NY)
    x = lax.rem(lax.div(dp, 2 * NY), 2) * 2 + x_lo
    z = lax.div(dp, 4 * NY)
    return x, y, z, core


def device(x, y, z, core):
    return (((z * 2 + lax.div(x, 2)) * NY + y) * 2 + core, lax.rem(x, 2))


def dot(a, b, contract):
    return lax.dot_general(a, b, (contract, ((), ())), preferred_element_type=F32)


def kernel(
    sup_i, sup_t, sel, bkt, wts, head_i, head_t, lscale, lbias, oscale,
    gs_i, gs_t, gw,
    va, vt, a, stage, cbuf, wfull, wother, unit, length,
    em, img, txt, g, p_f, p_out, p_in, t_out, rs_i, rs_t,
    bk, bo, gsv, dwf, dws, dwz, r1, rz, r3, zsum, zfin, psum, r2, fin, res,
    in_s, w_s, w_r, rows_s, rows_r, c_s, c_r, wo_s, wo_r,
    ia_s, ia_r, if_s, ta_s, ta_r, pi_s, pi_r, ri_s, ri_r, rt_s, rt_r,
    bk_s, bk_r, gs_s, r1_s, r1_r, rz_s, rz_r, r3_s, r3_r, r2_s, r2_r, f_s, f_r,
    zg_s, zg_r, zd_s, zd_r, own_s, ag_s, ag_r, ad_s, ad_r,
):
    x, y, z, core = place()
    half = lax.rem(x, 2)
    sib = device(x, y, z, 1 - core)
    first = core == 0

    def line(k, c=core):
        return device(x, y, lax.rem(z + k, NZ), c)

    def plane(k, c=core):
        return device(lax.rem(x + k // NY, NX), lax.rem(y + k % NY, NY), z, c)

    def remote(src, dst, send, recv, to):
        return pltpu.make_async_remote_copy(
            src_ref=src, dst_ref=dst, send_sem=send, recv_sem=recv,
            device_id=to, device_id_type=MESH,
        )

    def arrived(dst, recv, send):
        remote(dst, dst, send, recv, sib).wait_recv()

    def rows(ref, start, count):
        return ref.at[pl.ds(start, count), :]

    barrier = pltpu.get_barrier_semaphore()

    def greet(to):
        pl.semaphore_signal(barrier, inc=1, device_id=to, device_id_type=MESH)

    h_off = pl.multiple_of(half * H, H)
    sup_copies = [
        pltpu.make_async_copy(sup_i, va, in_s.at[0]),
        pltpu.make_async_copy(sup_t, vt, in_s.at[1]),
    ]
    head_copy = pltpu.make_async_copy(head_i, rows(wfull, h_off, H), in_s.at[2])
    for copy in sup_copies:
        copy.start()

    @pl.when(first)
    def _():
        head_copy.start()

    @pl.when(core == 1)
    def _():
        pltpu.make_async_copy(head_t, rows(wfull, h_off, H), in_s.at[2]).start()

    greet(sib)
    for k in range(1, NZ):
        greet(line(k))
    for k in range(1, PLANE):
        greet(plane(k, 0))
        greet(plane(k, 1))

    for copy in sup_copies:
        copy.wait()
    onehot = (lax.broadcasted_iota(jnp.int32, (S, N), 0) == sel[...]).astype(BF)
    rows_i = dot(onehot, va[...], ((0,), (0,))).astype(BF)
    rows_t = dot(onehot, vt[...], ((0,), (0,))).astype(BF)
    mine = pl.multiple_of(core * N, N)
    a[pl.ds(mine, N), :] = jnp.where(first, rows_i, rows_t)
    stage[...] = jnp.where(first, rows_t, rows_i)
    weight = jnp.zeros((1, N), F32)
    for n in range(NB):
        weight = jnp.where(bkt[...] == n, wts[:, n : n + 1], weight)
    weight = oscale[...] * weight / PAIRS
    cbuf[pl.ds(pl.multiple_of(core * 8, 8), 8), :] = jnp.concatenate(
        [jnp.broadcast_to(weight, (8, N)), jnp.zeros((8, N), F32)], axis=1
    )

    head_copy.wait()
    pl.semaphore_wait(barrier, 1 + (NZ - 1) + 2 * (PLANE - 1))

    heads = []
    for k, step in ((0, 1), (1, NX - 1)):
        src = rows(wfull, pl.multiple_of(h_off + k * (H // 2), H // 2), H // 2)
        heads.append(
            remote(src, src, w_s.at[k], w_r.at[k], device(lax.rem(x + step, NX), y, z, core))
        )
    rows_copy = remote(stage, rows(a, mine, N), rows_s, rows_r, sib)
    c_own = rows(cbuf, pl.multiple_of(core * 8, 8), 8)
    c_copy = remote(c_own, c_own, c_s, c_r, sib)
    for copy in heads:
        copy.start()
    rows_copy.start()
    c_copy.start()
    theirs = pl.multiple_of((1 - core) * N, N)
    o_off = pl.multiple_of((1 - half) * H, H)
    arrived(rows(a, theirs, N), rows_r, rows_s)
    arrived(rows(cbuf, pl.multiple_of((1 - core) * 8, 8), 8), c_r, c_s)
    for k in range(2):
        arrived(
            rows(wfull, pl.multiple_of(o_off + k * (H // 2), H // 2), H // 2), w_r.at[k], w_s.at[k]
        )

    raw = dot(a[...], wfull[...], ((1,), (0,)))
    size = jnp.sqrt(jnp.sum(raw * raw, axis=1, keepdims=True) + 1e-06)
    u = raw / size
    unit[...] = u
    length[...] = jnp.broadcast_to(size, (N2, 128))
    eye = lax.broadcasted_iota(jnp.int32, (N, N), 0) == lax.broadcasted_iota(jnp.int32, (N, N), 1)
    column = jnp.concatenate(
        [
            jnp.sum(jnp.where(eye, cbuf[8 * c : 8 * c + 1, 0:N], 0.0), axis=1, keepdims=True)
            for c in range(2)
        ],
        axis=0,
    )
    column = jnp.where(first, column, jnp.zeros_like(column))
    high = column.astype(BF)
    low = (column - high.astype(F32)).astype(BF)
    em[...] = jnp.concatenate([u.astype(BF), high, low, jnp.zeros((N2, EP - E - 2), BF)], axis=1)

    line_order, plane_order = LINE[1:], SHEET[1:]

    def img_at(k):
        return LINE.index(k % NZ) * N2

    def txt_at(k):
        return SHEET.index(k) * N

    def ia(k):
        return remote(
            em, rows(img, img_at(-k), N2), ia_s.at[k], ia_r.at[(NZ - k) % NZ], line(k)
        )

    def fwd(k):
        block = rows(img, img_at(k), N2)
        return remote(em if k == 0 else block, block, if_s.at[k], ia_r.at[k], sib)

    def ta(k, c):
        return remote(
            rows(em, c * N, N), rows(txt, txt_at(back_slot(k)), N),
            ta_s.at[2 * k + c], ta_r.at[back_slot(k)], plane(k, c),
        )

    @pl.when(first)
    def _():
        for k in line_order:
            ia(k).start()
        fwd(0).start()
        img[0:N2, :] = em[...]

    @pl.when(core == 1)
    def _():
        ta(0, 0).start()
        for k in plane_order:
            ta(k, 0).start()
            ta(k, 1).start()
        txt[0:N, :] = em[N:N2, :]

    wo_copy = remote(wfull, wother, wo_s, wo_r, sib)
    wo_copy.start()

    scale = lscale[...]
    neg_scale, neg_bias = -LOG2E * lscale[...], -LOG2E * lbias[...]

    def take_image(k):
        @pl.when(first)
        def _():
            if k:
                arrived(rows(img, img_at(k), N2), ia_r.at[k], ia_s.at[0])
                fwd(k).start()

        @pl.when(core == 1)
        def _():
            arrived(rows(img, img_at(k), N2), ia_r.at[k], ia_s.at[0])

    def take_text(k):
        if k:
            arrived(rows(txt, txt_at(k), N), ta_r.at[k], ta_s.at[0])
        else:

            @pl.when(first)
            def _():
                arrived(rows(txt, 0, N), ta_r.at[0], ta_s.at[0])

    def tile(i, j, diagonal=False):
        block = img[pl.ds(pl.multiple_of(i * B, B), B), :]
        weight = block[:, E : E + 1].astype(F32) + block[:, E + 1 : E + 2].astype(F32)
        other = txt[pl.ds(pl.multiple_of(j * B, B), B), :]
        e = jnp.exp2(neg_scale * dot(block, other, ((1,), (1,))) + neg_bias)
        value = weight / (1.0 + e)
        if diagonal:
            r = lax.broadcasted_iota(jnp.int32, (B, B), 0)
            c = lax.broadcasted_iota(jnp.int32, (B, B), 1)
            value = jnp.where((r == c + core * N) & (c < N), -value * e, value)
        g[pl.ds(pl.multiple_of(i * B, B), B), pl.ds(pl.multiple_of(j * B, B), B)] = value.astype(BF)

    for t in range(NZ * N2 // B):
        for k in SHEET[4 * t : 4 * t + 4]:
            take_text(k)
        for k in LINE[2 * t : 2 * t + 2]:
            take_image(k)
        tile(t, t, t == 0)
        if t:

            @pl.loop(0, t)
            def _(i, t=t):
                tile(i, t)
                tile(t, i)

    def pi(k):
        return remote(
            rows(p_out, img_at(k), N2), rows(p_in, img_at(k), N2), pi_s.at[k], pi_r.at[k], sib
        )

    def ri(k):
        return remote(
            rows(p_out, img_at(k), N2), rows(rs_i, (NZ - k) % NZ * N2, N2),
            ri_s.at[k], ri_r.at[(NZ - k) % NZ], line(k),
        )

    def rt(k):
        return remote(
            rows(t_out, txt_at(k), N), rows(rs_t, (core * PLANE + back_slot(k)) * N, N),
            rt_s.at[k], rt_r.at[core * PLANE + back_slot(k)], plane(k, 1),
        )

    def combine(k):
        at = img_at(k)
        arrived(rows(p_in, at, N2), pi_r.at[k], pi_s.at[k])
        total = p_f[at : at + N2, :] + p_in[at : at + N2, :].astype(F32)
        if k:
            p_out[at : at + N2, :] = total.astype(BF)
            ri(k).start()
        else:
            p_f[0:N2, :] = total

    back_order = LINE[::-1]
    for n in range(NZ + 1):
        if n < NZ:
            k = back_order[n]
            at = img_at(k)
            p_f[at : at + N2, :] = dot(g[at : at + N2, :], txt[:, 0:E], ((1,), (0,)))

            @pl.when(core == 1)
            def _(k=k, at=at):
                p_out[at : at + N2, :] = p_f[at : at + N2, :].astype(BF)
                pi(k).start()

            b = NZ - 1 - n
            block = dot(g[:, b * N2 : (b + 1) * N2], img[:, 0:E], ((0,), (0,)))
            t_out[b * N2 : (b + 1) * N2, :] = block.astype(BF)
            for k in SHEET[2 * b : 2 * b + 2]:
                if k:
                    rt(k).start()
        if n:

            @pl.when(first)
            def _(n=n):
                combine(back_order[n - 1])

    @pl.when(first)
    def _():
        rt(0).start()
        for k in line_order:
            arrived(rows(rs_i, k * N2, N2), ri_r.at[k], ri_s.at[0])
            p_f[0:N2, :] += rs_i[k * N2 : (k + 1) * N2, :].astype(F32)

    @pl.when(core == 1)
    def _(block=block):
        arrived(rows(rs_t, 0, N), rt_r.at[0], rt_s.at[0])
        p_f[0:N, :] = rs_t[0:N, :].astype(F32)
        p_f[N:N2, :] = block[0:N, :]
        for k in plane_order:
            for c in range(2):
                at = c * PLANE + k
                arrived(rows(rs_t, at * N, N), rt_r.at[at], rt_s.at[0])
                p_f[c * N : (c + 1) * N, :] += rs_t[at * N : (at + 1) * N, :].astype(F32)

    grad = p_f[0:N2, :] * scale
    u = unit[...]
    back = ((grad - u * jnp.sum(u * grad, axis=1, keepdims=True)) / length[:, 0:1]).astype(BF)
    bk[...] = back
    bk_copy = remote(rows(bk, theirs, N), bo, bk_s, bk_r, sib)
    bk_copy.start()

    dwf[...] = dot(a[...], back, ((0,), (0,)))

    def z_row(k):
        at = lax.rem(z + k, NZ)
        return lax.div(at, NZ // 2), lax.rem(at, NZ // 2) * PIECE

    def p_row(k):
        px, py = lax.rem(x + k // NY, NX), lax.rem(y + k % NY, NY)
        return lax.rem(px, 2), Z_ROWS + (lax.div(px, 2) * NY + py) * PIECE

    def part(where):
        which, row = where
        return dwf[pl.ds(pl.multiple_of(which * H + row, PIECE), PIECE), :]

    def block(ref, k):
        return rows(ref, k * PIECE, PIECE)

    def r1_copy(k):
        return remote(
            block(dws, k), block(r1, back_slot(k)), r1_s.at[k], r1_r.at[back_slot(k)], plane(k)
        )

    def rz_copy(k):
        back_k = (NZ - k) % NZ
        return remote(block(dwz, k), block(rz, back_k), rz_s.at[k], rz_r.at[back_k], line(k))

    def fill(ref, k, where):
        ref[k * PIECE : (k + 1) * PIECE, :] = part(where).astype(BF)

    for n, k in enumerate(plane_order[::-1]):
        if n % 2 == 0 and n // 2 < NZ - 1:
            kz = line_order[::-1][n // 2]
            fill(dwz, kz, z_row(kz))
            rz_copy(kz).start()
        fill(dws, k, p_row(k))
        r1_copy(k).start()

    arrived(bo, bk_r, bk_s)
    arrived(wother, wo_r, wo_s)
    own = bk[pl.ds(mine, N), :]
    moved = dot(onehot, own, ((1,), (0,))).astype(BF)
    gsv[core] = dot(moved, wfull[...], ((1,), (1,)))
    moved = dot(onehot, bo[...], ((1,), (0,))).astype(BF)
    gsv[1 - core] = dot(moved, wother[...], ((1,), (1,)))
    gs_copies = [
        pltpu.make_async_copy(gsv.at[0], gs_i, gs_s.at[0]),
        pltpu.make_async_copy(gsv.at[1], gs_t, gs_s.at[1]),
    ]
    for copy in gs_copies:
        copy.start()

    z_half, z_at = z_row(0)
    holder = half == z_half
    total = part((z_half, z_at))
    for k in line_order:
        arrived(block(rz, k), rz_r.at[k], rz_s.at[k])
        total += rz[k * PIECE : (k + 1) * PIECE, :].astype(F32)
    zsum[...] = total.astype(BF)

    def wants(k):
        return lax.rem(x + k // NY, 2) == z_half

    def r3_copy(k):
        return remote(zsum, block(r3, back_slot(k)), r3_s.at[k], r3_r.at[back_slot(k)], plane(k))

    for k in plane_order:

        @pl.when(wants(k))
        def _(k=k):
            r3_copy(k).start()

    dwf[0:PIECE, :] = total

    total = part(p_row(0))
    for k in plane_order:
        arrived(block(r1, k), r1_r.at[k], r1_s.at[k])
        total += r1[k * PIECE : (k + 1) * PIECE, :].astype(F32)
    psum[...] = total.astype(BF)
    rank = lax.rem(z + 4 * core, NZ)

    def rank_of(k):
        return lax.rem(rank + k, NZ)

    def sums(k):
        return lax.rem(rank_of(k), 3) == 0

    def tile_at(k):
        return pl.multiple_of(lax.div(rank_of(k), 3) * 16, 16)

    def r2_copy(k):
        back_k = (NZ - k) % NZ
        return remote(
            rows(psum, tile_at(k), 16), rows(r2, back_k * 16, 16),
            r2_s.at[k], r2_r.at[back_k], line(k),
        )

    for k in line_order:

        @pl.when(sums(k))
        def _(k=k):
            r2_copy(k).start()

    def f_copy(k):
        return remote(res, rows(fin, tile_at(0), 16), f_s.at[k], f_r.at[(NZ - k) % NZ], line(k))

    @pl.when(sums(0))
    def _():
        total = psum[pl.ds(tile_at(0), 16), :].astype(F32)
        for k in line_order:
            arrived(rows(r2, k * 16, 16), r2_r.at[k], r2_s.at[k])
            total += r2[k * 16 : (k + 1) * 16, :].astype(F32)
        res[...] = total.astype(BF)
        for k in line_order:
            f_copy(k).start()
        fin[pl.ds(tile_at(0), 16), :] = total.astype(BF)

    def shelf(modality, row):
        return gw.at[modality, pl.ds(pl.multiple_of(row, PIECE), PIECE), :]

    def zg_copy(k):
        return remote(
            zfin, shelf(core, z_row(0)[1]), zg_s.at[k], zg_r.at[(NZ - k) % NZ], line(k)
        )

    def zd_copy(k, modality=core):
        to = shelf(modality, z_row(k)[1])
        return remote(zfin if k == 0 else to, to, zd_s.at[k], zd_r.at[k], sib)

    def holds(k):
        return z_row(k)[0] == half

    own_z = pltpu.make_async_copy(zfin, shelf(core, z_row(0)[1]), own_s.at[0])

    @pl.when(holder)
    def _():
        for k in plane_order:
            arrived(block(r3, k), r3_r.at[k], r3_s.at[k])
            dwf[0:PIECE, :] += r3[k * PIECE : (k + 1) * PIECE, :].astype(F32)
        zfin[...] = dwf[0:PIECE, :].astype(BF)
        for k in line_order:
            zg_copy(k).start()
        zd_copy(0).start()
        own_z.start()

    for k in line_order:

        @pl.when(sums(k))
        def _(k=k):
            arrived(rows(fin, tile_at(k), 16), f_r.at[k], f_s.at[k])

    mates = [k for k in plane_order if (k // NY) % 2 == 0]

    def ag_copy(k):
        return remote(
            fin, shelf(core, p_row(0)[1]), ag_s.at[k], ag_r.at[back_slot(k)], plane(k)
        )

    def ad_copy(k, modality=core):
        to = shelf(modality, p_row(k)[1])
        return remote(fin if k == 0 else to, to, ad_s.at[k], ad_r.at[k], sib)

    for k in mates:
        ag_copy(k).start()
    ad_copy(0).start()
    own_p = pltpu.make_async_copy(fin, shelf(core, p_row(0)[1]), own_s.at[1])
    own_p.start()
    for k in line_order:

        @pl.when(holds(k))
        def _(k=k):
            arrived(shelf(core, z_row(k)[1]), zg_r.at[k], zg_s.at[k])
            zd_copy(k).start()

    for k in mates:
        arrived(shelf(core, p_row(k)[1]), ag_r.at[k], ag_s.at[k])
        ad_copy(k).start()
    for k in LINE:

        @pl.when(holds(k))
        def _(k=k):
            arrived(shelf(1 - core, z_row(k)[1]), zd_r.at[k], zd_s.at[k])

    for k in [0] + mates:
        arrived(shelf(1 - core, p_row(k)[1]), ad_r.at[k], ad_s.at[k])

    for copy in heads + [rows_copy, c_copy, wo_copy, bk_copy]:
        copy.wait_send()

    @pl.when(first)
    def _():
        for k in line_order:
            ia(k).wait_send()
            ri(k).wait_send()
        for k in LINE:
            fwd(k).wait_send()
        rt(0).wait_send()

    @pl.when(core == 1)
    def _():
        for k in LINE:
            pi(k).wait_send()
        ta(0, 0).wait_send()
        for k in plane_order:
            ta(k, 0).wait_send()
            ta(k, 1).wait_send()

    for k in plane_order:
        rt(k).wait_send()
        r1_copy(k).wait_send()
    for k in line_order:
        rz_copy(k).wait_send()

        @pl.when(sums(k))
        def _(k=k):
            r2_copy(k).wait_send()

    for k in plane_order:

        @pl.when(wants(k))
        def _(k=k):
            r3_copy(k).wait_send()

    @pl.when(sums(0))
    def _():
        for k in line_order:
            f_copy(k).wait_send()

    @pl.when(holder)
    def _():
        for k in line_order:
            zg_copy(k).wait_send()
        own_z.wait()

    for k in LINE:

        @pl.when(holds(k))
        def _(k=k):
            zd_copy(k).wait_send()

    for k in mates:
        ag_copy(k).wait_send()
    for k in [0] + mates:
        ad_copy(k).wait_send()
    own_p.wait()
    for copy in gs_copies:
        copy.wait()


def finish(gw, gs_i, gs_t, out_hi, out_ht, out_i, out_t, narrow, wide, in_s, out_s, gs_s):
    loads = [pltpu.make_async_copy(gw.at[m], narrow.at[m], in_s.at[m]) for m in range(2)]
    for copy in loads:
        copy.start()
    step = S // 4
    copies = []
    for m, (src, dst) in enumerate(((gs_i, out_i), (gs_t, out_t))):
        for n in range(4):
            at = pl.ds(n * step, step)
            copies.append(pltpu.make_async_copy(src.at[at, :], dst.at[at, :], gs_s.at[4 * m + n]))
    for copy in copies:
        copy.start()
    for m, dst in enumerate((out_hi, out_ht)):
        loads[m].wait()
        wide[m] = narrow[m].astype(F32)
        copies.append(pltpu.make_async_copy(wide.at[m], dst, out_s.at[m]))
        copies[-1].start()
    for copy in copies:
        copy.wait()


def body(sup_i, sup_t, selected, buckets, weights, head_i, head_t, lscale, lbias, oscale):
    vmem = pl.BlockSpec(memory_space=pltpu.VMEM)
    hbm = pl.BlockSpec(memory_space=pl.ANY)

    def space(shape, dtype=BF):
        return pltpu.VMEM(shape, dtype)

    dma = pltpu.SemaphoreType.DMA
    buffers = [
        space((S, D)), space((S, D)), space((N2, D)), space((N, D)), space((16, 128), F32),
        space((D, E)), space((D, E)),
        space((N2, E), F32), space((N2, 128), F32),
        space((N2, EP)), space((NZ * N2, EP)), space((PLANE * N, EP)),
        space((NZ * N2, PLANE * N)),
        space((NZ * N2, E), F32), space((NZ * N2, E)), space((NZ * N2, E)), space((PLANE * N, E)),
        space((NZ * N2, E)), space((2 * PLANE * N, E)),
        space((N2, E)), space((N, E)), space((2, S, D), F32), space((D, E), F32),
        space((PLANE * PIECE, E)), space((NZ * PIECE, E)), space((PLANE * PIECE, E)),
        space((NZ * PIECE, E)), space((PLANE * PIECE, E)), space((PIECE, E)), space((PIECE, E)),
        space((PIECE, E)), space((NZ * 16, E)), space((PIECE, E)), space((16, E)),
    ]
    counts = [
        3, 2, 2, 0, 0, 0, 0, 0, 0,
        NZ, NZ, NZ, 2 * PLANE, PLANE, NZ, NZ, NZ, NZ, PLANE, 2 * PLANE,
        0, 0, 2, PLANE, PLANE, NZ, NZ, PLANE, PLANE, NZ, NZ, NZ, NZ,
        NZ, NZ, NZ, NZ, 2, PLANE, PLANE, PLANE, PLANE,
    ]
    sems = [dma((n,)) if n else dma for n in counts]
    gs_i, gs_t, gw = pl.pallas_call(
        kernel,
        out_shape=(
            jax.ShapeDtypeStruct((S, D), F32),
            jax.ShapeDtypeStruct((S, D), F32),
            jax.ShapeDtypeStruct((2, H, E), BF),
        ),
        in_specs=[hbm] * 2 + [vmem] * 3 + [hbm] * 2 + [vmem] * 3,
        out_specs=(hbm, hbm, hbm),
        scratch_shapes=buffers + sems,
        compiler_params=pltpu.CompilerParams(
            collective_id=0, has_side_effects=True, vmem_limit_bytes=56 * 1024 * 1024
        ),
    )(
        sup_i, sup_t, selected.reshape(1, N), buckets.reshape(1, N), weights.reshape(1, NB),
        head_i, head_t, lscale.reshape(1, 1), lbias.reshape(1, 1), oscale.reshape(1, 1),
    )
    return pl.pallas_call(
        finish,
        out_shape=(jax.ShapeDtypeStruct((H, E), F32),) * 2 + (jax.ShapeDtypeStruct((S, D), F32),) * 2,
        in_specs=[hbm] * 3,
        out_specs=(hbm,) * 4,
        scratch_shapes=[space((2, H, E)), space((2, H, E), F32), dma((2,)), dma((2,)), dma((8,))],
    )(gw, gs_i, gs_t)


def solution(mesh):
    both = P(("dp", "fsdp"))
    wide = P(("dp", "fsdp"), None)
    head = P("fsdp", None)
    in_specs = (wide, wide, both, both, P(), head, head, P(), P(), P())
    out_specs = (head, head, wide, wide)
    return jax.shard_map(body, mesh=mesh, in_specs=in_specs, out_specs=out_specs, check_vma=False)
```

```python
import functools

import jax
import jax.numpy as jnp
from jax import lax
from jax.experimental import pallas as pl
from jax.experimental.pallas import tpu as pltpu
from jax.sharding import PartitionSpec as P

MESH = pl.DeviceIdType.MESH
BF = jnp.bfloat16
F32 = jnp.float32
NX, NY, NZ = 4, 4, 8
PLANE = NX * NY
PAIRS = 16384
N = 64
N2 = 2 * N
S = 320
D = 1152
H = D // 2
E = 576
EP = 640
PIECE = 48
TILES = 16
Z_ROWS = PIECE * NZ // 2
B = 256
NB = 16
LOG2E = 1.4426950408889634


def hops(k):
    return min(k // NY, NX - k // NY) + min(k % NY, NY - k % NY)


def back_slot(k):
    return (-(k // NY)) % NX * NY + (-(k % NY)) % NY


LINE = (0, 1, 7, 2, 6, 3, 5, 4)
SHEET = tuple(sorted(range(PLANE), key=lambda k: (hops(k), k)))


def place():
    dp, x_lo = lax.axis_index("dp"), lax.axis_index("fsdp")
    core = lax.rem(dp, 2)
    y = lax.rem(lax.div(dp, 2), NY)
    x = lax.rem(lax.div(dp, 2 * NY), 2) * 2 + x_lo
    z = lax.div(dp, 4 * NY)
    return x, y, z, core


def device(x, y, z, core):
    return (((z * 2 + lax.div(x, 2)) * NY + y) * 2 + core, lax.rem(x, 2))


def dot(a, b, contract):
    return lax.dot_general(a, b, (contract, ((), ())), preferred_element_type=F32)


def kernel(
    sup_i, sup_t, sel, bkt, wts, head_i, head_t, lscale, lbias, oscale,
    gs_i, gs_t, gw,
    va, vt, a, stage, cbuf, wfull, wother, unit, length,
    em, img, txt, g, p_f, p_out, p_in, t_out, rs_i, rs_t,
    bk, bo, gsv, dwf, dws, dwz, r1, rz, r3, zsum, zres, zft, zfin, psum, r2, res, fint, fin, gwv,
    in_s, w_s, w_r, rows_s, rows_r, c_s, c_r, wo_s, wo_r,
    ia_s, ia_r, if_s, ta_s, ta_r, pi_s, pi_r, ri_s, ri_r, rt_s, rt_r,
    bk_s, bk_r, gs_s, r1_s, r1_r, rz_s, rz_r, r3_s, r3_r, e3_s, e3_r, r2_s, r2_r, f_s, f_r,
    zg_s, zg_r, zd_s, zd_r, own_s, gw_s, ag_s, ag_r, ad_s, ad_r,
):
    x, y, z, core = place()
    half = lax.rem(x, 2)
    sib = device(x, y, z, 1 - core)
    first = core == 0

    def line(k, c=core):
        return device(x, y, lax.rem(z + k, NZ), c)

    def plane(k, c=core):
        return device(lax.rem(x + k // NY, NX), lax.rem(y + k % NY, NY), z, c)

    def remote(src, dst, send, recv, to):
        return pltpu.make_async_remote_copy(
            src_ref=src, dst_ref=dst, send_sem=send, recv_sem=recv,
            device_id=to, device_id_type=MESH,
        )

    def arrived(dst, recv, send):
        remote(dst, dst, send, recv, sib).wait_recv()

    def rows(ref, start, count):
        return ref.at[pl.ds(start, count), :]

    barrier = pltpu.get_barrier_semaphore()

    def greet(to):
        pl.semaphore_signal(barrier, inc=1, device_id=to, device_id_type=MESH)

    h_off = pl.multiple_of(half * H, H)
    sup_copies = [
        pltpu.make_async_copy(sup_i, va, in_s.at[0]),
        pltpu.make_async_copy(sup_t, vt, in_s.at[1]),
    ]
    head_copy = pltpu.make_async_copy(head_i, rows(wfull, h_off, H), in_s.at[2])
    for copy in sup_copies:
        copy.start()

    @pl.when(first)
    def _():
        head_copy.start()

    @pl.when(core == 1)
    def _():
        pltpu.make_async_copy(head_t, rows(wfull, h_off, H), in_s.at[2]).start()

    greet(sib)
    for k in range(1, NZ):
        greet(line(k))
    for k in range(1, PLANE):
        greet(plane(k, 0))
        greet(plane(k, 1))

    for copy in sup_copies:
        copy.wait()
    onehot = (lax.broadcasted_iota(jnp.int32, (S, N), 0) == sel[...]).astype(BF)
    rows_i = dot(onehot, va[...], ((0,), (0,))).astype(BF)
    rows_t = dot(onehot, vt[...], ((0,), (0,))).astype(BF)
    mine = pl.multiple_of(core * N, N)
    a[pl.ds(mine, N), :] = jnp.where(first, rows_i, rows_t)
    stage[...] = jnp.where(first, rows_t, rows_i)
    weight = jnp.zeros((1, N), F32)
    for n in range(NB):
        weight = jnp.where(bkt[...] == n, wts[:, n : n + 1], weight)
    weight = oscale[...] * weight / PAIRS
    cbuf[pl.ds(pl.multiple_of(core * 8, 8), 8), :] = jnp.concatenate(
        [jnp.broadcast_to(weight, (8, N)), jnp.zeros((8, N), F32)], axis=1
    )

    head_copy.wait()
    pl.semaphore_wait(barrier, 1 + (NZ - 1) + 2 * (PLANE - 1))

    heads = []
    for k, step in ((0, 1), (1, NX - 1)):
        src = rows(wfull, pl.multiple_of(h_off + k * (H // 2), H // 2), H // 2)
        heads.append(
            remote(src, src, w_s.at[k], w_r.at[k], device(lax.rem(x + step, NX), y, z, core))
        )
    rows_copy = remote(stage, rows(a, mine, N), rows_s, rows_r, sib)
    c_own = rows(cbuf, pl.multiple_of(core * 8, 8), 8)
    c_copy = remote(c_own, c_own, c_s, c_r, sib)
    for copy in heads:
        copy.start()
    rows_copy.start()
    c_copy.start()
    theirs = pl.multiple_of((1 - core) * N, N)
    o_off = pl.multiple_of((1 - half) * H, H)
    arrived(rows(a, theirs, N), rows_r, rows_s)
    arrived(rows(cbuf, pl.multiple_of((1 - core) * 8, 8), 8), c_r, c_s)
    for k in range(2):
        arrived(
            rows(wfull, pl.multiple_of(o_off + k * (H // 2), H // 2), H // 2), w_r.at[k], w_s.at[k]
        )

    raw = dot(a[...], wfull[...], ((1,), (0,)))
    size = jnp.sqrt(jnp.sum(raw * raw, axis=1, keepdims=True) + 1e-06)
    u = raw / size
    unit[...] = u
    length[...] = jnp.broadcast_to(size, (N2, 128))
    eye = lax.broadcasted_iota(jnp.int32, (N, N), 0) == lax.broadcasted_iota(jnp.int32, (N, N), 1)
    column = jnp.concatenate(
        [
            jnp.sum(jnp.where(eye, cbuf[8 * c : 8 * c + 1, 0:N], 0.0), axis=1, keepdims=True)
            for c in range(2)
        ],
        axis=0,
    )
    column = jnp.where(first, column, jnp.zeros_like(column))
    high = column.astype(BF)
    low = (column - high.astype(F32)).astype(BF)
    em[...] = jnp.concatenate([u.astype(BF), high, low, jnp.zeros((N2, EP - E - 2), BF)], axis=1)

    line_order, plane_order = LINE[1:], SHEET[1:]

    def img_at(k):
        return LINE.index(k % NZ) * N2

    def txt_at(k):
        return SHEET.index(k) * N

    def ia(k):
        return remote(
            em, rows(img, img_at(-k), N2), ia_s.at[k], ia_r.at[(NZ - k) % NZ], line(k)
        )

    def fwd(k):
        block = rows(img, img_at(k), N2)
        return remote(em if k == 0 else block, block, if_s.at[k], ia_r.at[k], sib)

    def ta(k, c):
        return remote(
            rows(em, c * N, N), rows(txt, txt_at(back_slot(k)), N),
            ta_s.at[2 * k + c], ta_r.at[back_slot(k)], plane(k, c),
        )

    @pl.when(first)
    def _():
        for k in line_order:
            ia(k).start()
        fwd(0).start()
        img[0:N2, :] = em[...]

    @pl.when(core == 1)
    def _():
        ta(0, 0).start()
        for k in plane_order:
            ta(k, 0).start()
            ta(k, 1).start()
        txt[0:N, :] = em[N:N2, :]

    wo_copy = remote(wfull, wother, wo_s, wo_r, sib)
    wo_copy.start()

    scale = lscale[...]
    neg_scale, neg_bias = -LOG2E * lscale[...], -LOG2E * lbias[...]

    def take_image(k):
        @pl.when(first)
        def _():
            if k:
                arrived(rows(img, img_at(k), N2), ia_r.at[k], ia_s.at[0])
                fwd(k).start()

        @pl.when(core == 1)
        def _():
            arrived(rows(img, img_at(k), N2), ia_r.at[k], ia_s.at[0])

    def take_text(k):
        if k:
            arrived(rows(txt, txt_at(k), N), ta_r.at[k], ta_s.at[0])
        else:

            @pl.when(first)
            def _():
                arrived(rows(txt, 0, N), ta_r.at[0], ta_s.at[0])

    def tile(i, j, diagonal=False):
        block = img[pl.ds(pl.multiple_of(i * B, B), B), :]
        weight = block[:, E : E + 1].astype(F32) + block[:, E + 1 : E + 2].astype(F32)
        other = txt[pl.ds(pl.multiple_of(j * B, B), B), :]
        e = jnp.exp2(neg_scale * dot(block, other, ((1,), (1,))) + neg_bias)
        value = weight / (1.0 + e)
        if diagonal:
            r = lax.broadcasted_iota(jnp.int32, (B, B), 0)
            c = lax.broadcasted_iota(jnp.int32, (B, B), 1)
            value = jnp.where((r == c + core * N) & (c < N), -value * e, value)
        g[pl.ds(pl.multiple_of(i * B, B), B), pl.ds(pl.multiple_of(j * B, B), B)] = value.astype(BF)

    for t in range(NZ * N2 // B):
        for k in SHEET[4 * t : 4 * t + 4]:
            take_text(k)
        for k in LINE[2 * t : 2 * t + 2]:
            take_image(k)
        tile(t, t, t == 0)
        if t:

            @pl.loop(0, t)
            def _(i, t=t):
                tile(i, t)
                tile(t, i)

    def pi(k):
        return remote(
            rows(p_out, img_at(k), N2), rows(p_in, img_at(k), N2), pi_s.at[k], pi_r.at[k], sib
        )

    def ri(k):
        return remote(
            rows(p_out, img_at(k), N2), rows(rs_i, (NZ - k) % NZ * N2, N2),
            ri_s.at[k], ri_r.at[(NZ - k) % NZ], line(k),
        )

    def rt(k):
        return remote(
            rows(t_out, txt_at(k), N), rows(rs_t, (core * PLANE + back_slot(k)) * N, N),
            rt_s.at[k], rt_r.at[core * PLANE + back_slot(k)], plane(k, 1),
        )

    def combine(k):
        at = img_at(k)
        arrived(rows(p_in, at, N2), pi_r.at[k], pi_s.at[k])
        total = p_f[at : at + N2, :] + p_in[at : at + N2, :].astype(F32)
        if k:
            p_out[at : at + N2, :] = total.astype(BF)
            ri(k).start()
        else:
            p_f[0:N2, :] = total

    back_order = LINE[::-1]
    for n in range(NZ + 1):
        if n < NZ:
            k = back_order[n]
            at = img_at(k)
            p_f[at : at + N2, :] = dot(g[at : at + N2, :], txt[:, 0:E], ((1,), (0,)))

            @pl.when(core == 1)
            def _(k=k, at=at):
                p_out[at : at + N2, :] = p_f[at : at + N2, :].astype(BF)
                pi(k).start()

            b = NZ - 1 - n
            block = dot(g[:, b * N2 : (b + 1) * N2], img[:, 0:E], ((0,), (0,)))
            t_out[b * N2 : (b + 1) * N2, :] = block.astype(BF)
            for k in SHEET[2 * b : 2 * b + 2]:
                if k:
                    rt(k).start()
        if n:

            @pl.when(first)
            def _(n=n):
                combine(back_order[n - 1])

    @pl.when(first)
    def _():
        rt(0).start()
        for k in line_order:
            arrived(rows(rs_i, k * N2, N2), ri_r.at[k], ri_s.at[0])
            p_f[0:N2, :] += rs_i[k * N2 : (k + 1) * N2, :].astype(F32)

    @pl.when(core == 1)
    def _(block=block):
        arrived(rows(rs_t, 0, N), rt_r.at[0], rt_s.at[0])
        p_f[0:N, :] = rs_t[0:N, :].astype(F32)
        p_f[N:N2, :] = block[0:N, :]
        for k in plane_order:
            for c in range(2):
                at = c * PLANE + k
                arrived(rows(rs_t, at * N, N), rt_r.at[at], rt_s.at[0])
                p_f[c * N : (c + 1) * N, :] += rs_t[at * N : (at + 1) * N, :].astype(F32)

    grad = p_f[0:N2, :] * scale
    u = unit[...]
    back = ((grad - u * jnp.sum(u * grad, axis=1, keepdims=True)) / length[:, 0:1]).astype(BF)
    bk[...] = back
    bk_copy = remote(rows(bk, theirs, N), bo, bk_s, bk_r, sib)
    bk_copy.start()

    dwf[...] = dot(a[...], back, ((0,), (0,)))

    def z_row(k):
        at = lax.rem(z + k, NZ)
        return lax.div(at, NZ // 2), lax.rem(at, NZ // 2) * PIECE

    def p_row(k):
        px, py = lax.rem(x + k // NY, NX), lax.rem(y + k % NY, NY)
        return lax.rem(px, 2), Z_ROWS + (lax.div(px, 2) * NY + py) * PIECE

    def part(where):
        which, row = where
        return dwf[pl.ds(pl.multiple_of(which * H + row, PIECE), PIECE), :]

    def block(ref, k):
        return rows(ref, k * PIECE, PIECE)

    def r1_copy(k):
        return remote(
            block(dws, k), block(r1, back_slot(k)), r1_s.at[k], r1_r.at[back_slot(k)], plane(k)
        )

    def rz_copy(k):
        back_k = (NZ - k) % NZ
        return remote(block(dwz, k), block(rz, back_k), rz_s.at[k], rz_r.at[back_k], line(k))

    def fill(ref, k, where):
        ref[k * PIECE : (k + 1) * PIECE, :] = part(where).astype(BF)

    for n, k in enumerate(plane_order[::-1]):
        if n % 2 == 0 and n // 2 < NZ - 1:
            kz = line_order[::-1][n // 2]
            fill(dwz, kz, z_row(kz))
            rz_copy(kz).start()
        fill(dws, k, p_row(k))
        r1_copy(k).start()

    arrived(bo, bk_r, bk_s)
    arrived(wother, wo_r, wo_s)
    own = bk[pl.ds(mine, N), :]
    moved = dot(onehot, own, ((1,), (0,))).astype(BF)
    gsv[core] = dot(moved, wfull[...], ((1,), (1,)))
    moved = dot(onehot, bo[...], ((1,), (0,))).astype(BF)
    gsv[1 - core] = dot(moved, wother[...], ((1,), (1,)))
    gs_copies = [
        pltpu.make_async_copy(gsv.at[0], gs_i, gs_s.at[0]),
        pltpu.make_async_copy(gsv.at[1], gs_t, gs_s.at[1]),
    ]
    for copy in gs_copies:
        copy.start()

    z_half, z_at = z_row(0)
    holder = half == z_half

    def to_tiles(ref, value):
        for t in range(TILES):
            r, c = 16 * (t // 5), 128 * (t % 5)
            if t == TILES - 1:
                piece = jnp.zeros((16, 128), F32)
            elif c + 128 > E:
                piece = jnp.concatenate([value[r : r + 16, c:E], jnp.zeros((16, c + 128 - E), F32)], axis=1)
            else:
                piece = value[r : r + 16, c : c + 128]
            ref[16 * t : 16 * t + 16, :] = piece.astype(BF)

    def from_tiles(ref):
        bands = []
        for r in range(3):
            tiles = [ref[16 * (5 * r + c) : 16 * (5 * r + c) + 16, :] for c in range(5)]
            bands.append(jnp.concatenate(tiles, axis=1)[:, 0:E])
        return jnp.concatenate(bands, axis=0)

    total = part((z_half, z_at))
    for k in line_order:
        arrived(block(rz, k), rz_r.at[k], rz_s.at[k])
        total += rz[k * PIECE : (k + 1) * PIECE, :].astype(F32)
    to_tiles(zsum, total)

    def p_tile(k):
        return pl.multiple_of((lax.rem(x + k // NY, NX) * NY + lax.rem(y + k % NY, NY)) * 16, 16)

    def r3_copy(k):
        return remote(
            rows(zsum, p_tile(k), 16), rows(r3, back_slot(k) * 16, 16),
            r3_s.at[k], r3_r.at[back_slot(k)], plane(k),
        )

    for k in plane_order[::-1]:
        r3_copy(k).start()

    total = part(p_row(0))
    for k in plane_order[::-1]:
        arrived(block(r1, k), r1_r.at[k], r1_s.at[k])
        total += r1[k * PIECE : (k + 1) * PIECE, :].astype(F32)
    to_tiles(psum, total)

    def l_tile(k):
        return pl.multiple_of(lax.rem(z + k, NZ) * 32, 32)

    def r2_copy(k):
        back_k = (NZ - k) % NZ
        return remote(
            rows(psum, l_tile(k), 32), rows(r2, back_k * 32, 32), r2_s.at[k], r2_r.at[back_k], line(k)
        )

    for k in line_order[::-1]:
        r2_copy(k).start()

    def wants(k):
        return lax.rem(x + k // NY, 2) == z_half

    def e3_copy(k):
        return remote(zres, rows(zft, p_tile(0), 16), e3_s.at[k], e3_r.at[back_slot(k)], plane(k))

    total = zsum[pl.ds(p_tile(0), 16), :].astype(F32)
    for k in plane_order:
        arrived(rows(r3, k * 16, 16), r3_r.at[k], r3_s.at[k])
        total += r3[k * 16 : (k + 1) * 16, :].astype(F32)
    zres[...] = total.astype(BF)
    for k in plane_order[::-1]:

        @pl.when(wants(k))
        def _(k=k):
            e3_copy(k).start()

    zft[pl.ds(p_tile(0), 16), :] = total.astype(BF)

    def f_copy(k):
        return remote(res, rows(fint, l_tile(0), 32), f_s.at[k], f_r.at[(NZ - k) % NZ], line(k))

    total = psum[pl.ds(l_tile(0), 32), :].astype(F32)
    for k in line_order:
        arrived(rows(r2, k * 32, 32), r2_r.at[k], r2_s.at[k])
        total += r2[k * 32 : (k + 1) * 32, :].astype(F32)
    res[...] = total.astype(BF)
    for k in line_order[::-1]:
        f_copy(k).start()
    fint[pl.ds(l_tile(0), 32), :] = total.astype(BF)

    def shelf(modality, row):
        return gwv.at[modality, pl.ds(pl.multiple_of(row, PIECE), PIECE), :]

    def zg_copy(k):
        return remote(
            zfin, shelf(core, z_row(0)[1]), zg_s.at[k], zg_r.at[(NZ - k) % NZ], line(k)
        )

    def zd_copy(k, modality=core):
        to = shelf(modality, z_row(k)[1])
        return remote(zfin if k == 0 else to, to, zd_s.at[k], zd_r.at[k], sib)

    def holds(k):
        return z_row(k)[0] == half

    own_z = pltpu.make_async_copy(zfin, shelf(core, z_row(0)[1]), own_s.at[0])

    @pl.when(holder)
    def _():
        for k in plane_order:
            arrived(rows(zft, p_tile(k), 16), e3_r.at[k], e3_s.at[k])
        zfin[...] = from_tiles(zft)
        for k in line_order:
            zg_copy(k).start()
        zd_copy(0).start()
        own_z.start()

    for k in line_order:
        arrived(rows(fint, l_tile(k), 32), f_r.at[k], f_s.at[k])
    fin[...] = from_tiles(fint)

    mates = [k for k in plane_order if (k // NY) % 2 == 0]

    def ag_copy(k):
        return remote(
            fin, shelf(core, p_row(0)[1]), ag_s.at[k], ag_r.at[back_slot(k)], plane(k)
        )

    def ad_copy(k, modality=core):
        to = shelf(modality, p_row(k)[1])
        return remote(fin if k == 0 else to, to, ad_s.at[k], ad_r.at[k], sib)

    for k in mates:
        ag_copy(k).start()
    ad_copy(0).start()
    own_p = pltpu.make_async_copy(fin, shelf(core, p_row(0)[1]), own_s.at[1])
    own_p.start()
    for k in line_order:

        @pl.when(holds(k))
        def _(k=k):
            arrived(shelf(core, z_row(k)[1]), zg_r.at[k], zg_s.at[k])
            zd_copy(k).start()

    for k in mates:
        arrived(shelf(core, p_row(k)[1]), ag_r.at[k], ag_s.at[k])
        ad_copy(k).start()
    @pl.when(holder)
    def _():
        own_z.wait()

    own_p.wait()
    gw_copies = [
        pltpu.make_async_copy(gwv.at[m], gw.at[m], gw_s.at[n]) for n, m in enumerate((core, 1 - core))
    ]
    gw_copies[0].start()
    for k in LINE:

        @pl.when(holds(k))
        def _(k=k):
            arrived(shelf(1 - core, z_row(k)[1]), zd_r.at[k], zd_s.at[k])

    for k in [0] + mates:
        arrived(shelf(1 - core, p_row(k)[1]), ad_r.at[k], ad_s.at[k])
    gw_copies[1].start()

    for copy in heads + [rows_copy, c_copy, wo_copy, bk_copy]:
        copy.wait_send()

    @pl.when(first)
    def _():
        for k in line_order:
            ia(k).wait_send()
            ri(k).wait_send()
        for k in LINE:
            fwd(k).wait_send()
        rt(0).wait_send()

    @pl.when(core == 1)
    def _():
        for k in LINE:
            pi(k).wait_send()
        ta(0, 0).wait_send()
        for k in plane_order:
            ta(k, 0).wait_send()
            ta(k, 1).wait_send()

    for k in plane_order:
        rt(k).wait_send()
        r1_copy(k).wait_send()
    for k in line_order:
        rz_copy(k).wait_send()
        r2_copy(k).wait_send()
        f_copy(k).wait_send()

    for k in plane_order:
        r3_copy(k).wait_send()

        @pl.when(wants(k))
        def _(k=k):
            e3_copy(k).wait_send()

    @pl.when(holder)
    def _():
        for k in line_order:
            zg_copy(k).wait_send()

    for k in LINE:

        @pl.when(holds(k))
        def _(k=k):
            zd_copy(k).wait_send()

    for k in mates:
        ag_copy(k).wait_send()
    for k in [0] + mates:
        ad_copy(k).wait_send()
    for copy in gs_copies + gw_copies:
        copy.wait()


def finish(gw, gs_i, gs_t, out_hi, out_ht, out_i, out_t, narrow, wide, held, in_s, out_s, gi_s, go_s):
    loads = [pltpu.make_async_copy(gw.at[m], narrow.at[m], in_s.at[m]) for m in range(2)]
    moves = []
    for m, (src, dst) in enumerate(((gs_i, out_i), (gs_t, out_t))):
        at = held.at[m]
        moves.append(
            (
                pltpu.make_async_copy(src, at, gi_s.at[m]),
                pltpu.make_async_copy(at, dst, go_s.at[m]),
            )
        )
    moves[0][0].start()
    for copy in loads:
        copy.start()
    moves[1][0].start()
    stores = [pltpu.make_async_copy(wide.at[m], dst, out_s.at[m]) for m, dst in enumerate((out_hi, out_ht))]
    moves[0][0].wait()
    moves[0][1].start()
    for m in range(2):
        loads[m].wait()
        wide[m] = narrow[m].astype(F32)
        stores[m].start()
    moves[1][0].wait()
    moves[1][1].start()
    for copy in stores:
        copy.wait()
    for _, copy in moves:
        copy.wait()


def body(sup_i, sup_t, selected, buckets, weights, head_i, head_t, lscale, lbias, oscale):
    vmem = pl.BlockSpec(memory_space=pltpu.VMEM)
    hbm = pl.BlockSpec(memory_space=pl.ANY)

    def space(shape, dtype=BF):
        return pltpu.VMEM(shape, dtype)

    dma = pltpu.SemaphoreType.DMA
    buffers = [
        space((S, D)), space((S, D)), space((N2, D)), space((N, D)), space((16, 128), F32),
        space((D, E)), space((D, E)),
        space((N2, E), F32), space((N2, 128), F32),
        space((N2, EP)), space((NZ * N2, EP)), space((PLANE * N, EP)),
        space((NZ * N2, PLANE * N)),
        space((NZ * N2, E), F32), space((NZ * N2, E)), space((NZ * N2, E)), space((PLANE * N, E)),
        space((NZ * N2, E)), space((2 * PLANE * N, E)),
        space((N2, E)), space((N, E)), space((2, S, D), F32), space((D, E), F32),
        space((PLANE * PIECE, E)), space((NZ * PIECE, E)), space((PLANE * PIECE, E)),
        space((NZ * PIECE, E)), space((TILES * 16, 128)), space((TILES * 16, 128)), space((16, 128)),
        space((TILES * 16, 128)), space((PIECE, E)), space((TILES * 16, 128)), space((TILES * 16, 128)),
        space((32, 128)), space((TILES * 16, 128)), space((PIECE, E)), space((2, H, E)),
    ]
    counts = [
        3, 2, 2, 0, 0, 0, 0, 0, 0,
        NZ, NZ, NZ, 2 * PLANE, PLANE, NZ, NZ, NZ, NZ, PLANE, 2 * PLANE,
        0, 0, 2, PLANE, PLANE, NZ, NZ, PLANE, PLANE, PLANE, PLANE, NZ, NZ, NZ, NZ,
        NZ, NZ, NZ, NZ, 2, 2, PLANE, PLANE, PLANE, PLANE,
    ]
    sems = [dma((n,)) if n else dma for n in counts]
    gs_i, gs_t, gw = pl.pallas_call(
        kernel,
        out_shape=(
            jax.ShapeDtypeStruct((S, D), F32),
            jax.ShapeDtypeStruct((S, D), F32),
            jax.ShapeDtypeStruct((2, H, E), BF),
        ),
        in_specs=[hbm] * 2 + [vmem] * 3 + [hbm] * 2 + [vmem] * 3,
        out_specs=(hbm, hbm, hbm),
        scratch_shapes=buffers + sems,
        compiler_params=pltpu.CompilerParams(
            collective_id=0, has_side_effects=True, vmem_limit_bytes=56 * 1024 * 1024
        ),
    )(
        sup_i, sup_t, selected.reshape(1, N), buckets.reshape(1, N), weights.reshape(1, NB),
        head_i, head_t, lscale.reshape(1, 1), lbias.reshape(1, 1), oscale.reshape(1, 1),
    )
    return pl.pallas_call(
        finish,
        out_shape=(jax.ShapeDtypeStruct((H, E), F32),) * 2 + (jax.ShapeDtypeStruct((S, D), F32),) * 2,
        in_specs=[hbm] * 3,
        out_specs=(hbm,) * 4,
        scratch_shapes=[
            space((2, H, E)), space((2, H, E), F32), space((2, S, D), F32),
            dma((2,)), dma((2,)), dma((2,)), dma((2,)),
        ],
        compiler_params=pltpu.CompilerParams(vmem_limit_bytes=60 * 1024 * 1024),
    )(gw, gs_i, gs_t)


def solution(mesh):
    both = P(("dp", "fsdp"))
    wide = P(("dp", "fsdp"), None)
    head = P("fsdp", None)
    in_specs = (wide, wide, both, both, P(), head, head, P(), P(), P())
    out_specs = (head, head, wide, wide)
    return jax.shard_map(body, mesh=mesh, in_specs=in_specs, out_specs=out_specs, check_vma=False)
```

```python
import functools

import jax
import jax.numpy as jnp
from jax import lax
from jax.experimental import pallas as pl
from jax.experimental.pallas import tpu as pltpu
from jax.sharding import PartitionSpec as P

MESH = pl.DeviceIdType.MESH
BF = jnp.bfloat16
F32 = jnp.float32
NX, NY, NZ = 4, 4, 8
PLANE = NX * NY
PAIRS = 16384
N = 64
N2 = 2 * N
S = 320
D = 1152
H = D // 2
E = 576
EP = 640
PIECE = 48
TILES = 16
Z_ROWS = PIECE * NZ // 2
B = 256
NB = 16
LOG2E = 1.4426950408889634


def hops(k):
    return min(k // NY, NX - k // NY) + min(k % NY, NY - k % NY)


def back_slot(k):
    return (-(k // NY)) % NX * NY + (-(k % NY)) % NY


LINE = (0, 2, 6, 1, 7, 3, 5, 4)
RING = (0, 1, 3, 2)
SHEET = tuple(sorted(range(PLANE), key=lambda k: (hops(k), k)))


def place():
    dp, x_lo = lax.axis_index("dp"), lax.axis_index("fsdp")
    core = lax.rem(dp, 2)
    y = lax.rem(lax.div(dp, 2), NY)
    x = lax.rem(lax.div(dp, 2 * NY), 2) * 2 + x_lo
    z = lax.div(dp, 4 * NY)
    return x, y, z, core


def device(x, y, z, core):
    return (((z * 2 + lax.div(x, 2)) * NY + y) * 2 + core, lax.rem(x, 2))


def dot(a, b, contract):
    return lax.dot_general(a, b, (contract, ((), ())), preferred_element_type=F32)


def kernel(
    sup_i, sup_t, sel, bkt, wts, head_i, head_t, lscale, lbias, oscale,
    gs_i, gs_t, gw,
    va, vt, a, stage, cbuf, wfull, wother, unit, length,
    em, img, txt, g, p_f, p_out, p_in, t_out, t_own, rv_in, u_out, rs_a, rs_b, rs_i, rs_t,
    bk, bo, gsv, dwf, dws, dwz, r1, rz, r3, zsum, zres, zft, zfin, psum, r2, res, fint, fin, gwv,
    in_s, w_s, w_r, rows_s, rows_r, c_s, c_r, wo_s, wo_r,
    ia_s, ia_r, ip_s, if_s, ta_s, ta_r, tp_s, pi_s, pi_r, ri_s, ri_r, ra_r, rb_s, rb_r,
    rv_s, rv_r, ru_s, ru_r,
    bk_s, bk_r, gs_s, r1_s, r1_r, rz_s, rz_r, r3_s, r3_r, e3_s, e3_r, r2_s, r2_r, f_s, f_r,
    zg_s, zg_r, zd_s, zd_r, own_s, gw_s, ag_s, ag_r, ad_s, ad_r,
):
    x, y, z, core = place()
    half = lax.rem(x, 2)
    sib = device(x, y, z, 1 - core)
    first = core == 0

    def line(k, c=core):
        return device(x, y, lax.rem(z + k, NZ), c)

    def plane(k, c=core):
        return device(lax.rem(x + k // NY, NX), lax.rem(y + k % NY, NY), z, c)

    def remote(src, dst, send, recv, to):
        return pltpu.make_async_remote_copy(
            src_ref=src, dst_ref=dst, send_sem=send, recv_sem=recv,
            device_id=to, device_id_type=MESH,
        )

    def arrived(dst, recv, send):
        remote(dst, dst, send, recv, sib).wait_recv()

    def rows(ref, start, count):
        return ref.at[pl.ds(start, count), :]

    barrier = pltpu.get_barrier_semaphore()

    def greet(to):
        pl.semaphore_signal(barrier, inc=1, device_id=to, device_id_type=MESH)

    h_off = pl.multiple_of(half * H, H)
    sup_copies = [
        pltpu.make_async_copy(sup_i, va, in_s.at[0]),
        pltpu.make_async_copy(sup_t, vt, in_s.at[1]),
    ]
    head_copy = pltpu.make_async_copy(head_i, rows(wfull, h_off, H), in_s.at[2])
    for copy in sup_copies:
        copy.start()

    @pl.when(first)
    def _():
        head_copy.start()

    @pl.when(core == 1)
    def _():
        pltpu.make_async_copy(head_t, rows(wfull, h_off, H), in_s.at[2]).start()

    greet(sib)
    for k in range(1, NZ):
        greet(line(k))
    for k in range(1, PLANE):
        greet(plane(k, 0))
        greet(plane(k, 1))

    for copy in sup_copies:
        copy.wait()
    onehot = (lax.broadcasted_iota(jnp.int32, (S, N), 0) == sel[...]).astype(BF)
    rows_i = dot(onehot, va[...], ((0,), (0,))).astype(BF)
    rows_t = dot(onehot, vt[...], ((0,), (0,))).astype(BF)
    mine = pl.multiple_of(core * N, N)
    a[pl.ds(mine, N), :] = jnp.where(first, rows_i, rows_t)
    stage[...] = jnp.where(first, rows_t, rows_i)
    weight = jnp.zeros((1, N), F32)
    for n in range(NB):
        weight = jnp.where(bkt[...] == n, wts[:, n : n + 1], weight)
    weight = oscale[...] * weight / PAIRS
    cbuf[pl.ds(pl.multiple_of(core * 8, 8), 8), :] = jnp.concatenate(
        [jnp.broadcast_to(weight, (8, N)), jnp.zeros((8, N), F32)], axis=1
    )

    head_copy.wait()
    pl.semaphore_wait(barrier, 1 + (NZ - 1) + 2 * (PLANE - 1))

    heads = []
    for k, step in ((0, 1), (1, NX - 1)):
        src = rows(wfull, pl.multiple_of(h_off + k * (H // 2), H // 2), H // 2)
        heads.append(
            remote(src, src, w_s.at[k], w_r.at[k], device(lax.rem(x + step, NX), y, z, core))
        )
    rows_copy = remote(stage, rows(a, mine, N), rows_s, rows_r, sib)
    c_own = rows(cbuf, pl.multiple_of(core * 8, 8), 8)
    c_copy = remote(c_own, c_own, c_s, c_r, sib)
    for copy in heads:
        copy.start()
    rows_copy.start()
    c_copy.start()
    theirs = pl.multiple_of((1 - core) * N, N)
    o_off = pl.multiple_of((1 - half) * H, H)
    arrived(rows(a, theirs, N), rows_r, rows_s)
    arrived(rows(cbuf, pl.multiple_of((1 - core) * 8, 8), 8), c_r, c_s)
    for k in range(2):
        arrived(
            rows(wfull, pl.multiple_of(o_off + k * (H // 2), H // 2), H // 2), w_r.at[k], w_s.at[k]
        )

    raw = dot(a[...], wfull[...], ((1,), (0,)))
    size = jnp.sqrt(jnp.sum(raw * raw, axis=1, keepdims=True) + 1e-06)
    u = raw / size
    unit[...] = u
    length[...] = jnp.broadcast_to(size, (N2, 128))
    eye = lax.broadcasted_iota(jnp.int32, (N, N), 0) == lax.broadcasted_iota(jnp.int32, (N, N), 1)
    column = jnp.concatenate(
        [
            jnp.sum(jnp.where(eye, cbuf[8 * c : 8 * c + 1, 0:N], 0.0), axis=1, keepdims=True)
            for c in range(2)
        ],
        axis=0,
    )
    column = jnp.where(first, column, jnp.zeros_like(column))
    high = column.astype(BF)
    low = (column - high.astype(F32)).astype(BF)
    em[...] = jnp.concatenate([u.astype(BF), high, low, jnp.zeros((N2, EP - E - 2), BF)], axis=1)

    line_order, plane_order = LINE[1:], SHEET[1:]

    def ahead(at, k, size):
        return lax.rem(at + k, size)

    def u_peer(k, c=core):
        return device(
            jnp.where(first, ahead(x, k, NX), x), jnp.where(first, y, ahead(y, k, NY)), z, c
        )

    def v_peer(k):
        return device(
            jnp.where(first, x, ahead(x, k, NX)), jnp.where(first, ahead(y, k, NY), y), z, core
        )

    def img_at(k):
        return LINE.index(k % NZ) * N2

    def txt_at(u, v):
        return (RING.index(v % 4) * 4 + RING.index(u % 4)) * N

    def ia(k):
        return remote(em, rows(img, img_at(-k), N2), ia_s.at[k], ia_r.at[(NZ - k) % NZ], line(k))

    def ip(k):
        step = 1 if k == 6 else NZ - 1
        src = rows(img, img_at(k), N2)
        off, n = (0, 4) if k == 2 else (N, NZ)
        return (
            remote(src, rows(img, img_at(k - step), N2), ip_s.at[k], ia_r.at[(k - step) % NZ], line(step)),
            remote(
                rows(img, img_at(k) + off, N), rows(img, img_at(4) + off, N),
                ip_s.at[(k + 1) % NZ], ia_r.at[n], line((NZ - k) % NZ),
            ),
        )

    def fwd(k):
        block = rows(img, img_at(k), N2)
        return remote(em if k == 0 else block, block, if_s.at[k], ia_r.at[k], sib)

    def ta0(k):
        to = device(ahead(x, k, NX), y, z, 0)
        return remote(rows(em, 0, N), rows(txt, txt_at(-k, 0), N), ta_s.at[k], ta_r.at[(-k) % 4], to)

    def ta1(k):
        to = device(x, ahead(y, k, NY), z, 1)
        return remote(
            rows(em, N, N), rows(txt, txt_at(-k, 0), N), ta_s.at[4 + k], ta_r.at[(-k) % 4], to
        )

    def tp(u, v):
        return remote(
            rows(txt, txt_at(u, 0), N), rows(txt, txt_at(u, -v), N),
            tp_s.at[4 * v + u], ta_r.at[(-v) % 4 * 4 + u], v_peer(v),
        )

    @pl.when(first)
    def _():
        for k in line_order[:4]:
            ia(k).start()
        fwd(0).start()
        img[0:N2, :] = em[...]

    @pl.when(core == 1)
    def _():
        txt[0:N, :] = em[N:N2, :]
        for k in RING[::-1]:
            ta0(k).start()
            if k:
                ta1(k).start()

    wo_copy = remote(wfull, wother, wo_s, wo_r, sib)
    wo_copy.start()

    scale = lscale[...]
    neg_scale, neg_bias = -LOG2E * lscale[...], -LOG2E * lbias[...]

    def take_image(k):
        @pl.when(first)
        def _():
            if k == 4:
                for n in range(2):
                    arrived(rows(img, img_at(4) + n * N, N), ia_r.at[4 + 4 * n], ia_s.at[0])
            elif k:
                arrived(rows(img, img_at(k), N2), ia_r.at[k], ia_s.at[0])
            if k in (2, 6):
                for copy in ip(k):
                    copy.start()
            if k:
                fwd(k).start()

        @pl.when(core == 1)
        def _():
            arrived(rows(img, img_at(k), N2), ia_r.at[k], ia_s.at[0])

    def take_text(u, v):
        if u or v:
            arrived(rows(txt, txt_at(u, v), N), ta_r.at[4 * v + u], ta_s.at[0])
        else:

            @pl.when(first)
            def _():
                arrived(rows(txt, 0, N), ta_r.at[0], ta_s.at[0])

        if v == 0:
            for k in RING[:0:-1]:
                tp(u, k).start()

    def tile(i, j, diagonal=False):
        block = img[pl.ds(pl.multiple_of(i * B, B), B), :]
        weight = block[:, E : E + 1].astype(F32) + block[:, E + 1 : E + 2].astype(F32)
        other = txt[pl.ds(pl.multiple_of(j * B, B), B), :]
        e = jnp.exp2(neg_scale * dot(block, other, ((1,), (1,))) + neg_bias)
        value = weight / (1.0 + e)
        if diagonal:
            r = lax.broadcasted_iota(jnp.int32, (B, B), 0)
            c = lax.broadcasted_iota(jnp.int32, (B, B), 1)
            value = jnp.where((r == c + core * N) & (c < N), -value * e, value)
        g[pl.ds(pl.multiple_of(i * B, B), B), pl.ds(pl.multiple_of(j * B, B), B)] = value.astype(BF)

    for t in range(NZ * N2 // B):
        for u in RING:
            take_text(u, RING[t])
        for k in LINE[2 * t : 2 * t + 2]:
            take_image(k)
        tile(t, t, t == 0)
        if t:

            @pl.loop(0, t)
            def _(i, t=t):
                tile(i, t)
                tile(t, i)

    def pi(k):
        return remote(
            rows(p_out, img_at(k), N2), rows(p_in, img_at(k), N2), pi_s.at[k], pi_r.at[k], sib
        )

    def ri(k):
        src = rows(p_out, img_at(k), N2)
        if k in (3, 5):
            n = 0 if k == 3 else 1
            return [remote(src, rows(rs_a, n * N2, N2), ri_s.at[k], ra_r.at[n], line(1 if k == 3 else 7))]
        if k == 4:
            return [
                remote(
                    rows(p_out, img_at(4) + n * N, N), rows(rs_b, n * N, N),
                    rb_s.at[n], rb_r.at[n], line((2, 6)[n]),
                )
                for n in range(2)
            ]
        back_k = (NZ - k) % NZ
        return [remote(src, rows(rs_i, back_k * N2, N2), ri_s.at[k], ri_r.at[back_k], line(k))]

    def combine(k):
        at = img_at(k)
        arrived(rows(p_in, at, N2), pi_r.at[k], pi_s.at[k])
        total = p_f[at : at + N2, :] + p_in[at : at + N2, :].astype(F32)
        if k in (2, 6):
            n = (2, 6).index(k)
            arrived(rows(rs_a, n * N2, N2), ra_r.at[n], ri_s.at[0])
            total += rs_a[n * N2 : (n + 1) * N2, :].astype(F32)
            arrived(rows(rs_b, n * N, N), rb_r.at[n], rb_s.at[n])
            more = rs_b[n * N : (n + 1) * N, :].astype(F32)
            half_of = total[n * N : (n + 1) * N, :] + more
            keep = total[(1 - n) * N : (2 - n) * N, :]
            total = jnp.concatenate([half_of, keep] if n == 0 else [keep, half_of], axis=0)
        if k:
            p_out[at : at + N2, :] = total.astype(BF)
            for copy in ri(k):
                copy.start()
        else:
            p_f[0:N2, :] = total

    def rv(v):
        n = RING.index(v) * 4 * N
        return remote(
            rows(t_out, n, 4 * N), rows(rv_in, (-v) % 4 * 4 * N, 4 * N),
            rv_s.at[v], rv_r.at[(-v) % 4], v_peer(v),
        )

    def ru(u):
        at = core * 4 + (-u) % 4
        return remote(
            rows(u_out, u * N, N), rows(rs_t, at * N, N), ru_s.at[u], ru_r.at[at], u_peer(u, 1)
        )

    back_order = (4, 3, 5, 1, 7, 2, 6, 0)
    text_order = (2, 1, 3, 0)
    for n in range(NZ + 1):
        if n < NZ:
            k = back_order[n]
            at = img_at(k)
            p_f[at : at + N2, :] = dot(g[at : at + N2, :], txt[:, 0:E], ((1,), (0,)))

            @pl.when(core == 1)
            def _(k=k, at=at):
                p_out[at : at + N2, :] = p_f[at : at + N2, :].astype(BF)
                pi(k).start()

            v = text_order[n // 2]
            b = 2 * RING.index(v) + n % 2
            block = dot(g[:, b * N2 : (b + 1) * N2], img[:, 0:E], ((0,), (0,)))
            if v:
                t_out[b * N2 : (b + 1) * N2, :] = block.astype(BF)
            else:
                t_own[b * N2 : (b + 1) * N2, :] = block
            if v and n % 2:
                rv(v).start()
        if n:

            @pl.when(first)
            def _(n=n):
                combine(back_order[n - 1])

    for v in text_order[:3]:
        arrived(rows(rv_in, v * 4 * N, 4 * N), rv_r.at[v], rv_s.at[v])
    for u in RING[::-1]:
        at = RING.index(u) * N
        total = t_own[at : at + N, :]
        for v in (1, 2, 3):
            row = v * 4 * N + at
            total += rv_in[row : row + N, :].astype(F32)
        if u:
            u_out[u * N : (u + 1) * N, :] = total.astype(BF)
            ru(u).start()
        else:

            @pl.when(first)
            def _(total=total):
                u_out[0:N, :] = total.astype(BF)
                remote(rows(u_out, 0, N), rows(rs_t, 0, N), ru_s.at[0], ru_r.at[0], sib).start()

            @pl.when(core == 1)
            def _(total=total):
                p_f[N:N2, :] = total

    @pl.when(first)
    def _():
        for k in (1, 7, 2, 6):
            arrived(rows(rs_i, k * N2, N2), ri_r.at[k], ri_s.at[0])
            p_f[0:N2, :] += rs_i[k * N2 : (k + 1) * N2, :].astype(F32)

    @pl.when(core == 1)
    def _():
        arrived(rows(rs_t, 0, N), ru_r.at[0], ru_s.at[0])
        p_f[0:N, :] = rs_t[0:N, :].astype(F32)
        for k in RING[1:]:
            for c in range(2):
                at = c * 4 + k
                arrived(rows(rs_t, at * N, N), ru_r.at[at], ru_s.at[0])
                p_f[c * N : (c + 1) * N, :] += rs_t[at * N : (at + 1) * N, :].astype(F32)

    grad = p_f[0:N2, :] * scale
    u = unit[...]
    back = ((grad - u * jnp.sum(u * grad, axis=1, keepdims=True)) / length[:, 0:1]).astype(BF)
    bk[...] = back
    bk_copy = remote(rows(bk, theirs, N), bo, bk_s, bk_r, sib)
    bk_copy.start()

    dwf[...] = dot(a[...], back, ((0,), (0,)))

    def z_row(k):
        at = lax.rem(z + k, NZ)
        return lax.div(at, NZ // 2), lax.rem(at, NZ // 2) * PIECE

    def p_row(k):
        px, py = lax.rem(x + k // NY, NX), lax.rem(y + k % NY, NY)
        return lax.rem(px, 2), Z_ROWS + (lax.div(px, 2) * NY + py) * PIECE

    def part(where):
        which, row = where
        return dwf[pl.ds(pl.multiple_of(which * H + row, PIECE), PIECE), :]

    def block(ref, k):
        return rows(ref, k * PIECE, PIECE)

    def r1_copy(k):
        return remote(
            block(dws, k), block(r1, back_slot(k)), r1_s.at[k], r1_r.at[back_slot(k)], plane(k)
        )

    def rz_copy(k):
        back_k = (NZ - k) % NZ
        return remote(block(dwz, k), block(rz, back_k), rz_s.at[k], rz_r.at[back_k], line(k))

    def fill(ref, k, where):
        ref[k * PIECE : (k + 1) * PIECE, :] = part(where).astype(BF)

    for n, k in enumerate(plane_order[::-1]):
        if n % 2 == 0 and n // 2 < NZ - 1:
            kz = line_order[::-1][n // 2]
            fill(dwz, kz, z_row(kz))
            rz_copy(kz).start()
        fill(dws, k, p_row(k))
        r1_copy(k).start()

    arrived(bo, bk_r, bk_s)
    arrived(wother, wo_r, wo_s)
    own = bk[pl.ds(mine, N), :]
    moved = dot(onehot, own, ((1,), (0,))).astype(BF)
    gsv[core] = dot(moved, wfull[...], ((1,), (1,)))
    moved = dot(onehot, bo[...], ((1,), (0,))).astype(BF)
    gsv[1 - core] = dot(moved, wother[...], ((1,), (1,)))
    gs_copies = [
        pltpu.make_async_copy(gsv.at[0], gs_i, gs_s.at[0]),
        pltpu.make_async_copy(gsv.at[1], gs_t, gs_s.at[1]),
    ]
    for copy in gs_copies:
        copy.start()

    z_half, z_at = z_row(0)
    holder = half == z_half

    def to_tiles(ref, value):
        for t in range(TILES):
            r, c = 16 * (t // 5), 128 * (t % 5)
            if t == TILES - 1:
                piece = jnp.zeros((16, 128), F32)
            elif c + 128 > E:
                piece = jnp.concatenate([value[r : r + 16, c:E], jnp.zeros((16, c + 128 - E), F32)], axis=1)
            else:
                piece = value[r : r + 16, c : c + 128]
            ref[16 * t : 16 * t + 16, :] = piece.astype(BF)

    def from_tiles(ref):
        bands = []
        for r in range(3):
            tiles = [ref[16 * (5 * r + c) : 16 * (5 * r + c) + 16, :] for c in range(5)]
            bands.append(jnp.concatenate(tiles, axis=1)[:, 0:E])
        return jnp.concatenate(bands, axis=0)

    total = part((z_half, z_at))
    for k in line_order:
        arrived(block(rz, k), rz_r.at[k], rz_s.at[k])
        total += rz[k * PIECE : (k + 1) * PIECE, :].astype(F32)
    to_tiles(zsum, total)

    def p_tile(k):
        return pl.multiple_of((lax.rem(x + k // NY, NX) * NY + lax.rem(y + k % NY, NY)) * 16, 16)

    def r3_copy(k):
        return remote(
            rows(zsum, p_tile(k), 16), rows(r3, back_slot(k) * 16, 16),
            r3_s.at[k], r3_r.at[back_slot(k)], plane(k),
        )

    for k in plane_order[::-1]:
        r3_copy(k).start()

    total = part(p_row(0))
    for k in plane_order[::-1]:
        arrived(block(r1, k), r1_r.at[k], r1_s.at[k])
        total += r1[k * PIECE : (k + 1) * PIECE, :].astype(F32)
    to_tiles(psum, total)

    def l_tile(k):
        return pl.multiple_of(lax.rem(z + k, NZ) * 32, 32)

    def r2_copy(k):
        back_k = (NZ - k) % NZ
        return remote(
            rows(psum, l_tile(k), 32), rows(r2, back_k * 32, 32), r2_s.at[k], r2_r.at[back_k], line(k)
        )

    for k in line_order[::-1]:
        r2_copy(k).start()

    def wants(k):
        return lax.rem(x + k // NY, 2) == z_half

    def e3_copy(k):
        return remote(zres, rows(zft, p_tile(0), 16), e3_s.at[k], e3_r.at[back_slot(k)], plane(k))

    total = zsum[pl.ds(p_tile(0), 16), :].astype(F32)
    for k in plane_order:
        arrived(rows(r3, k * 16, 16), r3_r.at[k], r3_s.at[k])
        total += r3[k * 16 : (k + 1) * 16, :].astype(F32)
    zres[...] = total.astype(BF)
    for k in plane_order[::-1]:

        @pl.when(wants(k))
        def _(k=k):
            e3_copy(k).start()

    zft[pl.ds(p_tile(0), 16), :] = total.astype(BF)

    def f_copy(k):
        return remote(res, rows(fint, l_tile(0), 32), f_s.at[k], f_r.at[(NZ - k) % NZ], line(k))

    total = psum[pl.ds(l_tile(0), 32), :].astype(F32)
    for k in line_order:
        arrived(rows(r2, k * 32, 32), r2_r.at[k], r2_s.at[k])
        total += r2[k * 32 : (k + 1) * 32, :].astype(F32)
    res[...] = total.astype(BF)
    for k in line_order[::-1]:
        f_copy(k).start()
    fint[pl.ds(l_tile(0), 32), :] = total.astype(BF)

    def shelf(modality, row):
        return gwv.at[modality, pl.ds(pl.multiple_of(row, PIECE), PIECE), :]

    def zg_copy(k):
        return remote(
            zfin, shelf(core, z_row(0)[1]), zg_s.at[k], zg_r.at[(NZ - k) % NZ], line(k)
        )

    def zd_copy(k, modality=core):
        to = shelf(modality, z_row(k)[1])
        return remote(zfin if k == 0 else to, to, zd_s.at[k], zd_r.at[k], sib)

    def holds(k):
        return z_row(k)[0] == half

    own_z = pltpu.make_async_copy(zfin, shelf(core, z_row(0)[1]), own_s.at[0])

    @pl.when(holder)
    def _():
        for k in plane_order:
            arrived(rows(zft, p_tile(k), 16), e3_r.at[k], e3_s.at[k])
        zfin[...] = from_tiles(zft)
        for k in line_order:
            zg_copy(k).start()
        zd_copy(0).start()
        own_z.start()

    for k in line_order:
        arrived(rows(fint, l_tile(k), 32), f_r.at[k], f_s.at[k])
    fin[...] = from_tiles(fint)

    mates = [k for k in plane_order if (k // NY) % 2 == 0]

    def ag_copy(k):
        return remote(
            fin, shelf(core, p_row(0)[1]), ag_s.at[k], ag_r.at[back_slot(k)], plane(k)
        )

    def ad_copy(k, modality=core):
        to = shelf(modality, p_row(k)[1])
        return remote(fin if k == 0 else to, to, ad_s.at[k], ad_r.at[k], sib)

    for k in mates:
        ag_copy(k).start()
    ad_copy(0).start()
    own_p = pltpu.make_async_copy(fin, shelf(core, p_row(0)[1]), own_s.at[1])
    own_p.start()
    for k in line_order:

        @pl.when(holds(k))
        def _(k=k):
            arrived(shelf(core, z_row(k)[1]), zg_r.at[k], zg_s.at[k])
            zd_copy(k).start()

    for k in mates:
        arrived(shelf(core, p_row(k)[1]), ag_r.at[k], ag_s.at[k])
        ad_copy(k).start()
    @pl.when(holder)
    def _():
        own_z.wait()

    own_p.wait()
    gw_copies = [
        pltpu.make_async_copy(gwv.at[m], gw.at[m], gw_s.at[n]) for n, m in enumerate((core, 1 - core))
    ]
    gw_copies[0].start()
    for k in LINE:

        @pl.when(holds(k))
        def _(k=k):
            arrived(shelf(1 - core, z_row(k)[1]), zd_r.at[k], zd_s.at[k])

    for k in [0] + mates:
        arrived(shelf(1 - core, p_row(k)[1]), ad_r.at[k], ad_s.at[k])
    gw_copies[1].start()

    for copy in heads + [rows_copy, c_copy, wo_copy, bk_copy]:
        copy.wait_send()

    @pl.when(first)
    def _():
        for k in line_order[:4]:
            ia(k).wait_send()
        for k in (2, 6):
            for copy in ip(k):
                copy.wait_send()
        for k in line_order:
            for copy in ri(k):
                copy.wait_send()
        for k in LINE:
            fwd(k).wait_send()
        remote(rows(u_out, 0, N), rows(rs_t, 0, N), ru_s.at[0], ru_r.at[0], sib).wait_send()

    @pl.when(core == 1)
    def _():
        for k in LINE:
            pi(k).wait_send()
        for k in RING:
            ta0(k).wait_send()
            if k:
                ta1(k).wait_send()

    for k in RING[1:]:
        for u in RING:
            tp(u, k).wait_send()
        rv(k).wait_send()
        ru(k).wait_send()
    for k in plane_order:
        r1_copy(k).wait_send()
    for k in line_order:
        rz_copy(k).wait_send()
        r2_copy(k).wait_send()
        f_copy(k).wait_send()

    for k in plane_order:
        r3_copy(k).wait_send()

        @pl.when(wants(k))
        def _(k=k):
            e3_copy(k).wait_send()

    @pl.when(holder)
    def _():
        for k in line_order:
            zg_copy(k).wait_send()

    for k in LINE:

        @pl.when(holds(k))
        def _(k=k):
            zd_copy(k).wait_send()

    for k in mates:
        ag_copy(k).wait_send()
    for k in [0] + mates:
        ad_copy(k).wait_send()
    for copy in gs_copies + gw_copies:
        copy.wait()


def finish(gw, gs_i, gs_t, out_hi, out_ht, out_i, out_t, narrow, wide, held, in_s, out_s, gi_s, go_s):
    loads = [pltpu.make_async_copy(gw.at[m], narrow.at[m], in_s.at[m]) for m in range(2)]
    moves = []
    for m, (src, dst) in enumerate(((gs_i, out_i), (gs_t, out_t))):
        at = held.at[m]
        moves.append(
            (
                pltpu.make_async_copy(src, at, gi_s.at[m]),
                pltpu.make_async_copy(at, dst, go_s.at[m]),
            )
        )
    moves[0][0].start()
    for copy in loads:
        copy.start()
    moves[1][0].start()
    stores = [pltpu.make_async_copy(wide.at[m], dst, out_s.at[m]) for m, dst in enumerate((out_hi, out_ht))]
    moves[0][0].wait()
    moves[0][1].start()
    for m in range(2):
        loads[m].wait()
        wide[m] = narrow[m].astype(F32)
        stores[m].start()
    moves[1][0].wait()
    moves[1][1].start()
    for copy in stores:
        copy.wait()
    for _, copy in moves:
        copy.wait()


def body(sup_i, sup_t, selected, buckets, weights, head_i, head_t, lscale, lbias, oscale):
    vmem = pl.BlockSpec(memory_space=pltpu.VMEM)
    hbm = pl.BlockSpec(memory_space=pl.ANY)

    def space(shape, dtype=BF):
        return pltpu.VMEM(shape, dtype)

    dma = pltpu.SemaphoreType.DMA
    buffers = [
        space((S, D)), space((S, D)), space((N2, D)), space((N, D)), space((16, 128), F32),
        space((D, E)), space((D, E)),
        space((N2, E), F32), space((N2, 128), F32),
        space((N2, EP)), space((NZ * N2, EP)), space((PLANE * N, EP)),
        space((NZ * N2, PLANE * N)),
        space((NZ * N2, E), F32), space((NZ * N2, E)), space((NZ * N2, E)), space((PLANE * N, E)),
        space((4 * N, E), F32), space((PLANE * N, E)), space((4 * N, E)), space((2 * N2, E)), space((N2, E)),
        space((NZ * N2, E)), space((8 * N, E)),
        space((N2, E)), space((N, E)), space((2, S, D), F32), space((D, E), F32),
        space((PLANE * PIECE, E)), space((NZ * PIECE, E)), space((PLANE * PIECE, E)),
        space((NZ * PIECE, E)), space((TILES * 16, 128)), space((TILES * 16, 128)), space((16, 128)),
        space((TILES * 16, 128)), space((PIECE, E)), space((TILES * 16, 128)), space((TILES * 16, 128)),
        space((32, 128)), space((TILES * 16, 128)), space((PIECE, E)), space((2, H, E)),
    ]
    counts = [
        3, 2, 2, 0, 0, 0, 0, 0, 0,
        NZ, NZ + 1, NZ, NZ, 8, PLANE, PLANE, NZ, NZ, NZ, NZ, 2, 2, 2, 4, 4, 4, 8,
        0, 0, 2, PLANE, PLANE, NZ, NZ, PLANE, PLANE, PLANE, PLANE, NZ, NZ, NZ, NZ,
        NZ, NZ, NZ, NZ, 2, 2, PLANE, PLANE, PLANE, PLANE,
    ]
    sems = [dma((n,)) if n else dma for n in counts]
    gs_i, gs_t, gw = pl.pallas_call(
        kernel,
        out_shape=(
            jax.ShapeDtypeStruct((S, D), F32),
            jax.ShapeDtypeStruct((S, D), F32),
            jax.ShapeDtypeStruct((2, H, E), BF),
        ),
        in_specs=[hbm] * 2 + [vmem] * 3 + [hbm] * 2 + [vmem] * 3,
        out_specs=(hbm, hbm, hbm),
        scratch_shapes=buffers + sems,
        compiler_params=pltpu.CompilerParams(
            collective_id=0, has_side_effects=True, vmem_limit_bytes=56 * 1024 * 1024
        ),
    )(
        sup_i, sup_t, selected.reshape(1, N), buckets.reshape(1, N), weights.reshape(1, NB),
        head_i, head_t, lscale.reshape(1, 1), lbias.reshape(1, 1), oscale.reshape(1, 1),
    )
    return pl.pallas_call(
        finish,
        out_shape=(jax.ShapeDtypeStruct((H, E), F32),) * 2 + (jax.ShapeDtypeStruct((S, D), F32),) * 2,
        in_specs=[hbm] * 3,
        out_specs=(hbm,) * 4,
        scratch_shapes=[
            space((2, H, E)), space((2, H, E), F32), space((2, S, D), F32),
            dma((2,)), dma((2,)), dma((2,)), dma((2,)),
        ],
        compiler_params=pltpu.CompilerParams(vmem_limit_bytes=60 * 1024 * 1024),
    )(gw, gs_i, gs_t)


def solution(mesh):
    both = P(("dp", "fsdp"))
    wide = P(("dp", "fsdp"), None)
    head = P("fsdp", None)
    in_specs = (wide, wide, both, both, P(), head, head, P(), P(), P())
    out_specs = (head, head, wide, wide)
    return jax.shard_map(body, mesh=mesh, in_specs=in_specs, out_specs=out_specs, check_vma=False)
```

```python
import functools

import jax
import jax.numpy as jnp
from jax import lax
from jax.experimental import pallas as pl
from jax.experimental.pallas import tpu as pltpu
from jax.sharding import PartitionSpec as P

MESH = pl.DeviceIdType.MESH
BF = jnp.bfloat16
F32 = jnp.float32
NX, NY, NZ = 4, 4, 8
PLANE = NX * NY
PAIRS = 16384
N = 64
N2 = 2 * N
S = 320
D = 1152
H = D // 2
E = 576
EP = 640
PIECE = 48
TILES = 16
Z_ROWS = PIECE * NZ // 2
B = 256
NB = 16
LOG2E = 1.4426950408889634


def hops(k):
    return min(k // NY, NX - k // NY) + min(k % NY, NY - k % NY)


def back_slot(k):
    return (-(k // NY)) % NX * NY + (-(k % NY)) % NY


LINE = (0, 2, 6, 1, 7, 3, 5, 4)
RING = (0, 1, 3, 2)
SHEET = tuple(sorted(range(PLANE), key=lambda k: (hops(k), k)))


def place():
    dp, x_lo = lax.axis_index("dp"), lax.axis_index("fsdp")
    core = lax.rem(dp, 2)
    y = lax.rem(lax.div(dp, 2), NY)
    x = lax.rem(lax.div(dp, 2 * NY), 2) * 2 + x_lo
    z = lax.div(dp, 4 * NY)
    return x, y, z, core


def device(x, y, z, core):
    return (((z * 2 + lax.div(x, 2)) * NY + y) * 2 + core, lax.rem(x, 2))


def dot(a, b, contract):
    return lax.dot_general(a, b, (contract, ((), ())), preferred_element_type=F32)


def kernel(
    sup_i, sup_t, sel, bkt, wts, head_i, head_t, lscale, lbias, oscale,
    gs_i, gs_t, gw,
    va, vt, a, stage, cbuf, wfull, wother, unit, length,
    em, img, txt, g, p_f, p_out, p_in, t_out, t_own, rv_in, u_out, rs_a, rs_b, rs_i, rs_t,
    bk, bo, gsv, dwf, dws, dwz, r1, rz, r3, zsum, zres, zft, zfin, psum, r2, res, fint, fin, gwv,
    in_s, w_s, w_r, rows_s, rows_r, c_s, c_r, wo_s, wo_r,
    ia_s, ia_r, ip_s, if_s, ta_s, ta_r, tp_s, pi_s, pi_r, ri_s, ri_r, ra_r, rb_s, rb_r,
    rv_s, rv_r, ru_s, ru_r,
    bk_s, bk_r, gs_s, r1_s, r1_r, rz_s, rz_r, r3_s, r3_r, e3_s, e3_r, r2_s, r2_r, f_s, f_r,
    zg_s, zg_r, zd_s, zd_r, own_s, gw_s, ag_s, ag_r, ad_s, ad_r,
):
    x, y, z, core = place()
    half = lax.rem(x, 2)
    sib = device(x, y, z, 1 - core)
    first = core == 0

    def line(k, c=core):
        return device(x, y, lax.rem(z + k, NZ), c)

    def plane(k, c=core):
        return device(lax.rem(x + k // NY, NX), lax.rem(y + k % NY, NY), z, c)

    def remote(src, dst, send, recv, to):
        return pltpu.make_async_remote_copy(
            src_ref=src, dst_ref=dst, send_sem=send, recv_sem=recv,
            device_id=to, device_id_type=MESH,
        )

    def arrived(dst, recv, send):
        remote(dst, dst, send, recv, sib).wait_recv()

    def rows(ref, start, count):
        return ref.at[pl.ds(start, count), :]

    barrier = pltpu.get_barrier_semaphore()

    def greet(to):
        pl.semaphore_signal(barrier, inc=1, device_id=to, device_id_type=MESH)

    h_off = pl.multiple_of(half * H, H)
    sup_copies = [
        pltpu.make_async_copy(sup_i, va, in_s.at[0]),
        pltpu.make_async_copy(sup_t, vt, in_s.at[1]),
    ]
    head_copy = pltpu.make_async_copy(head_i, rows(wfull, h_off, H), in_s.at[2])
    for copy in sup_copies:
        copy.start()

    @pl.when(first)
    def _():
        head_copy.start()

    @pl.when(core == 1)
    def _():
        pltpu.make_async_copy(head_t, rows(wfull, h_off, H), in_s.at[2]).start()

    greet(sib)
    for k in range(1, NZ):
        greet(line(k))
    for k in range(1, PLANE):
        greet(plane(k, 0))
        greet(plane(k, 1))

    for copy in sup_copies:
        copy.wait()
    onehot = (lax.broadcasted_iota(jnp.int32, (S, N), 0) == sel[...]).astype(BF)
    rows_i = dot(onehot, va[...], ((0,), (0,))).astype(BF)
    rows_t = dot(onehot, vt[...], ((0,), (0,))).astype(BF)
    mine = pl.multiple_of(core * N, N)
    a[pl.ds(mine, N), :] = jnp.where(first, rows_i, rows_t)
    stage[...] = jnp.where(first, rows_t, rows_i)
    weight = jnp.zeros((1, N), F32)
    for n in range(NB):
        weight = jnp.where(bkt[...] == n, wts[:, n : n + 1], weight)
    weight = oscale[...] * weight / PAIRS
    cbuf[pl.ds(pl.multiple_of(core * 8, 8), 8), :] = jnp.concatenate(
        [jnp.broadcast_to(weight, (8, N)), jnp.zeros((8, N), F32)], axis=1
    )

    head_copy.wait()
    pl.semaphore_wait(barrier, 1 + (NZ - 1) + 2 * (PLANE - 1))

    heads = []
    for k, step in ((0, 1), (1, NX - 1)):
        src = rows(wfull, pl.multiple_of(h_off + k * (H // 2), H // 2), H // 2)
        heads.append(
            remote(src, src, w_s.at[k], w_r.at[k], device(lax.rem(x + step, NX), y, z, core))
        )
    rows_copy = remote(stage, rows(a, mine, N), rows_s, rows_r, sib)
    c_own = rows(cbuf, pl.multiple_of(core * 8, 8), 8)
    c_copy = remote(c_own, c_own, c_s, c_r, sib)
    for copy in heads:
        copy.start()
    rows_copy.start()
    c_copy.start()
    theirs = pl.multiple_of((1 - core) * N, N)
    o_off = pl.multiple_of((1 - half) * H, H)
    arrived(rows(a, theirs, N), rows_r, rows_s)
    arrived(rows(cbuf, pl.multiple_of((1 - core) * 8, 8), 8), c_r, c_s)
    for k in range(2):
        arrived(
            rows(wfull, pl.multiple_of(o_off + k * (H // 2), H // 2), H // 2), w_r.at[k], w_s.at[k]
        )

    raw = dot(a[...], wfull[...], ((1,), (0,)))
    size = jnp.sqrt(jnp.sum(raw * raw, axis=1, keepdims=True) + 1e-06)
    u = raw / size
    unit[...] = u
    length[...] = jnp.broadcast_to(size, (N2, 128))
    eye = lax.broadcasted_iota(jnp.int32, (N, N), 0) == lax.broadcasted_iota(jnp.int32, (N, N), 1)
    column = jnp.concatenate(
        [
            jnp.sum(jnp.where(eye, cbuf[8 * c : 8 * c + 1, 0:N], 0.0), axis=1, keepdims=True)
            for c in range(2)
        ],
        axis=0,
    )
    column = jnp.where(first, column, jnp.zeros_like(column))
    high = column.astype(BF)
    low = (column - high.astype(F32)).astype(BF)
    em[...] = jnp.concatenate([u.astype(BF), high, low, jnp.zeros((N2, EP - E - 2), BF)], axis=1)

    line_order, plane_order = LINE[1:], SHEET[1:]

    def ahead(at, k, size):
        return lax.rem(at + k, size)

    def u_peer(k, c=core):
        return device(
            jnp.where(first, ahead(x, k, NX), x), jnp.where(first, y, ahead(y, k, NY)), z, c
        )

    def v_peer(k):
        return device(
            jnp.where(first, x, ahead(x, k, NX)), jnp.where(first, ahead(y, k, NY), y), z, core
        )

    def img_at(k):
        return LINE.index(k % NZ) * N2

    def txt_at(u, v):
        return (RING.index(v % 4) * 4 + RING.index(u % 4)) * N

    def ia(k):
        return remote(em, rows(img, img_at(-k), N2), ia_s.at[k], ia_r.at[(NZ - k) % NZ], line(k))

    def ip(k):
        step = 1 if k == 6 else NZ - 1
        src = rows(img, img_at(k), N2)
        off, n = (0, 4) if k == 2 else (N, NZ)
        return (
            remote(src, rows(img, img_at(k - step), N2), ip_s.at[k], ia_r.at[(k - step) % NZ], line(step)),
            remote(
                rows(img, img_at(k) + off, N), rows(img, img_at(4) + off, N),
                ip_s.at[(k + 1) % NZ], ia_r.at[n], line((NZ - k) % NZ),
            ),
        )

    def fwd(k):
        block = rows(img, img_at(k), N2)
        return remote(em if k == 0 else block, block, if_s.at[k], ia_r.at[k], sib)

    def ta0(k):
        to = device(ahead(x, k, NX), y, z, 0)
        return remote(rows(em, 0, N), rows(txt, txt_at(-k, 0), N), ta_s.at[k], ta_r.at[(-k) % 4], to)

    def ta1(k):
        to = device(x, ahead(y, k, NY), z, 1)
        return remote(
            rows(em, N, N), rows(txt, txt_at(-k, 0), N), ta_s.at[4 + k], ta_r.at[(-k) % 4], to
        )

    def tp(u, v):
        return remote(
            rows(txt, txt_at(u, 0), N), rows(txt, txt_at(u, -v), N),
            tp_s.at[4 * v + u], ta_r.at[(-v) % 4 * 4 + u], v_peer(v),
        )

    @pl.when(first)
    def _():
        for k in line_order[:4]:
            ia(k).start()
        fwd(0).start()
        img[0:N2, :] = em[...]

    @pl.when(core == 1)
    def _():
        txt[0:N, :] = em[N:N2, :]
        for k in RING[::-1]:
            ta0(k).start()
            if k:
                ta1(k).start()

    wo_copy = remote(wfull, wother, wo_s, wo_r, sib)
    wo_copy.start()

    scale = lscale[...]
    neg_scale, neg_bias = -LOG2E * lscale[...], -LOG2E * lbias[...]

    def take_image(k):
        @pl.when(first)
        def _():
            if k == 4:
                for n in range(2):
                    arrived(rows(img, img_at(4) + n * N, N), ia_r.at[4 + 4 * n], ia_s.at[0])
            elif k:
                arrived(rows(img, img_at(k), N2), ia_r.at[k], ia_s.at[0])
            if k in (2, 6):
                for copy in ip(k):
                    copy.start()
            if k:
                fwd(k).start()

        @pl.when(core == 1)
        def _():
            arrived(rows(img, img_at(k), N2), ia_r.at[k], ia_s.at[0])

    def take_text(u, v):
        if u or v:
            arrived(rows(txt, txt_at(u, v), N), ta_r.at[4 * v + u], ta_s.at[0])
        else:

            @pl.when(first)
            def _():
                arrived(rows(txt, 0, N), ta_r.at[0], ta_s.at[0])

        if v == 0:
            for k in RING[:0:-1]:
                tp(u, k).start()

    def tile(i, j, diagonal=False):
        block = img[pl.ds(pl.multiple_of(i * B, B), B), :]
        weight = block[:, E : E + 1].astype(F32) + block[:, E + 1 : E + 2].astype(F32)
        other = txt[pl.ds(pl.multiple_of(j * B, B), B), :]
        e = jnp.exp2(neg_scale * dot(block, other, ((1,), (1,))) + neg_bias)
        value = weight / (1.0 + e)
        if diagonal:
            r = lax.broadcasted_iota(jnp.int32, (B, B), 0)
            c = lax.broadcasted_iota(jnp.int32, (B, B), 1)
            value = jnp.where((r == c + core * N) & (c < N), -value * e, value)
        g[pl.ds(pl.multiple_of(i * B, B), B), pl.ds(pl.multiple_of(j * B, B), B)] = value.astype(BF)

    for u in RING:
        take_text(u, 0)
    for k in LINE[:3]:
        take_image(k)
    for t in range(NZ * N2 // B):
        if t:
            for k in LINE[max(2 * t, 3) : 2 * t + 2]:
                take_image(k)
            for u in RING:
                take_text(u, RING[t])
        tile(t, t, t == 0)
        if t:

            @pl.loop(0, t)
            def _(i, t=t):
                tile(i, t)
                tile(t, i)

    def pi(k):
        return remote(
            rows(p_out, img_at(k), N2), rows(p_in, img_at(k), N2), pi_s.at[k], pi_r.at[k], sib
        )

    def ri(k):
        src = rows(p_out, img_at(k), N2)
        if k in (3, 5):
            n = 0 if k == 3 else 1
            return [remote(src, rows(rs_a, n * N2, N2), ri_s.at[k], ra_r.at[n], line(1 if k == 3 else 7))]
        if k == 4:
            return [
                remote(
                    rows(p_out, img_at(4) + n * N, N), rows(rs_b, n * N, N),
                    rb_s.at[n], rb_r.at[n], line((2, 6)[n]),
                )
                for n in range(2)
            ]
        back_k = (NZ - k) % NZ
        return [remote(src, rows(rs_i, back_k * N2, N2), ri_s.at[k], ri_r.at[back_k], line(k))]

    def combine(k):
        at = img_at(k)
        arrived(rows(p_in, at, N2), pi_r.at[k], pi_s.at[k])
        total = p_f[at : at + N2, :] + p_in[at : at + N2, :].astype(F32)
        if k in (2, 6):
            n = (2, 6).index(k)
            arrived(rows(rs_a, n * N2, N2), ra_r.at[n], ri_s.at[0])
            total += rs_a[n * N2 : (n + 1) * N2, :].astype(F32)
            arrived(rows(rs_b, n * N, N), rb_r.at[n], rb_s.at[n])
            more = rs_b[n * N : (n + 1) * N, :].astype(F32)
            half_of = total[n * N : (n + 1) * N, :] + more
            keep = total[(1 - n) * N : (2 - n) * N, :]
            total = jnp.concatenate([half_of, keep] if n == 0 else [keep, half_of], axis=0)
        if k:
            p_out[at : at + N2, :] = total.astype(BF)
            for copy in ri(k):
                copy.start()
        else:
            p_f[0:N2, :] = total

    def rv(v):
        n = RING.index(v) * 4 * N
        return remote(
            rows(t_out, n, 4 * N), rows(rv_in, (-v) % 4 * 4 * N, 4 * N),
            rv_s.at[v], rv_r.at[(-v) % 4], v_peer(v),
        )

    def ru(u):
        at = core * 4 + (-u) % 4
        return remote(
            rows(u_out, u * N, N), rows(rs_t, at * N, N), ru_s.at[u], ru_r.at[at], u_peer(u, 1)
        )

    back_order = (4, 3, 5, 1, 7, 2, 6, 0)
    text_order = (2, 1, 3, 0)
    for n in range(NZ + 1):
        if n < NZ:
            k = back_order[n]
            at = img_at(k)
            p_f[at : at + N2, :] = dot(g[at : at + N2, :], txt[:, 0:E], ((1,), (0,)))

            @pl.when(core == 1)
            def _(k=k, at=at):
                p_out[at : at + N2, :] = p_f[at : at + N2, :].astype(BF)
                pi(k).start()

            v = text_order[n // 2]
            b = 2 * RING.index(v) + n % 2
            block = dot(g[:, b * N2 : (b + 1) * N2], img[:, 0:E], ((0,), (0,)))
            if v:
                t_out[b * N2 : (b + 1) * N2, :] = block.astype(BF)
            else:
                t_own[b * N2 : (b + 1) * N2, :] = block
            if v and n % 2:
                rv(v).start()
        if n:

            @pl.when(first)
            def _(n=n):
                combine(back_order[n - 1])

    for v in text_order[:3]:
        arrived(rows(rv_in, v * 4 * N, 4 * N), rv_r.at[v], rv_s.at[v])
    for u in RING[::-1]:
        at = RING.index(u) * N
        total = t_own[at : at + N, :]
        for v in (1, 2, 3):
            row = v * 4 * N + at
            total += rv_in[row : row + N, :].astype(F32)
        if u:
            u_out[u * N : (u + 1) * N, :] = total.astype(BF)
            ru(u).start()
        else:

            @pl.when(first)
            def _(total=total):
                u_out[0:N, :] = total.astype(BF)
                remote(rows(u_out, 0, N), rows(rs_t, 0, N), ru_s.at[0], ru_r.at[0], sib).start()

            @pl.when(core == 1)
            def _(total=total):
                p_f[N:N2, :] = total

    @pl.when(first)
    def _():
        for k in (1, 7, 2, 6):
            arrived(rows(rs_i, k * N2, N2), ri_r.at[k], ri_s.at[0])
            p_f[0:N2, :] += rs_i[k * N2 : (k + 1) * N2, :].astype(F32)

    @pl.when(core == 1)
    def _():
        arrived(rows(rs_t, 0, N), ru_r.at[0], ru_s.at[0])
        p_f[0:N, :] = rs_t[0:N, :].astype(F32)
        for k in RING[1:]:
            for c in range(2):
                at = c * 4 + k
                arrived(rows(rs_t, at * N, N), ru_r.at[at], ru_s.at[0])
                p_f[c * N : (c + 1) * N, :] += rs_t[at * N : (at + 1) * N, :].astype(F32)

    grad = p_f[0:N2, :] * scale
    u = unit[...]
    back = ((grad - u * jnp.sum(u * grad, axis=1, keepdims=True)) / length[:, 0:1]).astype(BF)
    bk[...] = back
    bk_copy = remote(rows(bk, theirs, N), bo, bk_s, bk_r, sib)
    bk_copy.start()

    dwf[...] = dot(a[...], back, ((0,), (0,)))

    def z_row(k):
        at = lax.rem(z + k, NZ)
        return lax.div(at, NZ // 2), lax.rem(at, NZ // 2) * PIECE

    def p_row(k):
        px, py = lax.rem(x + k // NY, NX), lax.rem(y + k % NY, NY)
        return lax.rem(px, 2), Z_ROWS + (lax.div(px, 2) * NY + py) * PIECE

    def part(where):
        which, row = where
        return dwf[pl.ds(pl.multiple_of(which * H + row, PIECE), PIECE), :]

    def block(ref, k):
        return rows(ref, k * PIECE, PIECE)

    def r1_copy(k):
        return remote(
            block(dws, k), block(r1, back_slot(k)), r1_s.at[k], r1_r.at[back_slot(k)], plane(k)
        )

    def rz_copy(k):
        back_k = (NZ - k) % NZ
        return remote(block(dwz, k), block(rz, back_k), rz_s.at[k], rz_r.at[back_k], line(k))

    def fill(ref, k, where):
        ref[k * PIECE : (k + 1) * PIECE, :] = part(where).astype(BF)

    for n, k in enumerate(plane_order[::-1]):
        if n % 2 == 0 and n // 2 < NZ - 1:
            kz = line_order[::-1][n // 2]
            fill(dwz, kz, z_row(kz))
            rz_copy(kz).start()
        fill(dws, k, p_row(k))
        r1_copy(k).start()

    arrived(bo, bk_r, bk_s)
    arrived(wother, wo_r, wo_s)
    own = bk[pl.ds(mine, N), :]
    moved = dot(onehot, own, ((1,), (0,))).astype(BF)
    gsv[core] = dot(moved, wfull[...], ((1,), (1,)))
    moved = dot(onehot, bo[...], ((1,), (0,))).astype(BF)
    gsv[1 - core] = dot(moved, wother[...], ((1,), (1,)))
    gs_copies = [
        pltpu.make_async_copy(gsv.at[0], gs_i, gs_s.at[0]),
        pltpu.make_async_copy(gsv.at[1], gs_t, gs_s.at[1]),
    ]
    for copy in gs_copies:
        copy.start()

    z_half, z_at = z_row(0)
    holder = half == z_half

    def to_tiles(ref, value):
        for t in range(TILES):
            r, c = 16 * (t // 5), 128 * (t % 5)
            if t == TILES - 1:
                piece = jnp.zeros((16, 128), F32)
            elif c + 128 > E:
                piece = jnp.concatenate([value[r : r + 16, c:E], jnp.zeros((16, c + 128 - E), F32)], axis=1)
            else:
                piece = value[r : r + 16, c : c + 128]
            ref[16 * t : 16 * t + 16, :] = piece.astype(BF)

    def from_tiles(ref):
        bands = []
        for r in range(3):
            tiles = [ref[16 * (5 * r + c) : 16 * (5 * r + c) + 16, :] for c in range(5)]
            bands.append(jnp.concatenate(tiles, axis=1)[:, 0:E])
        return jnp.concatenate(bands, axis=0)

    total = part((z_half, z_at))
    for k in line_order:
        arrived(block(rz, k), rz_r.at[k], rz_s.at[k])
        total += rz[k * PIECE : (k + 1) * PIECE, :].astype(F32)
    to_tiles(zsum, total)

    def p_tile(k):
        return pl.multiple_of((lax.rem(x + k // NY, NX) * NY + lax.rem(y + k % NY, NY)) * 16, 16)

    def r3_copy(k):
        return remote(
            rows(zsum, p_tile(k), 16), rows(r3, back_slot(k) * 16, 16),
            r3_s.at[k], r3_r.at[back_slot(k)], plane(k),
        )

    for k in plane_order[::-1]:
        r3_copy(k).start()

    total = part(p_row(0))
    for k in plane_order[::-1]:
        arrived(block(r1, k), r1_r.at[k], r1_s.at[k])
        total += r1[k * PIECE : (k + 1) * PIECE, :].astype(F32)
    to_tiles(psum, total)

    def l_tile(k):
        return pl.multiple_of(lax.rem(z + k, NZ) * 32, 32)

    def r2_copy(k):
        back_k = (NZ - k) % NZ
        return remote(
            rows(psum, l_tile(k), 32), rows(r2, back_k * 32, 32), r2_s.at[k], r2_r.at[back_k], line(k)
        )

    for k in line_order[::-1]:
        r2_copy(k).start()

    def wants(k):
        return lax.rem(x + k // NY, 2) == z_half

    def e3_copy(k):
        return remote(zres, rows(zft, p_tile(0), 16), e3_s.at[k], e3_r.at[back_slot(k)], plane(k))

    total = zsum[pl.ds(p_tile(0), 16), :].astype(F32)
    for k in plane_order:
        arrived(rows(r3, k * 16, 16), r3_r.at[k], r3_s.at[k])
        total += r3[k * 16 : (k + 1) * 16, :].astype(F32)
    zres[...] = total.astype(BF)
    for k in plane_order[::-1]:

        @pl.when(wants(k))
        def _(k=k):
            e3_copy(k).start()

    zft[pl.ds(p_tile(0), 16), :] = total.astype(BF)

    def f_copy(k):
        return remote(res, rows(fint, l_tile(0), 32), f_s.at[k], f_r.at[(NZ - k) % NZ], line(k))

    total = psum[pl.ds(l_tile(0), 32), :].astype(F32)
    for k in line_order:
        arrived(rows(r2, k * 32, 32), r2_r.at[k], r2_s.at[k])
        total += r2[k * 32 : (k + 1) * 32, :].astype(F32)
    res[...] = total.astype(BF)
    for k in line_order[::-1]:
        f_copy(k).start()
    fint[pl.ds(l_tile(0), 32), :] = total.astype(BF)

    def shelf(modality, row):
        return gwv.at[modality, pl.ds(pl.multiple_of(row, PIECE), PIECE), :]

    def zg_copy(k):
        return remote(
            zfin, shelf(core, z_row(0)[1]), zg_s.at[k], zg_r.at[(NZ - k) % NZ], line(k)
        )

    def zd_copy(k, modality=core):
        to = shelf(modality, z_row(k)[1])
        return remote(zfin if k == 0 else to, to, zd_s.at[k], zd_r.at[k], sib)

    def holds(k):
        return z_row(k)[0] == half

    own_z = pltpu.make_async_copy(zfin, shelf(core, z_row(0)[1]), own_s.at[0])

    @pl.when(holder)
    def _():
        for k in plane_order:
            arrived(rows(zft, p_tile(k), 16), e3_r.at[k], e3_s.at[k])
        zfin[...] = from_tiles(zft)
        for k in line_order:
            zg_copy(k).start()
        zd_copy(0).start()
        own_z.start()

    for k in line_order:
        arrived(rows(fint, l_tile(k), 32), f_r.at[k], f_s.at[k])
    fin[...] = from_tiles(fint)

    mates = [k for k in plane_order if (k // NY) % 2 == 0]

    def ag_copy(k):
        return remote(
            fin, shelf(core, p_row(0)[1]), ag_s.at[k], ag_r.at[back_slot(k)], plane(k)
        )

    def ad_copy(k, modality=core):
        to = shelf(modality, p_row(k)[1])
        return remote(fin if k == 0 else to, to, ad_s.at[k], ad_r.at[k], sib)

    for k in mates:
        ag_copy(k).start()
    ad_copy(0).start()
    own_p = pltpu.make_async_copy(fin, shelf(core, p_row(0)[1]), own_s.at[1])
    own_p.start()
    for k in line_order:

        @pl.when(holds(k))
        def _(k=k):
            arrived(shelf(core, z_row(k)[1]), zg_r.at[k], zg_s.at[k])
            zd_copy(k).start()

    for k in mates:
        arrived(shelf(core, p_row(k)[1]), ag_r.at[k], ag_s.at[k])
        ad_copy(k).start()
    @pl.when(holder)
    def _():
        own_z.wait()

    own_p.wait()
    gw_copies = [
        pltpu.make_async_copy(gwv.at[m], gw.at[m], gw_s.at[n]) for n, m in enumerate((core, 1 - core))
    ]
    gw_copies[0].start()
    for k in LINE:

        @pl.when(holds(k))
        def _(k=k):
            arrived(shelf(1 - core, z_row(k)[1]), zd_r.at[k], zd_s.at[k])

    for k in [0] + mates:
        arrived(shelf(1 - core, p_row(k)[1]), ad_r.at[k], ad_s.at[k])
    gw_copies[1].start()

    for copy in heads + [rows_copy, c_copy, wo_copy, bk_copy]:
        copy.wait_send()

    @pl.when(first)
    def _():
        for k in line_order[:4]:
            ia(k).wait_send()
        for k in (2, 6):
            for copy in ip(k):
                copy.wait_send()
        for k in line_order:
            for copy in ri(k):
                copy.wait_send()
        for k in LINE:
            fwd(k).wait_send()
        remote(rows(u_out, 0, N), rows(rs_t, 0, N), ru_s.at[0], ru_r.at[0], sib).wait_send()

    @pl.when(core == 1)
    def _():
        for k in LINE:
            pi(k).wait_send()
        for k in RING:
            ta0(k).wait_send()
            if k:
                ta1(k).wait_send()

    for k in RING[1:]:
        for u in RING:
            tp(u, k).wait_send()
        rv(k).wait_send()
        ru(k).wait_send()
    for k in plane_order:
        r1_copy(k).wait_send()
    for k in line_order:
        rz_copy(k).wait_send()
        r2_copy(k).wait_send()
        f_copy(k).wait_send()

    for k in plane_order:
        r3_copy(k).wait_send()

        @pl.when(wants(k))
        def _(k=k):
            e3_copy(k).wait_send()

    @pl.when(holder)
    def _():
        for k in line_order:
            zg_copy(k).wait_send()

    for k in LINE:

        @pl.when(holds(k))
        def _(k=k):
            zd_copy(k).wait_send()

    for k in mates:
        ag_copy(k).wait_send()
    for k in [0] + mates:
        ad_copy(k).wait_send()
    for copy in gs_copies + gw_copies:
        copy.wait()


def finish(gw, gs_i, gs_t, out_hi, out_ht, out_i, out_t, narrow, wide, held, in_s, out_s, gi_s, go_s):
    loads = [pltpu.make_async_copy(gw.at[m], narrow.at[m], in_s.at[m]) for m in range(2)]
    moves = []
    for m, (src, dst) in enumerate(((gs_i, out_i), (gs_t, out_t))):
        at = held.at[m]
        moves.append(
            (
                pltpu.make_async_copy(src, at, gi_s.at[m]),
                pltpu.make_async_copy(at, dst, go_s.at[m]),
            )
        )
    moves[0][0].start()
    for copy in loads:
        copy.start()
    moves[1][0].start()
    stores = [pltpu.make_async_copy(wide.at[m], dst, out_s.at[m]) for m, dst in enumerate((out_hi, out_ht))]
    moves[0][0].wait()
    moves[0][1].start()
    for m in range(2):
        loads[m].wait()
        wide[m] = narrow[m].astype(F32)
        stores[m].start()
    moves[1][0].wait()
    moves[1][1].start()
    for copy in stores:
        copy.wait()
    for _, copy in moves:
        copy.wait()


def body(sup_i, sup_t, selected, buckets, weights, head_i, head_t, lscale, lbias, oscale):
    vmem = pl.BlockSpec(memory_space=pltpu.VMEM)
    hbm = pl.BlockSpec(memory_space=pl.ANY)

    def space(shape, dtype=BF):
        return pltpu.VMEM(shape, dtype)

    dma = pltpu.SemaphoreType.DMA
    buffers = [
        space((S, D)), space((S, D)), space((N2, D)), space((N, D)), space((16, 128), F32),
        space((D, E)), space((D, E)),
        space((N2, E), F32), space((N2, 128), F32),
        space((N2, EP)), space((NZ * N2, EP)), space((PLANE * N, EP)),
        space((NZ * N2, PLANE * N)),
        space((NZ * N2, E), F32), space((NZ * N2, E)), space((NZ * N2, E)), space((PLANE * N, E)),
        space((4 * N, E), F32), space((PLANE * N, E)), space((4 * N, E)), space((2 * N2, E)), space((N2, E)),
        space((NZ * N2, E)), space((8 * N, E)),
        space((N2, E)), space((N, E)), space((2, S, D), F32), space((D, E), F32),
        space((PLANE * PIECE, E)), space((NZ * PIECE, E)), space((PLANE * PIECE, E)),
        space((NZ * PIECE, E)), space((TILES * 16, 128)), space((TILES * 16, 128)), space((16, 128)),
        space((TILES * 16, 128)), space((PIECE, E)), space((TILES * 16, 128)), space((TILES * 16, 128)),
        space((32, 128)), space((TILES * 16, 128)), space((PIECE, E)), space((2, H, E)),
    ]
    counts = [
        3, 2, 2, 0, 0, 0, 0, 0, 0,
        NZ, NZ + 1, NZ, NZ, 8, PLANE, PLANE, NZ, NZ, NZ, NZ, 2, 2, 2, 4, 4, 4, 8,
        0, 0, 2, PLANE, PLANE, NZ, NZ, PLANE, PLANE, PLANE, PLANE, NZ, NZ, NZ, NZ,
        NZ, NZ, NZ, NZ, 2, 2, PLANE, PLANE, PLANE, PLANE,
    ]
    sems = [dma((n,)) if n else dma for n in counts]
    gs_i, gs_t, gw = pl.pallas_call(
        kernel,
        out_shape=(
            jax.ShapeDtypeStruct((S, D), F32),
            jax.ShapeDtypeStruct((S, D), F32),
            jax.ShapeDtypeStruct((2, H, E), BF),
        ),
        in_specs=[hbm] * 2 + [vmem] * 3 + [hbm] * 2 + [vmem] * 3,
        out_specs=(hbm, hbm, hbm),
        scratch_shapes=buffers + sems,
        compiler_params=pltpu.CompilerParams(
            collective_id=0, has_side_effects=True, vmem_limit_bytes=56 * 1024 * 1024
        ),
    )(
        sup_i, sup_t, selected.reshape(1, N), buckets.reshape(1, N), weights.reshape(1, NB),
        head_i, head_t, lscale.reshape(1, 1), lbias.reshape(1, 1), oscale.reshape(1, 1),
    )
    return pl.pallas_call(
        finish,
        out_shape=(jax.ShapeDtypeStruct((H, E), F32),) * 2 + (jax.ShapeDtypeStruct((S, D), F32),) * 2,
        in_specs=[hbm] * 3,
        out_specs=(hbm,) * 4,
        scratch_shapes=[
            space((2, H, E)), space((2, H, E), F32), space((2, S, D), F32),
            dma((2,)), dma((2,)), dma((2,)), dma((2,)),
        ],
        compiler_params=pltpu.CompilerParams(vmem_limit_bytes=60 * 1024 * 1024),
    )(gw, gs_i, gs_t)


def solution(mesh):
    both = P(("dp", "fsdp"))
    wide = P(("dp", "fsdp"), None)
    head = P("fsdp", None)
    in_specs = (wide, wide, both, both, P(), head, head, P(), P(), P())
    out_specs = (head, head, wide, wide)
    return jax.shard_map(body, mesh=mesh, in_specs=in_specs, out_specs=out_specs, check_vma=False)
```

```python
import functools

import jax
import jax.numpy as jnp
from jax import lax
from jax.experimental import pallas as pl
from jax.experimental.pallas import tpu as pltpu
from jax.sharding import PartitionSpec as P

MESH = pl.DeviceIdType.MESH
BF = jnp.bfloat16
F32 = jnp.float32
NX, NY, NZ = 4, 4, 8
PLANE = NX * NY
PAIRS = 16384
N = 64
N2 = 2 * N
S = 320
D = 1152
H = D // 2
E = 576
EP = 640
PIECE = 48
TILES = 16
Z_ROWS = PIECE * NZ // 2
B = 256
NB = 16
LOG2E = 1.4426950408889634


def hops(k):
    return min(k // NY, NX - k // NY) + min(k % NY, NY - k % NY)


def back_slot(k):
    return (-(k // NY)) % NX * NY + (-(k % NY)) % NY


LINE = (0, 2, 6, 1, 7, 3, 5, 4)
RING = (0, 1, 3, 2)
SHEET = tuple(sorted(range(PLANE), key=lambda k: (hops(k), k)))


def place():
    dp, x_lo = lax.axis_index("dp"), lax.axis_index("fsdp")
    core = lax.rem(dp, 2)
    y = lax.rem(lax.div(dp, 2), NY)
    x = lax.rem(lax.div(dp, 2 * NY), 2) * 2 + x_lo
    z = lax.div(dp, 4 * NY)
    return x, y, z, core


def device(x, y, z, core):
    return (((z * 2 + lax.div(x, 2)) * NY + y) * 2 + core, lax.rem(x, 2))


def dot(a, b, contract):
    return lax.dot_general(a, b, (contract, ((), ())), preferred_element_type=F32)


def kernel(
    sup_i, sup_t, sel, bkt, wts, head_i, head_t, lscale, lbias, oscale,
    gs_i, gs_t, gw,
    va, vt, a, stage, cbuf, wfull, wother, unit, length,
    em, img, txt, g, p_f, p_out, p_in, t_out, t_own, rv_in, u_out, rs_a, rs_b, rs_i, rs_t,
    bk, bo, gsv, dwf, dws, dwz, r1, rz, r3, zsum, zres, zft, zfin, psum, r2, res, fint, fin, gwv,
    in_s, w_s, w_r, rows_s, rows_r, c_s, c_r, wo_s, wo_r,
    ia_s, ia_r, ip_s, if_s, ta_s, ta_r, tp_s, pi_s, pi_r, ri_s, ri_r, ra_r, rb_s, rb_r,
    rv_s, rv_r, ru_s, ru_r,
    bk_s, bk_r, gs_s, r1_s, r1_r, rz_s, rz_r, r3_s, r3_r, e3_s, e3_r, r2_s, r2_r, f_s, f_r,
    zg_s, zg_r, zd_s, zd_r, own_s, gw_s, ag_s, ag_r, ad_s, ad_r,
):
    x, y, z, core = place()
    half = lax.rem(x, 2)
    sib = device(x, y, z, 1 - core)
    first = core == 0

    def line(k, c=core):
        return device(x, y, lax.rem(z + k, NZ), c)

    def plane(k, c=core):
        return device(lax.rem(x + k // NY, NX), lax.rem(y + k % NY, NY), z, c)

    def remote(src, dst, send, recv, to):
        return pltpu.make_async_remote_copy(
            src_ref=src, dst_ref=dst, send_sem=send, recv_sem=recv,
            device_id=to, device_id_type=MESH,
        )

    def arrived(dst, recv, send):
        remote(dst, dst, send, recv, sib).wait_recv()

    def rows(ref, start, count):
        return ref.at[pl.ds(start, count), :]

    barrier = pltpu.get_barrier_semaphore()

    def greet(to):
        pl.semaphore_signal(barrier, inc=1, device_id=to, device_id_type=MESH)

    for k in SHEET[:0:-1]:
        greet(plane(k))
    for k in LINE[:0:-1]:
        greet(line(k))
    for k in range(NY, PLANE, NY):
        greet(plane(k, 1 - core))
    greet(sib)

    h_off = pl.multiple_of(half * H, H)
    sup_copies = [
        pltpu.make_async_copy(sup_i, va, in_s.at[0]),
        pltpu.make_async_copy(sup_t, vt, in_s.at[1]),
    ]
    head_copy = pltpu.make_async_copy(head_i, rows(wfull, h_off, H), in_s.at[2])
    for copy in sup_copies:
        copy.start()

    @pl.when(first)
    def _():
        head_copy.start()

    @pl.when(core == 1)
    def _():
        pltpu.make_async_copy(head_t, rows(wfull, h_off, H), in_s.at[2]).start()

    for copy in sup_copies:
        copy.wait()
    onehot = (lax.broadcasted_iota(jnp.int32, (S, N), 0) == sel[...]).astype(BF)
    rows_i = dot(onehot, va[...], ((0,), (0,))).astype(BF)
    rows_t = dot(onehot, vt[...], ((0,), (0,))).astype(BF)
    mine = pl.multiple_of(core * N, N)
    a[pl.ds(mine, N), :] = jnp.where(first, rows_i, rows_t)
    stage[...] = jnp.where(first, rows_t, rows_i)
    weight = jnp.zeros((1, N), F32)
    for n in range(NB):
        weight = jnp.where(bkt[...] == n, wts[:, n : n + 1], weight)
    weight = oscale[...] * weight / PAIRS
    cbuf[pl.ds(pl.multiple_of(core * 8, 8), 8), :] = jnp.concatenate(
        [jnp.broadcast_to(weight, (8, N)), jnp.zeros((8, N), F32)], axis=1
    )

    head_copy.wait()
    pl.semaphore_wait(barrier, 1 + (NZ - 1) + (PLANE - 1) + (NX - 1))

    heads = []
    for k, step in ((0, 1), (1, NX - 1)):
        src = rows(wfull, pl.multiple_of(h_off + k * (H // 2), H // 2), H // 2)
        heads.append(
            remote(src, src, w_s.at[k], w_r.at[k], device(lax.rem(x + step, NX), y, z, core))
        )
    rows_copy = remote(stage, rows(a, mine, N), rows_s, rows_r, sib)
    c_own = rows(cbuf, pl.multiple_of(core * 8, 8), 8)
    c_copy = remote(c_own, c_own, c_s, c_r, sib)
    for copy in heads:
        copy.start()
    rows_copy.start()
    c_copy.start()
    theirs = pl.multiple_of((1 - core) * N, N)
    o_off = pl.multiple_of((1 - half) * H, H)
    arrived(rows(a, theirs, N), rows_r, rows_s)
    arrived(rows(cbuf, pl.multiple_of((1 - core) * 8, 8), 8), c_r, c_s)
    for k in range(2):
        arrived(
            rows(wfull, pl.multiple_of(o_off + k * (H // 2), H // 2), H // 2), w_r.at[k], w_s.at[k]
        )

    raw = dot(a[...], wfull[...], ((1,), (0,)))
    size = jnp.sqrt(jnp.sum(raw * raw, axis=1, keepdims=True) + 1e-06)
    u = raw / size
    unit[...] = u
    length[...] = jnp.broadcast_to(size, (N2, 128))
    eye = lax.broadcasted_iota(jnp.int32, (N, N), 0) == lax.broadcasted_iota(jnp.int32, (N, N), 1)
    column = jnp.concatenate(
        [
            jnp.sum(jnp.where(eye, cbuf[8 * c : 8 * c + 1, 0:N], 0.0), axis=1, keepdims=True)
            for c in range(2)
        ],
        axis=0,
    )
    column = jnp.where(first, column, jnp.zeros_like(column))
    high = column.astype(BF)
    low = (column - high.astype(F32)).astype(BF)
    em[...] = jnp.concatenate([u.astype(BF), high, low, jnp.zeros((N2, EP - E - 2), BF)], axis=1)

    line_order, plane_order = LINE[1:], SHEET[1:]

    def ahead(at, k, size):
        return lax.rem(at + k, size)

    def u_peer(k, c=core):
        return device(
            jnp.where(first, ahead(x, k, NX), x), jnp.where(first, y, ahead(y, k, NY)), z, c
        )

    def v_peer(k):
        return device(
            jnp.where(first, x, ahead(x, k, NX)), jnp.where(first, ahead(y, k, NY), y), z, core
        )

    def img_at(k):
        return LINE.index(k % NZ) * N2

    def txt_at(u, v):
        return (RING.index(v % 4) * 4 + RING.index(u % 4)) * N

    def ia(k):
        return remote(em, rows(img, img_at(-k), N2), ia_s.at[k], ia_r.at[(NZ - k) % NZ], line(k))

    def ip(k):
        step = 1 if k == 6 else NZ - 1
        src = rows(img, img_at(k), N2)
        off, n = (0, 4) if k == 2 else (N, NZ)
        return (
            remote(src, rows(img, img_at(k - step), N2), ip_s.at[k], ia_r.at[(k - step) % NZ], line(step)),
            remote(
                rows(img, img_at(k) + off, N), rows(img, img_at(4) + off, N),
                ip_s.at[(k + 1) % NZ], ia_r.at[n], line((NZ - k) % NZ),
            ),
        )

    def fwd(k):
        block = rows(img, img_at(k), N2)
        return remote(em if k == 0 else block, block, if_s.at[k], ia_r.at[k], sib)

    def ta0(k):
        to = device(ahead(x, k, NX), y, z, 0)
        return remote(rows(em, 0, N), rows(txt, txt_at(-k, 0), N), ta_s.at[k], ta_r.at[(-k) % 4], to)

    def ta1(k):
        to = device(x, ahead(y, k, NY), z, 1)
        return remote(
            rows(em, N, N), rows(txt, txt_at(-k, 0), N), ta_s.at[4 + k], ta_r.at[(-k) % 4], to
        )

    def tp(u, v):
        return remote(
            rows(txt, txt_at(u, 0), N), rows(txt, txt_at(u, -v), N),
            tp_s.at[4 * v + u], ta_r.at[(-v) % 4 * 4 + u], v_peer(v),
        )

    @pl.when(first)
    def _():
        for k in line_order[:4]:
            ia(k).start()
        fwd(0).start()
        img[0:N2, :] = em[...]

    @pl.when(core == 1)
    def _():
        txt[0:N, :] = em[N:N2, :]
        for k in RING[::-1]:
            ta0(k).start()
            if k:
                ta1(k).start()

    wo_copy = remote(wfull, wother, wo_s, wo_r, sib)
    wo_copy.start()

    scale = lscale[...]
    neg_scale, neg_bias = -LOG2E * lscale[...], -LOG2E * lbias[...]

    def take_image(k):
        @pl.when(first)
        def _():
            if k == 4:
                for n in range(2):
                    arrived(rows(img, img_at(4) + n * N, N), ia_r.at[4 + 4 * n], ia_s.at[0])
            elif k:
                arrived(rows(img, img_at(k), N2), ia_r.at[k], ia_s.at[0])
            if k in (2, 6):
                for copy in ip(k):
                    copy.start()
            if k:
                fwd(k).start()

        @pl.when(core == 1)
        def _():
            arrived(rows(img, img_at(k), N2), ia_r.at[k], ia_s.at[0])

    def take_text(u, v):
        if u or v:
            arrived(rows(txt, txt_at(u, v), N), ta_r.at[4 * v + u], ta_s.at[0])
        else:

            @pl.when(first)
            def _():
                arrived(rows(txt, 0, N), ta_r.at[0], ta_s.at[0])

        if v == 0:
            for k in RING[:0:-1]:
                tp(u, k).start()

    def tile(i, j, diagonal=False):
        block = img[pl.ds(pl.multiple_of(i * B, B), B), :]
        weight = block[:, E : E + 1].astype(F32) + block[:, E + 1 : E + 2].astype(F32)
        other = txt[pl.ds(pl.multiple_of(j * B, B), B), :]
        e = jnp.exp2(neg_scale * dot(block, other, ((1,), (1,))) + neg_bias)
        value = weight / (1.0 + e)
        if diagonal:
            r = lax.broadcasted_iota(jnp.int32, (B, B), 0)
            c = lax.broadcasted_iota(jnp.int32, (B, B), 1)
            value = jnp.where((r == c + core * N) & (c < N), -value * e, value)
        g[pl.ds(pl.multiple_of(i * B, B), B), pl.ds(pl.multiple_of(j * B, B), B)] = value.astype(BF)

    for u in RING:
        take_text(u, 0)
    for k in LINE[:3]:
        take_image(k)
    for t in range(NZ * N2 // B):
        if t:
            for k in LINE[max(2 * t, 3) : 2 * t + 2]:
                take_image(k)
            for u in RING:
                take_text(u, RING[t])
        tile(t, t, t == 0)
        if t:

            @pl.loop(0, t)
            def _(i, t=t):
                tile(i, t)
                tile(t, i)

    def pi(k):
        return remote(
            rows(p_out, img_at(k), N2), rows(p_in, img_at(k), N2), pi_s.at[k], pi_r.at[k], sib
        )

    def ri(k):
        src = rows(p_out, img_at(k), N2)
        if k in (3, 5):
            n = 0 if k == 3 else 1
            return [remote(src, rows(rs_a, n * N2, N2), ri_s.at[k], ra_r.at[n], line(1 if k == 3 else 7))]
        if k == 4:
            return [
                remote(
                    rows(p_out, img_at(4) + n * N, N), rows(rs_b, n * N, N),
                    rb_s.at[n], rb_r.at[n], line((2, 6)[n]),
                )
                for n in range(2)
            ]
        back_k = (NZ - k) % NZ
        return [remote(src, rows(rs_i, back_k * N2, N2), ri_s.at[k], ri_r.at[back_k], line(k))]

    def combine(k):
        at = img_at(k)
        arrived(rows(p_in, at, N2), pi_r.at[k], pi_s.at[k])
        total = p_f[at : at + N2, :] + p_in[at : at + N2, :].astype(F32)
        if k in (2, 6):
            n = (2, 6).index(k)
            arrived(rows(rs_a, n * N2, N2), ra_r.at[n], ri_s.at[0])
            total += rs_a[n * N2 : (n + 1) * N2, :].astype(F32)
            arrived(rows(rs_b, n * N, N), rb_r.at[n], rb_s.at[n])
            more = rs_b[n * N : (n + 1) * N, :].astype(F32)
            half_of = total[n * N : (n + 1) * N, :] + more
            keep = total[(1 - n) * N : (2 - n) * N, :]
            total = jnp.concatenate([half_of, keep] if n == 0 else [keep, half_of], axis=0)
        if k:
            p_out[at : at + N2, :] = total.astype(BF)
            for copy in ri(k):
                copy.start()
        else:
            p_f[0:N2, :] = total

    def rv(v):
        n = RING.index(v) * 4 * N
        return remote(
            rows(t_out, n, 4 * N), rows(rv_in, (-v) % 4 * 4 * N, 4 * N),
            rv_s.at[v], rv_r.at[(-v) % 4], v_peer(v),
        )

    def ru(u):
        at = core * 4 + (-u) % 4
        return remote(
            rows(u_out, u * N, N), rows(rs_t, at * N, N), ru_s.at[u], ru_r.at[at], u_peer(u, 1)
        )

    back_order = (4, 3, 5, 1, 7, 2, 6, 0)
    text_order = (2, 1, 3, 0)
    for n in range(NZ + 1):
        if n < NZ:
            k = back_order[n]
            at = img_at(k)
            p_f[at : at + N2, :] = dot(g[at : at + N2, :], txt[:, 0:E], ((1,), (0,)))

            @pl.when(core == 1)
            def _(k=k, at=at):
                p_out[at : at + N2, :] = p_f[at : at + N2, :].astype(BF)
                pi(k).start()

            v = text_order[n // 2]
            b = 2 * RING.index(v) + n % 2
            block = dot(g[:, b * N2 : (b + 1) * N2], img[:, 0:E], ((0,), (0,)))
            if v:
                t_out[b * N2 : (b + 1) * N2, :] = block.astype(BF)
            else:
                t_own[b * N2 : (b + 1) * N2, :] = block
            if v and n % 2:
                rv(v).start()
        if n:

            @pl.when(first)
            def _(n=n):
                combine(back_order[n - 1])

    for v in text_order[:3]:
        arrived(rows(rv_in, v * 4 * N, 4 * N), rv_r.at[v], rv_s.at[v])
    for u in RING[::-1]:
        at = RING.index(u) * N
        total = t_own[at : at + N, :]
        for v in (1, 2, 3):
            row = v * 4 * N + at
            total += rv_in[row : row + N, :].astype(F32)
        if u:
            u_out[u * N : (u + 1) * N, :] = total.astype(BF)
            ru(u).start()
        else:

            @pl.when(first)
            def _(total=total):
                u_out[0:N, :] = total.astype(BF)
                remote(rows(u_out, 0, N), rows(rs_t, 0, N), ru_s.at[0], ru_r.at[0], sib).start()

            @pl.when(core == 1)
            def _(total=total):
                p_f[N:N2, :] = total

    @pl.when(first)
    def _():
        for k in (1, 7, 2, 6):
            arrived(rows(rs_i, k * N2, N2), ri_r.at[k], ri_s.at[0])
            p_f[0:N2, :] += rs_i[k * N2 : (k + 1) * N2, :].astype(F32)

    @pl.when(core == 1)
    def _():
        arrived(rows(rs_t, 0, N), ru_r.at[0], ru_s.at[0])
        p_f[0:N, :] = rs_t[0:N, :].astype(F32)
        for k in RING[1:]:
            for c in range(2):
                at = c * 4 + k
                arrived(rows(rs_t, at * N, N), ru_r.at[at], ru_s.at[0])
                p_f[c * N : (c + 1) * N, :] += rs_t[at * N : (at + 1) * N, :].astype(F32)

    grad = p_f[0:N2, :] * scale
    u = unit[...]
    back = ((grad - u * jnp.sum(u * grad, axis=1, keepdims=True)) / length[:, 0:1]).astype(BF)
    bk[...] = back
    bk_copy = remote(rows(bk, theirs, N), bo, bk_s, bk_r, sib)
    bk_copy.start()

    dwf[...] = dot(a[...], back, ((0,), (0,)))

    def z_row(k):
        at = lax.rem(z + k, NZ)
        return lax.div(at, NZ // 2), lax.rem(at, NZ // 2) * PIECE

    def p_row(k):
        px, py = lax.rem(x + k // NY, NX), lax.rem(y + k % NY, NY)
        return lax.rem(px, 2), Z_ROWS + (lax.div(px, 2) * NY + py) * PIECE

    def part(where):
        which, row = where
        return dwf[pl.ds(pl.multiple_of(which * H + row, PIECE), PIECE), :]

    def block(ref, k):
        return rows(ref, k * PIECE, PIECE)

    def r1_copy(k):
        return remote(
            block(dws, k), block(r1, back_slot(k)), r1_s.at[k], r1_r.at[back_slot(k)], plane(k)
        )

    def rz_copy(k):
        back_k = (NZ - k) % NZ
        return remote(block(dwz, k), block(rz, back_k), rz_s.at[k], rz_r.at[back_k], line(k))

    def fill(ref, k, where):
        ref[k * PIECE : (k + 1) * PIECE, :] = part(where).astype(BF)

    for n, k in enumerate(plane_order[::-1]):
        if n % 2 == 0 and n // 2 < NZ - 1:
            kz = line_order[::-1][n // 2]
            fill(dwz, kz, z_row(kz))
            rz_copy(kz).start()
        fill(dws, k, p_row(k))
        r1_copy(k).start()

    arrived(bo, bk_r, bk_s)
    arrived(wother, wo_r, wo_s)
    own = bk[pl.ds(mine, N), :]
    moved = dot(onehot, own, ((1,), (0,))).astype(BF)
    gsv[core] = dot(moved, wfull[...], ((1,), (1,)))
    moved = dot(onehot, bo[...], ((1,), (0,))).astype(BF)
    gsv[1 - core] = dot(moved, wother[...], ((1,), (1,)))
    gs_copies = [
        pltpu.make_async_copy(gsv.at[0], gs_i, gs_s.at[0]),
        pltpu.make_async_copy(gsv.at[1], gs_t, gs_s.at[1]),
    ]
    for copy in gs_copies:
        copy.start()

    z_half, z_at = z_row(0)
    holder = half == z_half

    def to_tiles(ref, value):
        for t in range(TILES):
            r, c = 16 * (t // 5), 128 * (t % 5)
            if t == TILES - 1:
                piece = jnp.zeros((16, 128), F32)
            elif c + 128 > E:
                piece = jnp.concatenate([value[r : r + 16, c:E], jnp.zeros((16, c + 128 - E), F32)], axis=1)
            else:
                piece = value[r : r + 16, c : c + 128]
            ref[16 * t : 16 * t + 16, :] = piece.astype(BF)

    def from_tiles(ref):
        bands = []
        for r in range(3):
            tiles = [ref[16 * (5 * r + c) : 16 * (5 * r + c) + 16, :] for c in range(5)]
            bands.append(jnp.concatenate(tiles, axis=1)[:, 0:E])
        return jnp.concatenate(bands, axis=0)

    total = part((z_half, z_at))
    for k in line_order:
        arrived(block(rz, k), rz_r.at[k], rz_s.at[k])
        total += rz[k * PIECE : (k + 1) * PIECE, :].astype(F32)
    to_tiles(zsum, total)

    def p_tile(k):
        return pl.multiple_of((lax.rem(x + k // NY, NX) * NY + lax.rem(y + k % NY, NY)) * 16, 16)

    def r3_copy(k):
        return remote(
            rows(zsum, p_tile(k), 16), rows(r3, back_slot(k) * 16, 16),
            r3_s.at[k], r3_r.at[back_slot(k)], plane(k),
        )

    for k in plane_order[::-1]:
        r3_copy(k).start()

    total = part(p_row(0))
    for k in plane_order[::-1]:
        arrived(block(r1, k), r1_r.at[k], r1_s.at[k])
        total += r1[k * PIECE : (k + 1) * PIECE, :].astype(F32)
    to_tiles(psum, total)

    def l_tile(k):
        return pl.multiple_of(lax.rem(z + k, NZ) * 32, 32)

    def r2_copy(k):
        back_k = (NZ - k) % NZ
        return remote(
            rows(psum, l_tile(k), 32), rows(r2, back_k * 32, 32), r2_s.at[k], r2_r.at[back_k], line(k)
        )

    for k in line_order[::-1]:
        r2_copy(k).start()

    def wants(k):
        return lax.rem(x + k // NY, 2) == z_half

    def e3_copy(k):
        return remote(zres, rows(zft, p_tile(0), 16), e3_s.at[k], e3_r.at[back_slot(k)], plane(k))

    total = zsum[pl.ds(p_tile(0), 16), :].astype(F32)
    for k in plane_order:
        arrived(rows(r3, k * 16, 16), r3_r.at[k], r3_s.at[k])
        total += r3[k * 16 : (k + 1) * 16, :].astype(F32)
    zres[...] = total.astype(BF)
    for k in plane_order[::-1]:

        @pl.when(wants(k))
        def _(k=k):
            e3_copy(k).start()

    zft[pl.ds(p_tile(0), 16), :] = total.astype(BF)

    def f_copy(k):
        return remote(res, rows(fint, l_tile(0), 32), f_s.at[k], f_r.at[(NZ - k) % NZ], line(k))

    total = psum[pl.ds(l_tile(0), 32), :].astype(F32)
    for k in line_order:
        arrived(rows(r2, k * 32, 32), r2_r.at[k], r2_s.at[k])
        total += r2[k * 32 : (k + 1) * 32, :].astype(F32)
    res[...] = total.astype(BF)
    for k in line_order[::-1]:
        f_copy(k).start()
    fint[pl.ds(l_tile(0), 32), :] = total.astype(BF)

    def shelf(modality, row):
        return gwv.at[modality, pl.ds(pl.multiple_of(row, PIECE), PIECE), :]

    def zg_copy(k):
        return remote(
            zfin, shelf(core, z_row(0)[1]), zg_s.at[k], zg_r.at[(NZ - k) % NZ], line(k)
        )

    def zd_copy(k, modality=core):
        to = shelf(modality, z_row(k)[1])
        return remote(zfin if k == 0 else to, to, zd_s.at[k], zd_r.at[k], sib)

    def holds(k):
        return z_row(k)[0] == half

    own_z = pltpu.make_async_copy(zfin, shelf(core, z_row(0)[1]), own_s.at[0])

    @pl.when(holder)
    def _():
        for k in plane_order:
            arrived(rows(zft, p_tile(k), 16), e3_r.at[k], e3_s.at[k])
        zfin[...] = from_tiles(zft)
        for k in line_order:
            zg_copy(k).start()
        zd_copy(0).start()
        own_z.start()

    for k in line_order:
        arrived(rows(fint, l_tile(k), 32), f_r.at[k], f_s.at[k])
    fin[...] = from_tiles(fint)

    mates = [k for k in plane_order if (k // NY) % 2 == 0]

    def ag_copy(k):
        return remote(
            fin, shelf(core, p_row(0)[1]), ag_s.at[k], ag_r.at[back_slot(k)], plane(k)
        )

    def ad_copy(k, modality=core):
        to = shelf(modality, p_row(k)[1])
        return remote(fin if k == 0 else to, to, ad_s.at[k], ad_r.at[k], sib)

    for k in mates:
        ag_copy(k).start()
    ad_copy(0).start()
    own_p = pltpu.make_async_copy(fin, shelf(core, p_row(0)[1]), own_s.at[1])
    own_p.start()
    for k in line_order:

        @pl.when(holds(k))
        def _(k=k):
            arrived(shelf(core, z_row(k)[1]), zg_r.at[k], zg_s.at[k])
            zd_copy(k).start()

    for k in mates:
        arrived(shelf(core, p_row(k)[1]), ag_r.at[k], ag_s.at[k])
        ad_copy(k).start()
    @pl.when(holder)
    def _():
        own_z.wait()

    own_p.wait()
    gw_copies = [
        pltpu.make_async_copy(gwv.at[m], gw.at[m], gw_s.at[n]) for n, m in enumerate((core, 1 - core))
    ]
    gw_copies[0].start()
    for k in LINE:

        @pl.when(holds(k))
        def _(k=k):
            arrived(shelf(1 - core, z_row(k)[1]), zd_r.at[k], zd_s.at[k])

    for k in [0] + mates:
        arrived(shelf(1 - core, p_row(k)[1]), ad_r.at[k], ad_s.at[k])
    gw_copies[1].start()

    for copy in heads + [rows_copy, c_copy, wo_copy, bk_copy]:
        copy.wait_send()

    @pl.when(first)
    def _():
        for k in line_order[:4]:
            ia(k).wait_send()
        for k in (2, 6):
            for copy in ip(k):
                copy.wait_send()
        for k in line_order:
            for copy in ri(k):
                copy.wait_send()
        for k in LINE:
            fwd(k).wait_send()
        remote(rows(u_out, 0, N), rows(rs_t, 0, N), ru_s.at[0], ru_r.at[0], sib).wait_send()

    @pl.when(core == 1)
    def _():
        for k in LINE:
            pi(k).wait_send()
        for k in RING:
            ta0(k).wait_send()
            if k:
                ta1(k).wait_send()

    for k in RING[1:]:
        for u in RING:
            tp(u, k).wait_send()
        rv(k).wait_send()
        ru(k).wait_send()
    for k in plane_order:
        r1_copy(k).wait_send()
    for k in line_order:
        rz_copy(k).wait_send()
        r2_copy(k).wait_send()
        f_copy(k).wait_send()

    for k in plane_order:
        r3_copy(k).wait_send()

        @pl.when(wants(k))
        def _(k=k):
            e3_copy(k).wait_send()

    @pl.when(holder)
    def _():
        for k in line_order:
            zg_copy(k).wait_send()

    for k in LINE:

        @pl.when(holds(k))
        def _(k=k):
            zd_copy(k).wait_send()

    for k in mates:
        ag_copy(k).wait_send()
    for k in [0] + mates:
        ad_copy(k).wait_send()
    for copy in gs_copies + gw_copies:
        copy.wait()


def finish(gw, gs_i, gs_t, out_hi, out_ht, out_i, out_t, narrow, wide, held, in_s, out_s, gi_s, go_s):
    loads = [pltpu.make_async_copy(gw.at[m], narrow.at[m], in_s.at[m]) for m in range(2)]
    moves = []
    for m, (src, dst) in enumerate(((gs_i, out_i), (gs_t, out_t))):
        at = held.at[m]
        moves.append(
            (
                pltpu.make_async_copy(src, at, gi_s.at[m]),
                pltpu.make_async_copy(at, dst, go_s.at[m]),
            )
        )
    moves[0][0].start()
    for copy in loads:
        copy.start()
    moves[1][0].start()
    stores = [pltpu.make_async_copy(wide.at[m], dst, out_s.at[m]) for m, dst in enumerate((out_hi, out_ht))]
    moves[0][0].wait()
    moves[0][1].start()
    for m in range(2):
        loads[m].wait()
        wide[m] = narrow[m].astype(F32)
        stores[m].start()
    moves[1][0].wait()
    moves[1][1].start()
    for copy in stores:
        copy.wait()
    for _, copy in moves:
        copy.wait()


def body(sup_i, sup_t, selected, buckets, weights, head_i, head_t, lscale, lbias, oscale):
    vmem = pl.BlockSpec(memory_space=pltpu.VMEM)
    hbm = pl.BlockSpec(memory_space=pl.ANY)

    def space(shape, dtype=BF):
        return pltpu.VMEM(shape, dtype)

    dma = pltpu.SemaphoreType.DMA
    buffers = [
        space((S, D)), space((S, D)), space((N2, D)), space((N, D)), space((16, 128), F32),
        space((D, E)), space((D, E)),
        space((N2, E), F32), space((N2, 128), F32),
        space((N2, EP)), space((NZ * N2, EP)), space((PLANE * N, EP)),
        space((NZ * N2, PLANE * N)),
        space((NZ * N2, E), F32), space((NZ * N2, E)), space((NZ * N2, E)), space((PLANE * N, E)),
        space((4 * N, E), F32), space((PLANE * N, E)), space((4 * N, E)), space((2 * N2, E)), space((N2, E)),
        space((NZ * N2, E)), space((8 * N, E)),
        space((N2, E)), space((N, E)), space((2, S, D), F32), space((D, E), F32),
        space((PLANE * PIECE, E)), space((NZ * PIECE, E)), space((PLANE * PIECE, E)),
        space((NZ * PIECE, E)), space((TILES * 16, 128)), space((TILES * 16, 128)), space((16, 128)),
        space((TILES * 16, 128)), space((PIECE, E)), space((TILES * 16, 128)), space((TILES * 16, 128)),
        space((32, 128)), space((TILES * 16, 128)), space((PIECE, E)), space((2, H, E)),
    ]
    counts = [
        3, 2, 2, 0, 0, 0, 0, 0, 0,
        NZ, NZ + 1, NZ, NZ, 8, PLANE, PLANE, NZ, NZ, NZ, NZ, 2, 2, 2, 4, 4, 4, 8,
        0, 0, 2, PLANE, PLANE, NZ, NZ, PLANE, PLANE, PLANE, PLANE, NZ, NZ, NZ, NZ,
        NZ, NZ, NZ, NZ, 2, 2, PLANE, PLANE, PLANE, PLANE,
    ]
    sems = [dma((n,)) if n else dma for n in counts]
    gs_i, gs_t, gw = pl.pallas_call(
        kernel,
        out_shape=(
            jax.ShapeDtypeStruct((S, D), F32),
            jax.ShapeDtypeStruct((S, D), F32),
            jax.ShapeDtypeStruct((2, H, E), BF),
        ),
        in_specs=[hbm] * 2 + [vmem] * 3 + [hbm] * 2 + [vmem] * 3,
        out_specs=(hbm, hbm, hbm),
        scratch_shapes=buffers + sems,
        compiler_params=pltpu.CompilerParams(
            collective_id=0, has_side_effects=True, vmem_limit_bytes=56 * 1024 * 1024
        ),
    )(
        sup_i, sup_t, selected.reshape(1, N), buckets.reshape(1, N), weights.reshape(1, NB),
        head_i, head_t, lscale.reshape(1, 1), lbias.reshape(1, 1), oscale.reshape(1, 1),
    )
    return pl.pallas_call(
        finish,
        out_shape=(jax.ShapeDtypeStruct((H, E), F32),) * 2 + (jax.ShapeDtypeStruct((S, D), F32),) * 2,
        in_specs=[hbm] * 3,
        out_specs=(hbm,) * 4,
        scratch_shapes=[
            space((2, H, E)), space((2, H, E), F32), space((2, S, D), F32),
            dma((2,)), dma((2,)), dma((2,)), dma((2,)),
        ],
        compiler_params=pltpu.CompilerParams(vmem_limit_bytes=60 * 1024 * 1024),
    )(gw, gs_i, gs_t)


def solution(mesh):
    both = P(("dp", "fsdp"))
    wide = P(("dp", "fsdp"), None)
    head = P("fsdp", None)
    in_specs = (wide, wide, both, both, P(), head, head, P(), P(), P())
    out_specs = (head, head, wide, wide)
    return jax.shard_map(body, mesh=mesh, in_specs=in_specs, out_specs=out_specs, check_vma=False)
```
